32 devices in a mesh: gx: 8 (over z, x), gy: 4 (over y, core).
Axes of the slice: x: 2, y: 2, z: 4, core: 2. Of those that a mesh axis runs over, the one named last changes fastest.
Arguments:
- density: float32 [8, 4, 8, 64, 1024], P('gx', 'gy'), may hold values from -0.07 to 1.15
- moves: int32 [8, 4, 8], P('gx', 'gy'), may hold values from 0 to 255, as said below
- cols: int32 [8, 4, 8, 16], P('gx', 'gy'), may hold values from 0 to 39, as said below
- halo_rows: int32 [8, 4, 4], P('gx', 'gy'), may hold values from 0 to 7, as said below
Outputs:
- purified: float32 [8, 4, 8, 64, 1024], P('gx', 'gy')
- occupation: float32 [4], replicated
The draws below stay inside these ranges and needn't reach their ends.
Inputs may be any that keep to these rules, and one draw needn't show every extreme that they name: moves is a permutation of the 256 row ids. Rows leave in 8 waves: in each wave every brick sends one row to the brick beside it (periodic, among the eight around it) in that wave's direction, the waves' directions all differ, and the row lands in the slot that the receiving brick emptied in the same wave; all other rows keep their id. cols[i, j, r, 0] is r; the 16 entries of a row are distinct. `halo_rows`: the 4 entries of a brick are distinct.
All inputs are finite; a program needn't handle non-finite values.
Results may differ from the reference program's by a relative error of at most 0.0003.
Values sent between devices are 32-bit elements; how exact they have to be, the bound alone decides.
No kernel may reach another device: no remote copies, remote signals or barrier semaphores. Data moves between devices by JAX's collectives and lax.ppermute only.
A program may use at most 192 MiB of HBM per device.

```python
import jax
import jax.numpy as jnp
import numpy as np
from jax import lax

BLOCK = 64
K = 16
ROWS_DEV = 8
HALO = 4
WAVES = 8
STEPS = 2
N_GX = 8
N_GY = 4


noise_spread = 0.015625


shift_table_x = (-1, -1, -1, 0, 0, 1, 1, 1)


shift_table_y = (-1, 0, 1, -1, 1, -1, 0, 1)


def draw_density(key, part):
    key = jax.random.fold_in(key, 11)
    noise_key, jitter_key = jax.random.split(key)
    shape = (N_GX, N_GY, ROWS_DEV, BLOCK, K * BLOCK)
    across = jnp.arange(N_GX, dtype=jnp.float32)[:, None]
    along = jnp.arange(N_GY, dtype=jnp.float32)[None, :]
    place = (across * N_GY + along) / (N_GX * N_GY - 1)
    noise = jax.random.truncated_normal(noise_key, -4.0, 4.0, shape, jnp.float32) * noise_spread
    level = 0.3 * (1.0 + 2.0 * place)
    jitter = jax.random.uniform(jitter_key, shape[:4], jnp.float32, 0.8, 1.2)
    diagonal = (jnp.arange(BLOCK)[:, None] == jnp.arange(K * BLOCK)[None, :]).astype(jnp.float32)
    occupied = level[:, :, None, None] * jitter
    return noise + occupied[..., None] * diagonal[None, None, None]


def draw_moves(key, part):
    key = jax.random.fold_in(key, 14)
    slot_key, order_key = jax.random.split(key)
    bricks = N_GX * N_GY
    orders = jax.vmap(lambda one: jax.random.permutation(one, ROWS_DEV))(jax.random.split(slot_key, bricks))
    orders = orders.reshape(N_GX, N_GY, ROWS_DEV).astype(jnp.int32)
    directions = jax.random.permutation(order_key, 8)
    table_x = jnp.array(shift_table_x, dtype=jnp.int32)
    table_y = jnp.array(shift_table_y, dtype=jnp.int32)
    across = jnp.arange(N_GX, dtype=jnp.int32)[:, None]
    along = jnp.arange(N_GY, dtype=jnp.int32)[None, :]
    slot_ids = jnp.arange(ROWS_DEV, dtype=jnp.int32)
    result = ((across * N_GY + along) * ROWS_DEV)[:, :, None] + slot_ids[None, None, :]
    for wave in range(WAVES):
        chosen = directions[wave]
        other_x = (across + table_x[chosen]) % N_GX
        other_y = (along + table_y[chosen]) % N_GY
        emptied = orders[:, :, wave]
        landing = emptied[other_x, other_y]
        target = (other_x * N_GY + other_y) * ROWS_DEV + landing
        result = jnp.where(slot_ids[None, None, :] == emptied[:, :, None], target[:, :, None], result)
    return result.astype(jnp.int32)


def draw_cols(key, part):
    key = jax.random.fold_in(key, 12)
    pool = ROWS_DEV + 8 * HALO
    count = N_GX * N_GY * ROWS_DEV
    orders = jax.vmap(lambda one: jax.random.permutation(one, pool - 1))(jax.random.split(key, count))
    orders = orders[:, :K - 1].astype(jnp.int32)
    itself = jnp.tile(jnp.arange(ROWS_DEV, dtype=jnp.int32), N_GX * N_GY)
    others = orders + (orders >= itself[:, None]).astype(jnp.int32)
    result = jnp.concatenate([itself[:, None], others], axis=1)
    return result.reshape(N_GX, N_GY, ROWS_DEV, K).astype(jnp.int32)


def draw_halo_rows(key, part):
    key = jax.random.fold_in(key, 13)
    count = N_GX * N_GY
    orders = jax.vmap(lambda one: jax.random.permutation(one, ROWS_DEV))(jax.random.split(key, count))
    return orders[:, :HALO].reshape(N_GX, N_GY, HALO).astype(jnp.int32)


def setup_inputs(seed: int = 0) -> dict:
    keys = jax.random.split(jax.random.key(seed), 5)
    density = draw_density(jax.random.fold_in(keys[4], 71), 0)
    moves = draw_moves(jax.random.fold_in(keys[4], 71), 0)
    cols = draw_cols(jax.random.fold_in(keys[4], 71), 0)
    halo_rows = draw_halo_rows(jax.random.fold_in(keys[4], 71), 0)
    return {"density": density, "moves": moves, "cols": cols, "halo_rows": halo_rows}


step_x = np.array([-1, -1, -1, 0, 0, 1, 1, 1])
step_y = np.array([-1, 0, 1, -1, 1, -1, 0, 1])


def global_columns(cols, halo_rows):
    across = jnp.arange(N_GX, dtype=jnp.int32)[:, None]
    along = jnp.arange(N_GY, dtype=jnp.int32)[None, :]
    firsts = (across * N_GY + along) * ROWS_DEV
    pieces = [firsts[:, :, None] + jnp.arange(ROWS_DEV, dtype=jnp.int32)[None, None, :]]
    for direction in range(8):
        other_x = (across + int(step_x[direction])) % N_GX
        other_y = (along + int(step_y[direction])) % N_GY
        listed = halo_rows[other_x, other_y].astype(jnp.int32)
        pieces.append(((other_x * N_GY + other_y) * ROWS_DEV)[:, :, None] + listed)
    table = jnp.concatenate(pieces, axis=2).astype(jnp.int32)
    picked = jnp.take_along_axis(table, cols.reshape(N_GX, N_GY, ROWS_DEV * K).astype(jnp.int32), axis=2)
    return picked.reshape(N_GX * N_GY * ROWS_DEV, K).astype(jnp.int32)


def square_on_pattern(current, columns):
    total = current.shape[0]
    blocks = current.reshape(total, BLOCK, K, BLOCK)

    def one_group(start):
        mine = lax.dynamic_slice_in_dim(blocks, start, ROWS_DEV, 0)
        my_cols = lax.dynamic_slice_in_dim(columns, start, ROWS_DEV, 0)
        far = jnp.take(blocks, my_cols, axis=0)
        far_cols = jnp.take(columns, my_cols, axis=0)
        match = (far_cols[:, :, :, None] == my_cols[:, None, None, :]).astype(jnp.float32)
        aligned = jnp.einsum('gtbuc,gtus->gtbsc', far, match, precision=lax.Precision.HIGHEST)
        return jnp.einsum('gatb,gtbsc->gasc', mine, aligned, precision=lax.Precision.HIGHEST)

    starts = jnp.arange(total // ROWS_DEV, dtype=jnp.int32) * ROWS_DEV
    return lax.map(one_group, starts).reshape(total, BLOCK, K * BLOCK)


def slot_trace(current):
    return jnp.sum(jnp.diagonal(current[:, :, :BLOCK], axis1=1, axis2=2))


def reference(density, moves, cols, halo_rows):
    total = N_GX * N_GY * ROWS_DEV
    flat = density.reshape(total, BLOCK, K * BLOCK)
    current = jnp.zeros_like(flat).at[moves.reshape(total).astype(jnp.int32)].set(flat)
    columns = global_columns(cols, halo_rows)
    scale = 1.0 / (total * BLOCK)
    sums = []
    for step in range(STEPS):
        squared = square_on_pattern(current, columns)
        sums.append(slot_trace(current) * scale)
        sums.append(slot_trace(squared) * scale)
        if step % 2 == 1:
            current = 2.0 * current - squared
        else:
            current = squared
    return current.reshape(density.shape), jnp.stack(sums).astype(jnp.float32)
```

```python
import functools

import jax
import jax.numpy as jnp
import numpy as np
from jax import lax
from jax.experimental import pallas as pl
from jax.experimental.pallas import tpu as pltpu
from jax.sharding import PartitionSpec as P

STEPS = 2
AXES = ("gx", "gy")
LANES = 128
TILE = 256

step_x = np.array([-1, -1, -1, 0, 0, 1, 1, 1])
step_y = np.array([-1, 0, 1, -1, 1, -1, 0, 1])

GROUPS = ("C", "A", "Y", "CA", "B", "YA", "CB", "YB")
FRAME = {
    "C": (0, 1),
    "A": (1, 0),
    "Y": (0, -1),
    "CA": (1, 1),
    "B": (-1, 0),
    "YA": (1, -1),
    "CB": (-1, 1),
    "YB": (-1, -1),
}


def flat_perm(count_x, count_y, move):
    pairs = []
    for i in range(count_x):
        for j in range(count_y):
            x, y = move(i, j)
            pairs.append((i * count_y + j, (x % count_x) * count_y + y % count_y))
    return pairs


def toward_a(i, j):
    return i ^ 1, j


def along_b(i, j):
    return (i + 2 if i % 2 == 0 else i - 2), j


def toward_c(i, j):
    return i, j ^ 1


def toward_y(i, j):
    return i, (j - 1 if j % 2 == 0 else j + 1)


def half_pair(ref_rows, left, right):
    lane = lax.broadcasted_iota(jnp.int32, (64, LANES), 1)
    one = jnp.maximum(left, 0)
    two = jnp.maximum(right, 0)
    low = ref_rows(one >> 1)
    high = ref_rows(two >> 1)
    low = pltpu.roll(low, (one & 1) * 64, 1)
    high = pltpu.roll(high, (1 - (two & 1)) * 64, 1)
    low_end = jnp.where(left >= 0, 64, 0)
    high_start = jnp.where(right >= 0, 64, 128)
    return jnp.where(lane < low_end, low, jnp.where(lane >= high_start, high, 0.0))


def split(value):
    high = value.astype(jnp.bfloat16)
    low = (value - high.astype(jnp.float32)).astype(jnp.bfloat16)
    return high, low


def trace_of(block):
    row = lax.broadcasted_iota(jnp.int32, block.shape, 0)
    lane = lax.broadcasted_iota(jnp.int32, block.shape, 1)
    return jnp.sum(jnp.where(row == lane, block, 0.0))


def place(slots, rims, arrived):
    rows = len(arrived)
    block, strip = arrived[0].shape
    half = rims.shape[0] // 2

    def kernel(slots_ref, rims_ref, *refs):
        ins, (current_ref, first_ref, second_ref, trace_ref) = refs[:rows], refs[rows:]
        total = jnp.float32(0.0)
        for d in range(rows):
            current_ref[slots_ref[d]] = ins[d][...]
            total += trace_of(ins[d][:, :LANES])
        trace_ref[0, 0] = total
        for m in range(half):
            first_ref[m] = current_ref[rims_ref[m]]
            second_ref[m] = current_ref[rims_ref[half + m]]

    vmem = pl.BlockSpec(memory_space=pltpu.VMEM)
    smem = pl.BlockSpec(memory_space=pltpu.SMEM)
    return pl.pallas_call(
        kernel,
        out_shape=(
            jax.ShapeDtypeStruct((rows, block, strip), jnp.float32),
            jax.ShapeDtypeStruct((half, block, strip), jnp.float32),
            jax.ShapeDtypeStruct((half, block, strip), jnp.float32),
            jax.ShapeDtypeStruct((1, 1), jnp.float32),
        ),
        in_specs=[smem, smem] + [vmem] * rows,
        out_specs=(vmem, vmem, vmem, smem),
        compiler_params=pltpu.CompilerParams(vmem_limit_bytes=32 * 2**20),
        name="place_rows",
    )(slots, rims, *arrived)


def product_kernel(spec, *refs):
    first, counts, has_total, last, blend, pool = spec
    refs = list(refs)
    slot_ref = refs.pop(0)
    if last:
        where_ref, rims_ref = refs.pop(0), refs.pop(0)
    own_ref = refs.pop(0)
    parts = [refs.pop(0) for _ in counts] if counts else [own_ref]
    total_ref = refs.pop(0) if has_total else None
    if last:
        out_ref, rim_a_ref, rim_b_ref, trace_ref = (refs.pop(0) for _ in range(4))
    else:
        total_out = refs.pop(0)
    a_high, a_low, d_high, d_low = (refs.pop(0) for _ in range(4))
    rows = own_ref.shape[0]
    members = sum(ref.shape[0] for ref in parts)
    n = pl.program_id(0)

    @pl.when(n == 0)
    def _():
        def one_row(g, carry):
            at = pl.ds(pl.multiple_of(g * 64, 64), 64)
            for k in range(members // 2):
                spot = first + 2 * k
                value = half_pair(
                    lambda s: own_ref[g, :, pl.ds(pl.multiple_of(s * LANES, LANES), LANES)],
                    slot_ref[g, spot],
                    slot_ref[g, spot + 1],
                )
                high, low = split(value)
                a_high[at, pl.ds(k * LANES, LANES)] = high
                a_low[at, pl.ds(k * LANES, LANES)] = low
            return carry

        lax.fori_loop(0, rows, one_row, 0)

    base = 0
    for ref in parts:

        def one_member(c, carry, ref=ref, base=base):
            at = pl.ds(pl.multiple_of((base + c) * 64, 64), 64)
            for q in range(TILE // LANES):
                spot = n * (TILE // 64) + 2 * q
                left = slot_ref[first + base + c, spot]
                right = slot_ref[first + base + c, spot + 1]
                to = pl.ds(q * LANES, LANES)

                @pl.when(jnp.maximum(left, right) >= 0)
                def _():
                    value = half_pair(
                        lambda s: ref[c, :, pl.ds(pl.multiple_of(s * LANES, LANES), LANES)],
                        left,
                        right,
                    )
                    high, low = split(value)
                    d_high[at, to] = high
                    d_low[at, to] = low

                @pl.when(jnp.maximum(left, right) < 0)
                def _():
                    d_high[at, to] = jnp.zeros((64, LANES), jnp.bfloat16)
                    d_low[at, to] = jnp.zeros((64, LANES), jnp.bfloat16)

            return carry

        lax.fori_loop(0, ref.shape[0], one_member, 0)
        base += ref.shape[0]

    dot = functools.partial(jnp.dot, preferred_element_type=jnp.float32)
    result = dot(a_high[...], d_high[...])
    result += dot(a_high[...], d_low[...])
    result += dot(a_low[...], d_high[...])
    if has_total:
        result += total_ref[...]
    if not last:
        total_out[...] = result
        return
    dense_ref = refs.pop(0)
    dense_ref[:, pl.ds(pl.multiple_of(n * TILE, TILE), TILE)] = result

    @pl.when(n == pl.num_programs(0) - 1)
    def _():
        trace_ref[0, 0] = jnp.float32(0.0)

        def one_row(g, carry):
            at = pl.ds(pl.multiple_of(g * 64, 64), 64)
            for k in range(own_ref.shape[2] // LANES):
                value = half_pair(
                    lambda s: dense_ref[at, pl.ds(pl.multiple_of(s * LANES, LANES), LANES)],
                    where_ref[g, 2 * k],
                    where_ref[g, 2 * k + 1],
                )
                if k == 0:
                    trace_ref[0, 0] += trace_of(value)
                to = pl.ds(k * LANES, LANES)
                if blend:
                    value = 2.0 * own_ref[g, :, to] - value
                out_ref[g, :, to] = value
            return carry

        lax.fori_loop(0, rows, one_row, 0)
        if rim_a_ref is not None:
            half = rim_a_ref.shape[0]
            for m in range(half):
                rim_a_ref[m] = out_ref[rims_ref[m]]
                rim_b_ref[m] = out_ref[rims_ref[half + m]]


def product(first, slot_table, own, parts, total, last=None, name="product"):
    rows, block, strip = own.shape
    pool = slot_table.shape[0]
    members = sum(p.shape[0] for p in parts) if parts else rows
    depth = members * block
    width = pool * block
    whole = lambda a: pl.BlockSpec(a.shape, lambda n: (0,) * a.ndim, pipeline_mode=pl.Buffered(1))
    smem = pl.BlockSpec(memory_space=pltpu.SMEM)
    tile = pl.BlockSpec((rows * block, TILE), lambda n: (0, n))
    ins = [slot_table]
    in_specs = [smem]
    if last is not None:
        where, rims, blend = last
        ins += [where, rims]
        in_specs += [smem, smem]
    ins += [own, *parts]
    in_specs += [whole(own), *(whole(p) for p in parts)]
    if total is not None:
        ins.append(total)
        in_specs.append(tile)
    scratch = [
        pltpu.VMEM((rows * block, depth), jnp.bfloat16),
        pltpu.VMEM((rows * block, depth), jnp.bfloat16),
        pltpu.VMEM((depth, TILE), jnp.bfloat16),
        pltpu.VMEM((depth, TILE), jnp.bfloat16),
    ]
    if last is None:
        out_shape = jax.ShapeDtypeStruct((rows * block, width), jnp.float32)
        out_specs = tile
    else:
        half = rims.shape[0] // 2
        rim = jax.ShapeDtypeStruct((half, block, strip), jnp.float32)
        out_shape = (
            jax.ShapeDtypeStruct(own.shape, jnp.float32),
            rim,
            rim,
            jax.ShapeDtypeStruct((1, 1), jnp.float32),
        )
        fixed = lambda a: pl.BlockSpec(a.shape, lambda n: (0, 0, 0))
        out_specs = (fixed(own), fixed(rim), fixed(rim), smem)
        scratch.append(pltpu.VMEM((rows * block, width), jnp.float32))
    spec = (
        first,
        tuple(p.shape[0] for p in parts),
        total is not None,
        last is not None,
        last is not None and last[2],
        pool,
    )
    return pl.pallas_call(
        functools.partial(product_kernel, spec),
        grid=(width // TILE,),
        out_shape=out_shape,
        in_specs=in_specs,
        out_specs=out_specs,
        scratch_shapes=scratch,
        compiler_params=pltpu.CompilerParams(
            dimension_semantics=("arbitrary",), vmem_limit_bytes=48 * 2**20
        ),
        cost_estimate=pl.CostEstimate(
            flops=6 * rows * block * depth * width,
            bytes_accessed=4 * (rows + members) * block * strip + 8 * rows * block * width,
            transcendentals=0,
        ),
        name=name,
    )(*ins)


def butterfly(value, count_x, count_y):
    for bit in [1 << b for b in range(count_y.bit_length() - 1)]:
        perm = flat_perm(count_x, count_y, lambda i, j: (i, j ^ bit))
        value = value + lax.ppermute(value, AXES, perm)
    for bit in [1 << b for b in range(count_x.bit_length() - 1)]:
        perm = flat_perm(count_x, count_y, lambda i, j: (i ^ bit, j))
        value = value + lax.ppermute(value, AXES, perm)
    return value


def tables(cols, halo, index_x, index_y, count_x, count_y):
    rows, slots = cols.shape
    rims = halo.shape[0]
    sign_x = 1 - 2 * (index_x % 2)
    sign_y = 1 - 2 * (index_y % 2)
    frame = np.array([FRAME[name] for name in GROUPS])
    away = cols - rows
    direction = away // rims
    listed = away % rims
    linear = direction + (direction >= 4).astype(jnp.int32)
    in_list = halo[None, None, :] == cols[:, :, None]
    spot = jnp.sum(jnp.where(in_list, jnp.arange(rims, dtype=jnp.int32), 0), axis=2)
    inner = jnp.where(jnp.any(in_list, axis=2), 4 * rims + spot, -1)
    code = jnp.where(cols < rows, inner, linear * rims + listed)
    mine = jnp.sum(
        jnp.where((halo[:, None] == jnp.arange(rows, dtype=jnp.int32))[:, :, None], code[None], 0),
        axis=1,
    )
    codes = lax.all_gather(mine, AXES).reshape(count_x * count_y, rims, slots)
    other_x = (index_x + jnp.asarray(frame[:, 0], jnp.int32) * sign_x) % count_x
    other_y = (index_y + jnp.asarray(frame[:, 1], jnp.int32) * sign_y) % count_y
    near = jnp.take(codes, other_x * count_y + other_y, axis=0)

    base_of = np.zeros((9,), np.int32)
    for g, name in enumerate(GROUPS):
        x, y = FRAME[name]
        base_of[3 * (x + 1) + y + 1] = rows + g * rims

    def locate(place, index, shift_x, shift_y):
        x = (place // 3 - 1) * sign_x + shift_x
        y = (place % 3 - 1) * sign_y + shift_y
        inside = (jnp.abs(x) <= 1) & (jnp.abs(y) <= 1)
        at = 3 * (x + 1) + y + 1
        spot = index
        for k in range(9):
            if k != 4:
                spot = spot + jnp.where(at == k, int(base_of[k]), 0)
        own = index * 0
        for m in range(rims):
            own = own + jnp.where(index == m, halo[m], 0)
        return jnp.where(inside, jnp.where(at == 4, own, spot), -1)

    own_spots = jnp.where(cols < rows, cols, locate(linear, listed, 0, 0))
    shift_x = frame[:, 0].astype(np.int32)[:, None, None]
    shift_y = frame[:, 1].astype(np.int32)[:, None, None]
    near_spots = locate(near // rims, near % rims, shift_x, shift_y)
    near_spots = jnp.where(near < 0, -1, near_spots)
    spots = jnp.concatenate([own_spots, near_spots.reshape(-1, slots)], 0)
    pool = spots.shape[0]
    hit = spots[:, :, None] == jnp.arange(pool, dtype=jnp.int32)
    slot_table = (
        jnp.sum(jnp.where(hit, jnp.arange(1, slots + 1, dtype=jnp.int32)[:, None], 0), axis=1) - 1
    )
    return own_spots.astype(jnp.int32), slot_table.astype(jnp.int32)


def shards(density, moves, cols, halo_rows):
    row_count, block, strip = density.shape[2:]
    rim_count = halo_rows.shape[2]
    count_x = lax.axis_size("gx")
    count_y = lax.axis_size("gy")
    index_x = lax.axis_index("gx")
    index_y = lax.axis_index("gy")
    rows = density.reshape(row_count, block, strip)
    rims = halo_rows.reshape(rim_count)

    owner = moves.reshape(row_count) // row_count
    other = (index_x + jnp.asarray(step_x, jnp.int32)) % count_x * count_y
    other = other + (index_y + jnp.asarray(step_y, jnp.int32)) % count_y
    slot_ids = jnp.arange(row_count, dtype=jnp.int32)
    slots = jnp.sum(jnp.where(owner[None, :] == other[:, None], slot_ids, 0), axis=1)
    arrived = []
    for d in range(len(step_x)):
        dx, dy = int(step_x[d]), int(step_y[d])
        perm = flat_perm(count_x, count_y, lambda i, j: (i + dx, j + dy))
        leaving = lax.dynamic_index_in_dim(rows, slots[d], 0, keepdims=False)
        arrived.append(lax.ppermute(leaving, AXES, perm))

    own_spots, slot_table = tables(
        cols.reshape(row_count, -1), rims, index_x, index_y, count_x, count_y
    )
    current, rim_0, rim_1, trace = place(slots, rims, arrived)
    swap = {
        "A": flat_perm(count_x, count_y, toward_a),
        "B": flat_perm(count_x, count_y, along_b),
        "C": flat_perm(count_x, count_y, toward_c),
        "Y": flat_perm(count_x, count_y, toward_y),
    }
    go = lambda value, way: lax.ppermute(value, AXES, swap[way])
    traces = [trace]
    for step in range(STEPS):
        y_0, a_0 = go(rim_0, "Y"), go(rim_0, "A")
        y_1, a_1 = go(rim_1, "Y"), go(rim_1, "A")
        c_0, c_1 = go(rim_0, "C"), go(rim_1, "C")
        b_0, b_1 = go(a_0, "B"), go(a_1, "B")
        ya_0, ya_1 = go(y_0, "A"), go(a_1, "Y")
        ca_0, ca_1 = go(a_0, "C"), go(a_1, "C")
        yb_0, yb_1 = go(ya_0, "B"), go(b_1, "Y")
        cb_0, cb_1 = go(b_0, "C"), go(b_1, "C")
        four = 2 * rim_0.shape[0]
        total = product(0, slot_table, current, [], None, name="own_rows")
        total = product(
            row_count, slot_table, current, [c_0, c_1, a_0, a_1, y_0, y_1], total, name="near_rows"
        )
        total = product(
            row_count + 3 * four,
            slot_table,
            current,
            [ca_0, ca_1, b_0, b_1, ya_0, ya_1],
            total,
            name="corner_rows",
        )
        current, rim_0, rim_1, trace = product(
            row_count + 6 * four,
            slot_table,
            current,
            [cb_0, cb_1, yb_0, yb_1],
            total,
            last=(own_spots, rims, step % 2 == 1),
            name="last_rows",
        )
        traces.append(trace)
    scale = 1.0 / (count_x * count_y * row_count * block)
    early = butterfly(jnp.concatenate([traces[0], traces[1]], axis=0), count_x, count_y)
    late = butterfly(traces[2], count_x, count_y)
    occupation = jnp.stack([early[0, 0], early[1, 0], early[1, 0], late[0, 0]]) * scale
    return (current.reshape(density.shape), occupation)


def solution(mesh):
    in_specs = (
        P("gx", "gy", None, None, None),
        P("gx", "gy", None),
        P("gx", "gy", None, None),
        P("gx", "gy", None),
    )
    out_specs = (P("gx", "gy", None, None, None), P())
    return jax.shard_map(shards, mesh=mesh, in_specs=in_specs, out_specs=out_specs, check_vma=False)
```

```python
import functools

import jax
import jax.numpy as jnp
import numpy as np
from jax import lax
from jax.experimental import pallas as pl
from jax.experimental.pallas import tpu as pltpu
from jax.sharding import PartitionSpec as P

STEPS = 2
AXES = ("gx", "gy")
LANES = 128
TILE = 256

step_x = np.array([-1, -1, -1, 0, 0, 1, 1, 1])
step_y = np.array([-1, 0, 1, -1, 1, -1, 0, 1])
send_order = (0, 7, 2, 5, 1, 6, 3, 4)

GROUPS = ("C", "A", "Y", "CA", "B", "YA", "CB", "YB")
FRAME = {
    "C": (0, 1),
    "A": (1, 0),
    "Y": (0, -1),
    "CA": (1, 1),
    "B": (-1, 0),
    "YA": (1, -1),
    "CB": (-1, 1),
    "YB": (-1, -1),
}


def flat_perm(count_x, count_y, move):
    pairs = []
    for i in range(count_x):
        for j in range(count_y):
            x, y = move(i, j)
            pairs.append((i * count_y + j, (x % count_x) * count_y + y % count_y))
    return pairs


def toward_a(i, j):
    return i ^ 1, j


def along_b(i, j):
    return (i + 2 if i % 2 == 0 else i - 2), j


def toward_c(i, j):
    return i, j ^ 1


def toward_y(i, j):
    return i, (j - 1 if j % 2 == 0 else j + 1)


def split(value):
    high = value.astype(jnp.bfloat16)
    low = (value - high.astype(jnp.float32)).astype(jnp.bfloat16)
    return high, low


def trace_of(block):
    row = lax.broadcasted_iota(jnp.int32, block.shape, 0)
    lane = lax.broadcasted_iota(jnp.int32, block.shape, 1)
    return jnp.sum(jnp.where(row == lane, block, 0.0))


def quotient(value, by, most):
    total = jnp.zeros_like(value)
    for k in range(1, most + 1):
        total += (value >= by * k).astype(jnp.int32)
    return total


VMEM = pl.BlockSpec(memory_space=pltpu.VMEM)
SMEM = pl.BlockSpec(memory_space=pltpu.SMEM)


def pack(moves, rims, cols, rows, count_x, count_y):
    row_count, block, strip = rows.shape
    slots = cols.shape[1]
    rim_count = rims.shape[0]
    tiles = strip // LANES
    ways = len(step_x)

    def kernel(moves_ref, rims_ref, cols_ref, rows_ref, *refs):
        outs, (slots_ref, codes_ref, tail_ref) = refs[:ways], refs[ways:]
        index_x = lax.axis_index("gx")
        index_y = lax.axis_index("gy")
        cols = cols_ref[...]
        inner = jnp.full(cols.shape, -1, jnp.int32)
        for m in range(rim_count):
            inner = jnp.where(cols == rims_ref[m], 4 * rim_count + m, inner)
        away = cols - row_count
        direction = quotient(away, rim_count, ways - 1)
        place = direction + (direction >= 4).astype(jnp.int32)
        code = jnp.where(
            cols < row_count, inner, place * rim_count + away - direction * rim_count
        )
        codes_ref[...] = jnp.zeros(codes_ref.shape, jnp.float32)
        tail_ref[...] = jnp.zeros(tail_ref.shape, jnp.float32)
        codes_ref[:, :slots] = code.astype(jnp.float32)
        for m in range(rim_count):
            tail_ref[pl.ds(m, 1), :] = codes_ref[pl.ds(rims_ref[m], 1), :]
        for d in range(ways):
            x = lax.rem(index_x + int(step_x[d]) + count_x, count_x)
            y = lax.rem(index_y + int(step_y[d]) + count_y, count_y)
            first = (x * count_y + y) * row_count
            slot = jnp.int32(0)
            for r in range(1, row_count):
                target = moves_ref[r]
                slot = jnp.where((target >= first) & (target < first + row_count), r, slot)
            slots_ref[d] = slot
            for k in range(tiles):
                outs[d][k * block : (k + 1) * block, :] = rows_ref[
                    slot, :, k * LANES : (k + 1) * LANES
                ]
            outs[d][tiles * block :, :] = tail_ref[...]

    message = jax.ShapeDtypeStruct((tiles * block + 8, LANES), jnp.float32)
    return pl.pallas_call(
        kernel,
        out_shape=(message,) * ways + (jax.ShapeDtypeStruct((ways,), jnp.int32),),
        in_specs=[SMEM, SMEM, VMEM, VMEM],
        out_specs=(VMEM,) * ways + (SMEM,),
        scratch_shapes=[
            pltpu.VMEM((row_count, LANES), jnp.float32),
            pltpu.VMEM((8, LANES), jnp.float32),
        ],
        compiler_params=pltpu.CompilerParams(vmem_limit_bytes=16 * 2**20),
        name="pack_rows",
    )(moves, rims, cols, rows)


def place(slots, rims, arrived, strip):
    rows = len(arrived)
    tiles = strip // LANES
    block = (arrived[0].shape[0] - 8) // tiles
    count = rims.shape[0]
    half = count // 2

    def kernel(slots_ref, rims_ref, *refs):
        ins, outs = refs[:rows], refs[rows:]
        current_ref, rim_ref, first_ref, second_ref, trace_ref = outs
        total = jnp.float32(0.0)
        for d in range(rows):
            for k in range(tiles):
                current_ref[slots_ref[d], :, k * LANES : (k + 1) * LANES] = ins[d][
                    k * block : (k + 1) * block, :
                ]
            total += trace_of(ins[d][:block, :])
        trace_ref[0] = total
        for m in range(count):
            row = current_ref[rims_ref[m]]
            rim_ref[m] = row
            (first_ref if m < half else second_ref)[m % half] = row

    rim = lambda n: jax.ShapeDtypeStruct((n, block, strip), jnp.float32)
    return pl.pallas_call(
        kernel,
        out_shape=(rim(rows), rim(count), rim(half), rim(half))
        + (jax.ShapeDtypeStruct((1,), jnp.float32),),
        in_specs=[SMEM, SMEM] + [VMEM] * rows,
        out_specs=(VMEM, VMEM, VMEM, VMEM, SMEM),
        compiler_params=pltpu.CompilerParams(vmem_limit_bytes=16 * 2**20),
        name="place_rows",
    )(slots, rims, *arrived)


def tables(rims, cols, arrived):
    rows, slots = cols.shape
    rim_count = rims.shape[0]
    pool = rows + len(GROUPS) * rim_count
    tail = arrived[0].shape[0] // 8 - 1
    base_of = [0] * 9
    for g, name in enumerate(GROUPS):
        x, y = FRAME[name]
        base_of[3 * (x + 1) + y + 1] = rows + g * rim_count

    def kernel(rims_ref, cols_ref, *refs):
        tails, (spots_ref, table_ref, all_ref) = refs[: len(arrived)], refs[len(arrived) :]
        sign_x = 1 - 2 * lax.rem(lax.axis_index("gx"), 2)
        sign_y = 1 - 2 * lax.rem(lax.axis_index("gy"), 2)

        def locate(place, index, shift_x, shift_y):
            third = quotient(place, 3, 2)
            x = (third - 1) * sign_x + shift_x
            y = (place - 3 * third - 1) * sign_y + shift_y
            inside = (x >= -1) & (x <= 1) & (y >= -1) & (y <= 1)
            at = 3 * (x + 1) + y + 1
            spot = index
            for k in range(9):
                if k != 4:
                    spot = spot + jnp.where(at == k, base_of[k], 0)
            for m in range(rim_count):
                spot = jnp.where((at == 4) & (index == m), rims_ref[m], spot)
            return jnp.where(inside, spot, -1)

        cols = cols_ref[...]
        away = cols - rows
        direction = quotient(away, rim_count, 7)
        place = direction + (direction >= 4).astype(jnp.int32)
        spots = locate(place, away - direction * rim_count, 0, 0)
        spots = jnp.where(cols < rows, cols, spots)
        spots_ref[...] = spots
        all_ref[...] = jnp.full(all_ref.shape, -1, jnp.int32)
        all_ref[:rows, :slots] = spots
        for d in range(len(arrived)):
            x = -int(step_x[d]) * sign_x
            y = -int(step_y[d]) * sign_y
            at = 3 * (x + 1) + y + 1
            base = jnp.int32(0)
            for k in range(9):
                base = jnp.where(at == k, base_of[k], base)
            near = tails[d][...].astype(jnp.int32)
            place = quotient(near, rim_count, 8)
            spots = locate(place, near - place * rim_count, x, y)
            spots = jnp.where(near < 0, -1, spots)
            for m in range(rim_count):
                all_ref[pl.ds(base + m, 1), :] = spots[m : m + 1, :]
        lane = lax.broadcasted_iota(jnp.int32, (pool, LANES), 1)
        found = jnp.full((pool, LANES), -1, jnp.int32)
        for u in range(slots):
            found = jnp.where(all_ref[:, u : u + 1] == lane, u, found)
        entry = (found >> 1) + 16 * ((found ^ lane) & 1)
        table_ref[...] = jnp.where(found < 0, slots // 2, entry)

    last = pl.BlockSpec((8, LANES), lambda n: (tail, 0))
    full = lambda shape: pl.BlockSpec(shape, lambda n: (0, 0))
    return pl.pallas_call(
        kernel,
        grid=(1,),
        out_shape=(
            jax.ShapeDtypeStruct((rows, slots), jnp.int32),
            jax.ShapeDtypeStruct((pool, LANES), jnp.int32),
        ),
        in_specs=[SMEM, full((rows, slots))] + [last] * len(arrived),
        out_specs=(full((rows, slots)), full((pool, LANES))),
        scratch_shapes=[pltpu.VMEM((pool, LANES), jnp.int32)],
        name="make_tables",
    )(rims, cols, *arrived)


def spread(parts, high_ref, low_ref):
    base = 0
    strip = parts[0].shape[2]
    for ref in parts:

        def one(c, carry, ref=ref, base=base):
            at = pl.ds(pl.multiple_of((base + c) * 64, 64), 64)
            for k in range(strip // LANES):
                to = pl.ds(k * LANES, LANES)
                value = ref[c, :, to]
                for turn in range(2):
                    high, low = split(pltpu.roll(value, 64, 1) if turn else value)
                    high_ref[turn, at, to] = high
                    low_ref[turn, at, to] = low
            zeros = jnp.zeros((64, LANES), jnp.bfloat16)
            high_ref[0, at, pl.ds(strip, LANES)] = zeros
            low_ref[0, at, pl.ds(strip, LANES)] = zeros
            return carry

        lax.fori_loop(0, ref.shape[0], one, 0)
        base += ref.shape[0]


def fill(table_ref, first, member, members, tile, source, targets):
    left_half = lax.broadcasted_iota(jnp.int32, (64, LANES), 1) < 64
    spot = tile * (TILE // 64)
    for c in range(members):
        at = pl.ds(pl.multiple_of((member + c) * 64, 64), 64)
        for q in range(TILE // LANES):
            left = table_ref[first + member + c, spot + 2 * q]
            right = table_ref[first + member + c, spot + 2 * q + 1]
            from_left = pl.ds(pl.multiple_of((left & 15) * LANES, LANES), LANES)
            from_right = pl.ds(pl.multiple_of((right & 15) * LANES, LANES), LANES)
            for k in range(2):
                value = jnp.where(
                    left_half,
                    source[k][left >> 4, at, from_left],
                    source[k][right >> 4, at, from_right],
                )
                for refs, lane in targets:
                    to = pl.ds(pl.multiple_of(lane + q * LANES, LANES), LANES)
                    refs[k][pl.ds(c * 64, 64), to] = value


def three_products(a_high, a_low, d_high, d_low):
    left = jnp.concatenate([a_high, a_high, a_low], axis=1)
    right = jnp.concatenate([d_high, d_low, d_high], axis=0)
    return jnp.dot(left, right, preferred_element_type=jnp.float32)


def wide_scratch(members, strip):
    return [pltpu.VMEM((2, members * 64, strip + LANES), jnp.bfloat16)] * 2


def pipelined(units, fill_one, multiply, buffers):
    even, odd = buffers
    fill_one(jnp.int32(0), even)

    def two(j, carry):
        fill_one(2 * j + 1, odd)
        multiply(2 * j, even)
        fill_one(jnp.minimum(2 * j + 2, units - 1), even)
        multiply(2 * j + 1, odd)
        return carry

    lax.fori_loop(0, units // 2, two, 0)
    if units % 2:
        multiply(units - 1, even)


def own_product(table, current):
    rows, block, strip = current.shape
    width = table.shape[0] * block
    depth = rows * block
    tiles = width // TILE

    def kernel(table_ref, current_ref, high_ref, low_ref, total_ref, *scratch):
        wide, own, even, odd = scratch[0:2], scratch[2:4], scratch[4:6], scratch[6:8]
        spread([current_ref], *wide)
        for n in range(depth // TILE):
            fill(table_ref, 0, 0, rows, n, wide, [(own, n * TILE)])

        def fill_one(n, buffers):
            fill(table_ref, 0, 0, rows, n, wide, [(buffers, 0), ((high_ref, low_ref), n * TILE)])

        def multiply(n, buffers):
            to = pl.ds(pl.multiple_of(n * TILE, TILE), TILE)
            total_ref[:, to] = three_products(
                own[0][...], own[1][...], buffers[0][...], buffers[1][...]
            )

        pipelined(tiles, fill_one, multiply, (even, odd))

    dense = lambda t: jax.ShapeDtypeStruct((depth, width), t)
    return pl.pallas_call(
        kernel,
        out_shape=(dense(jnp.bfloat16), dense(jnp.bfloat16), dense(jnp.float32)),
        in_specs=[SMEM, VMEM],
        out_specs=(VMEM, VMEM, VMEM),
        scratch_shapes=wide_scratch(rows, strip)
        + [pltpu.VMEM((depth, depth), jnp.bfloat16)] * 2
        + [pltpu.VMEM((depth, TILE), jnp.bfloat16)] * 4,
        compiler_params=pltpu.CompilerParams(vmem_limit_bytes=24 * 2**20),
        cost_estimate=cost(2 * tiles),
        name="own_product",
    )(table, current)


def cost(units):
    return pl.CostEstimate(
        flops=units * 3 * 2 * 512 * TILE * TILE * 2, bytes_accessed=12 * 2**20, transcendentals=0
    )


def columns_of(name):
    x, y = FRAME[name]
    tiles = [0, 1]
    for g, other in enumerate(GROUPS):
        if abs(FRAME[other][0] - x) <= 1 and abs(FRAME[other][1] - y) <= 1:
            tiles.append(2 + g)
    return tiles


def add_product(names, table, high, low, parts, total, label, last=None):
    depth_own, width = total.shape
    _, block, strip = parts[0].shape
    rows = depth_own // block
    count = TILE // block
    members = count * len(names)
    start = GROUPS.index(names[0])
    first = rows + start * count
    lists = [columns_of(name) for name in names]
    begins = [sum(len(t) for t in lists[:k]) for k in range(len(lists) + 1)]
    codes = [sum(t << (4 * k) for k, t in enumerate(tiles)) for tiles in lists]

    def unit(i):
        group, begin, code = jnp.int32(0), jnp.int32(0), jnp.int32(codes[0])
        for k in range(1, len(lists)):
            after = i >= begins[k]
            group = jnp.where(after, k, group)
            begin = jnp.where(after, begins[k], begin)
            code = jnp.where(after, codes[k], code)
        return group, (code >> (4 * (i - begin))) & 15

    def kernel(table_ref, high_ref, low_ref, *refs):
        refs = list(refs)
        part_refs = [refs.pop(0) for _ in parts]
        total_in = refs.pop(0)
        if last is not None:
            spots_ref, rims_ref, traces_ref, current_ref = (refs.pop(0) for _ in range(4))
            out_ref, rim_ref, first_ref, second_ref, trace_ref = (refs.pop(0) for _ in range(5))
            total_ref = refs.pop(-1)
        else:
            total_ref = refs.pop(0)
        wide, even, odd = refs[0:2], refs[2:4], refs[4:6]
        spread(part_refs, *wide)

        def fill_one(i, buffers):
            group, tile = unit(i)
            fill(table_ref, first, group * count, count, tile, wide, [(buffers, 0)])

        def multiply(i, buffers):
            group, tile = unit(i)
            at = pl.ds(pl.multiple_of(first * block + group * TILE, TILE), TILE)
            to = pl.ds(pl.multiple_of(tile * TILE, TILE), TILE)
            total_ref[:, to] = total_in[:, to] + three_products(
                high_ref[:, at], low_ref[:, at], buffers[0][...], buffers[1][...]
            )

        if last is not None:
            for n in range(width // TILE):
                if n not in lists[0]:
                    to = pl.ds(n * TILE, TILE)
                    total_ref[:, to] = total_in[:, to]
        pipelined(begins[-1], fill_one, multiply, (even, odd))
        if last is None:
            return
        known = traces_ref.shape[0]
        for k in range(known):
            trace_ref[k] = traces_ref[k]
        lane = lax.broadcasted_iota(jnp.int32, (64, LANES), 1)

        def one_row(g, trace):
            at = pl.ds(pl.multiple_of(g * 64, 64), 64)
            for k in range(strip // LANES):
                sides = []
                for side in range(2):
                    spot = spots_ref[g, 2 * k + side]
                    tile = pl.ds(pl.multiple_of((spot >> 1) * LANES, LANES), LANES)
                    sides.append(pltpu.roll(total_ref[at, tile], ((spot ^ side) & 1) * 64, 1))
                value = jnp.where(lane < 64, *sides)
                if k == 0:
                    trace += trace_of(value)
                to = pl.ds(k * LANES, LANES)
                if blend:
                    value = 2.0 * current_ref[g, :, to] - value
                out_ref[g, :, to] = value
            return trace

        trace_ref[known] = lax.fori_loop(0, rows, one_row, jnp.float32(0.0))
        for m in range(count):
            row = out_ref[rims_ref[m]]
            rim_ref[m] = row
            (first_ref if m < count // 2 else second_ref)[m % (count // 2)] = row

    ins = [table, high, low, *parts, total]
    in_specs = [SMEM] + [VMEM] * (3 + len(parts))
    if last is None:
        out_shape = (jax.ShapeDtypeStruct((depth_own, width), jnp.float32),)
        small = ()
    else:
        spots, rims, traces, current, blend = last
        ins += [spots, rims, traces, current]
        in_specs += [SMEM, SMEM, SMEM, VMEM]
        shape = lambda n: jax.ShapeDtypeStruct((n, block, strip), jnp.float32)
        out_shape = (shape(rows), shape(count), shape(count // 2), shape(count // 2))
        small = (jax.ShapeDtypeStruct((traces.shape[0] + 1,), jnp.float32),)
    scratch = wide_scratch(members, strip) + [pltpu.VMEM((TILE, TILE), jnp.bfloat16)] * 4
    if last is not None:
        scratch.append(pltpu.VMEM((depth_own, width), jnp.float32))
    result = pl.pallas_call(
        kernel,
        out_shape=out_shape + small,
        in_specs=in_specs,
        out_specs=(VMEM,) * len(out_shape) + (SMEM,) * len(small),
        scratch_shapes=scratch,
        input_output_aliases={3 + len(parts): 0} if last is None else {},
        compiler_params=pltpu.CompilerParams(vmem_limit_bytes=24 * 2**20),
        cost_estimate=cost(begins[-1]),
        name=label,
    )(*ins)
    return result[0] if last is None else result


def sum_everywhere(value, count_x, count_y):
    for count, at in ((count_y, 1), (count_x, 0)):
        bit = 1
        while bit < count:
            send = lambda b: lax.ppermute(
                value,
                AXES,
                flat_perm(
                    count_x, count_y, lambda i, j: (i, j ^ b) if at else (i ^ b, j)
                ),
            )
            if 2 * bit < count:
                one, two, three = send(bit), send(2 * bit), send(3 * bit)
                value = (value + one) + (two + three)
                bit *= 4
            else:
                value = value + send(bit)
                bit *= 2
    return value


def shards(density, moves, cols, halo_rows):
    row_count, block, strip = density.shape[2:]
    rim_count = halo_rows.shape[2]
    count_x = lax.axis_size("gx")
    count_y = lax.axis_size("gy")
    rows = density.reshape(row_count, block, strip)
    rims = halo_rows.reshape(rim_count)
    own_cols = cols.reshape(row_count, -1)

    *leaving, slots = pack(moves.reshape(row_count), rims, own_cols, rows, count_x, count_y)
    arrived = [None] * len(step_x)
    for d in send_order:
        dx, dy = int(step_x[d]), int(step_y[d])
        perm = flat_perm(count_x, count_y, lambda i, j: (i + dx, j + dy))
        arrived[d] = lax.ppermute(leaving[d], AXES, perm)

    current, rim, rim_0, rim_1, traces = place(slots, rims, arrived, strip)
    spots, table = tables(rims, own_cols, arrived)
    swap = {
        "A": flat_perm(count_x, count_y, toward_a),
        "B": flat_perm(count_x, count_y, along_b),
        "C": flat_perm(count_x, count_y, toward_c),
        "Y": flat_perm(count_x, count_y, toward_y),
    }
    go = lambda value, way: lax.ppermute(value, AXES, swap[way])
    for step in range(STEPS):
        a_0, y_0 = go(rim_0, "A"), go(rim_0, "Y")
        a_1, y_1 = go(rim_1, "A"), go(rim_1, "Y")
        c = go(rim, "C")
        high, low, total = own_product(table, current)
        a_0, y_0, total = lax.optimization_barrier((a_0, y_0, total))
        b_0, ya_0, ca_0 = go(a_0, "B"), go(y_0, "A"), go(a_0, "C")
        b_1, ya_1, ca_1 = go(a_1, "B"), go(a_1, "Y"), go(a_1, "C")
        add = functools.partial(add_product, table=table, high=high, low=low)
        total = add(
            ("C", "A", "Y"), parts=[c, a_0, a_1, y_0, y_1], total=total, label="near_product"
        )
        b_0, b_1, ya_0, total = lax.optimization_barrier((b_0, b_1, ya_0, total))
        cb_0, cb_1 = go(b_0, "C"), go(b_1, "C")
        yb_0, yb_1 = go(ya_0, "B"), go(b_1, "Y")
        corner = [ca_0, ca_1, b_0, b_1, ya_0, ya_1, cb_0, cb_1]
        total = add(("CA", "B", "YA", "CB"), parts=corner, total=total, label="corner_product")
        last = (spots, rims, traces, current, step % 2 == 1)
        current, rim, rim_0, rim_1, traces = add(
            ("YB",), parts=[yb_0, yb_1], total=total, label="last_product", last=last
        )
    scale = 1.0 / (count_x * count_y * row_count * block)
    sums = sum_everywhere(traces, count_x, count_y) * scale
    occupation = jnp.stack([sums[0], sums[1], sums[1], sums[2]])
    return (current.reshape(density.shape), occupation)


def solution(mesh):
    in_specs = (
        P("gx", "gy", None, None, None),
        P("gx", "gy", None),
        P("gx", "gy", None, None),
        P("gx", "gy", None),
    )
    out_specs = (P("gx", "gy", None, None, None), P())
    return jax.shard_map(shards, mesh=mesh, in_specs=in_specs, out_specs=out_specs, check_vma=False)
```

```python
import functools

import jax
import jax.numpy as jnp
import numpy as np
from jax import lax
from jax.experimental import pallas as pl
from jax.experimental.pallas import tpu as pltpu
from jax.sharding import PartitionSpec as P

STEPS = 2
AXES = ("gx", "gy")
LANES = 128
TILE = 256

step_x = np.array([0, 0, -1, 1, -1, 1, -1, 1])
step_y = np.array([-1, 1, -1, 1, 1, -1, 0, 0])

FRAME = {
    "C": (0, 1),
    "A": (1, 0),
    "Y": (0, -1),
    "CA": (1, 1),
    "B": (-1, 0),
    "YA": (1, -1),
    "CB": (-1, 1),
    "YB": (-1, -1),
}


OWN_TILES = 2
TILES = (
    (("C", 0, 4),),
    (("A", 2, 2), ("Y", 0, 2)),
    (("A", 0, 2), ("Y", 2, 2)),
    (("B", 2, 2), ("YA", 2, 2)),
    (("B", 0, 2), ("YA", 0, 2)),
    (("CA", 0, 4),),
    (("CB", 0, 4),),
    (("YB", 0, 4),),
)


def pool_places(rows):
    places = {}
    for t, members in enumerate(TILES):
        at = rows + 4 * t
        for name, begin, count in members:
            places.setdefault(name, [0, 0])
            if begin == 0:
                places[name][0] = at
            if begin + count == 4:
                places[name][1] = at + count - 2
            at += count
    return places


def reach(t):
    def frames(n):
        return [(0, 0)] if n < OWN_TILES else [FRAME[m[0]] for m in TILES[n - OWN_TILES]]

    near = lambda p, q: abs(p[0] - q[0]) <= 1 and abs(p[1] - q[1]) <= 1
    count = OWN_TILES + len(TILES)
    found = [n for n in range(count) if any(near(p, q) for p in frames(t) for q in frames(n))]
    if len(found) % 2:
        found.append(next(n for n in range(count) if n not in found))
    return found


def flat_perm(count_x, count_y, move):
    pairs = []
    for i in range(count_x):
        for j in range(count_y):
            x, y = move(i, j)
            pairs.append((i * count_y + j, (x % count_x) * count_y + y % count_y))
    return pairs


def toward_a(i, j):
    return i ^ 1, j


def along_b(i, j):
    return (i + 2 if i % 2 == 0 else i - 2), j


def toward_c(i, j):
    return i, j ^ 1


def toward_y(i, j):
    return i, (j - 1 if j % 2 == 0 else j + 1)


def split(value):
    high = value.astype(jnp.bfloat16)
    low = (value - high.astype(jnp.float32)).astype(jnp.bfloat16)
    return high, low


def trace_of(block):
    row = lax.broadcasted_iota(jnp.int32, block.shape, 0)
    lane = lax.broadcasted_iota(jnp.int32, block.shape, 1)
    return jnp.sum(jnp.where(row == lane, block, 0.0))


def quotient(value, by, most):
    total = jnp.zeros_like(value)
    for k in range(1, most + 1):
        total += (value >= by * k).astype(jnp.int32)
    return total


VMEM = pl.BlockSpec(memory_space=pltpu.VMEM)
SMEM = pl.BlockSpec(memory_space=pltpu.SMEM)


def pack(moves, rims, cols, rows, count_x, count_y):
    row_count, block, strip = rows.shape
    slots = cols.shape[1]
    rim_count = rims.shape[0]
    tiles = strip // LANES
    ways = len(step_x)

    def kernel(moves_in, rims_in, cols_in, rows_in, *refs):
        outs, refs = refs[:ways], refs[ways:]
        small_ref, cols_ref, moves_ref, rims_ref, rows_ref, codes_ref, tail_ref, sems = refs
        copies = [
            pltpu.make_async_copy(source, target, sems.at[k])
            for k, (source, target) in enumerate(
                (
                    (moves_in, moves_ref),
                    (rims_in, rims_ref),
                    (cols_in, cols_ref),
                    (rows_in, rows_ref),
                )
            )
        ]
        for copy in copies:
            copy.start()
        index_x = lax.axis_index("gx")
        index_y = lax.axis_index("gy")
        for copy in copies[:3]:
            copy.wait()
        cols = cols_ref[...]
        inner = jnp.full(cols.shape, -1, jnp.int32)
        for m in range(rim_count):
            small_ref[ways + m] = rims_ref[m]
            inner = jnp.where(cols == rims_ref[m], 4 * rim_count + m, inner)
        away = cols - row_count
        direction = quotient(away, rim_count, ways - 1)
        place = direction + (direction >= 4).astype(jnp.int32)
        code = jnp.where(
            cols < row_count, inner, place * rim_count + away - direction * rim_count
        )
        codes_ref[...] = jnp.zeros(codes_ref.shape, jnp.float32)
        tail_ref[...] = jnp.zeros(tail_ref.shape, jnp.float32)
        codes_ref[:, :slots] = code.astype(jnp.float32)
        for m in range(rim_count):
            tail_ref[pl.ds(m, 1), :] = codes_ref[pl.ds(rims_ref[m], 1), :]
        leaving = []
        for d in range(ways):
            x = lax.rem(index_x + int(step_x[d]) + count_x, count_x)
            y = lax.rem(index_y + int(step_y[d]) + count_y, count_y)
            first = (x * count_y + y) * row_count
            slot = jnp.int32(0)
            for r in range(1, row_count):
                target = moves_ref[r]
                slot = jnp.where((target >= first) & (target < first + row_count), r, slot)
            small_ref[d] = slot
            leaving.append(slot)
        copies[3].wait()
        for d in range(ways):
            for k in range(tiles):
                outs[d][k * block : (k + 1) * block, :] = rows_ref[
                    leaving[d], :, k * LANES : (k + 1) * LANES
                ]
            outs[d][tiles * block :, :] = tail_ref[...]

    message = jax.ShapeDtypeStruct((tiles * block + 8, LANES), jnp.float32)
    return pl.pallas_call(
        kernel,
        out_shape=(message,) * ways
        + (
            jax.ShapeDtypeStruct((ways + rim_count,), jnp.int32),
            jax.ShapeDtypeStruct(cols.shape, jnp.int32),
        ),
        in_specs=[pl.BlockSpec(memory_space=pltpu.HBM)] * 4,
        out_specs=(VMEM,) * ways + (SMEM, VMEM),
        scratch_shapes=[
            pltpu.SMEM((row_count,), jnp.int32),
            pltpu.SMEM((rim_count,), jnp.int32),
            pltpu.VMEM(rows.shape, jnp.float32),
            pltpu.VMEM((row_count, LANES), jnp.float32),
            pltpu.VMEM((8, LANES), jnp.float32),
            pltpu.SemaphoreType.DMA((4,)),
        ],
        compiler_params=pltpu.CompilerParams(vmem_limit_bytes=16 * 2**20),
        name="pack_rows",
    )(moves, rims, cols, rows)


def share(rows_ref, small_ref, rim_refs):
    rim_ref, a_1, y_0, a_0, y_1 = rim_refs
    count = rim_ref.shape[0]
    for m in range(count):
        row = rows_ref[small_ref[len(step_x) + m]]
        rim_ref[m] = row
        for ref in (a_0, y_0) if m < count // 2 else (a_1, y_1):
            ref[m % (count // 2)] = row


def place(small, arrived, strip):
    rows = len(arrived)
    tiles = strip // LANES
    block = (arrived[0].shape[0] - 8) // tiles
    count = small.shape[0] - rows
    half = count // 2

    def kernel(small_ref, *refs):
        ins, outs = refs[:rows], refs[rows:]
        current_ref, *rim_refs, trace_ref = outs
        total = jnp.float32(0.0)
        for d in range(rows):
            for k in range(tiles):
                current_ref[small_ref[d], :, k * LANES : (k + 1) * LANES] = ins[d][
                    k * block : (k + 1) * block, :
                ]
            total += trace_of(ins[d][:block, :])
        trace_ref[0] = total
        share(current_ref, small_ref, rim_refs)

    rim = lambda n: jax.ShapeDtypeStruct((n, block, strip), jnp.float32)
    return pl.pallas_call(
        kernel,
        out_shape=(rim(rows), rim(count), rim(half), rim(half), rim(half), rim(half))
        + (jax.ShapeDtypeStruct((1,), jnp.float32),),
        in_specs=[SMEM] + [VMEM] * rows,
        out_specs=(VMEM,) * 6 + (SMEM,),
        compiler_params=pltpu.CompilerParams(vmem_limit_bytes=16 * 2**20),
        name="place_rows",
    )(small, *arrived)


def tables(small, cols, arrived):
    rows, slots = cols.shape
    rim_count = small.shape[0] - len(arrived)
    half = rim_count // 2
    pool = rows + len(TILES) * rim_count
    tail = arrived[0].shape[0] // 8 - 1
    base_of = [[0, 0]] * 9
    for name, (one, two) in pool_places(rows).items():
        x, y = FRAME[name]
        base_of[3 * (x + 1) + y + 1] = [one, two - half]

    def kernel(small_ref, cols_ref, *refs):
        tails, (spots_ref, table_ref, all_ref) = refs[: len(arrived)], refs[len(arrived) :]
        sign_x = 1 - 2 * lax.rem(lax.axis_index("gx"), 2)
        sign_y = 1 - 2 * lax.rem(lax.axis_index("gy"), 2)

        def locate(place, index, shift_x, shift_y):
            third = quotient(place, 3, 2)
            x = (third - 1) * sign_x + shift_x
            y = (place - 3 * third - 1) * sign_y + shift_y
            inside = (x >= -1) & (x <= 1) & (y >= -1) & (y <= 1)
            at = 3 * (x + 1) + y + 1
            one = two = jnp.zeros_like(index)
            for k in range(9):
                one = jnp.where(at == k, base_of[k][0], one)
                two = jnp.where(at == k, base_of[k][1], two)
            spot = index + jnp.where(index < half, one, two)
            for m in range(rim_count):
                spot = jnp.where((at == 4) & (index == m), small_ref[len(arrived) + m], spot)
            return jnp.where(inside, spot, -1)

        cols = cols_ref[...]
        away = cols - rows
        direction = quotient(away, rim_count, 7)
        place = direction + (direction >= 4).astype(jnp.int32)
        spots = locate(place, away - direction * rim_count, 0, 0)
        spots = jnp.where(cols < rows, cols, spots)
        spots_ref[...] = spots
        all_ref[...] = jnp.full(all_ref.shape, -1, jnp.int32)
        all_ref[:rows, :slots] = spots
        for d in range(len(arrived)):
            x = -int(step_x[d]) * sign_x
            y = -int(step_y[d]) * sign_y
            at = 3 * (x + 1) + y + 1
            bases = []
            for part in range(2):
                base = jnp.int32(0)
                for k in range(9):
                    base = jnp.where(at == k, base_of[k][part], base)
                bases.append(base)
            near = tails[d][...].astype(jnp.int32)
            place = quotient(near, rim_count, 8)
            spots = locate(place, near - place * rim_count, x, y)
            spots = jnp.where(near < 0, -1, spots)
            for m in range(rim_count):
                all_ref[pl.ds(bases[m // half] + m, 1), :] = spots[m : m + 1, :]
        lane = lax.broadcasted_iota(jnp.int32, (pool, LANES), 1)
        found = jnp.full((pool, LANES), -1, jnp.int32)
        for u in range(slots):
            found = jnp.where(all_ref[:, u : u + 1] == lane, u, found)
        entry = (found >> 1) + 16 * ((found ^ lane) & 1)
        table_ref[...] = jnp.where(found < 0, slots // 2, entry)

    last = pl.BlockSpec((8, LANES), lambda n: (tail, 0))
    full = lambda shape: pl.BlockSpec(shape, lambda n: (0, 0))
    return pl.pallas_call(
        kernel,
        grid=(1,),
        out_shape=(
            jax.ShapeDtypeStruct((rows, slots), jnp.int32),
            jax.ShapeDtypeStruct((pool, LANES), jnp.int32),
        ),
        in_specs=[SMEM, full((rows, slots))] + [last] * len(arrived),
        out_specs=(full((rows, slots)), full((pool, LANES))),
        scratch_shapes=[pltpu.VMEM((pool, LANES), jnp.int32)],
        name="make_tables",
    )(small, cols, *arrived)


def spread(parts, high_ref, low_ref):
    base = 0
    strip = parts[0].shape[2]
    for ref in parts:

        def one(c, carry, ref=ref, base=base):
            at = pl.ds(pl.multiple_of((base + c) * 64, 64), 64)
            for k in range(strip // LANES):
                to = pl.ds(k * LANES, LANES)
                value = ref[c, :, to]
                for turn in range(2):
                    high, low = split(pltpu.roll(value, 64, 1) if turn else value)
                    high_ref[turn, at, to] = high
                    low_ref[turn, at, to] = low
            zeros = jnp.zeros((64, LANES), jnp.bfloat16)
            high_ref[0, at, pl.ds(strip, LANES)] = zeros
            low_ref[0, at, pl.ds(strip, LANES)] = zeros
            return carry

        lax.fori_loop(0, ref.shape[0], one, 0)
        base += ref.shape[0]


def fill(table_ref, first, member, members, tile, source, targets):
    left_half = lax.broadcasted_iota(jnp.int32, (64, LANES), 1) < 64
    spot = tile * (TILE // 64)
    for c in range(members):
        at = pl.ds(pl.multiple_of((member + c) * 64, 64), 64)
        for q in range(TILE // LANES):
            left = table_ref[first + member + c, spot + 2 * q]
            right = table_ref[first + member + c, spot + 2 * q + 1]
            from_left = pl.ds(pl.multiple_of((left & 15) * LANES, LANES), LANES)
            from_right = pl.ds(pl.multiple_of((right & 15) * LANES, LANES), LANES)
            for k in range(2):
                value = jnp.where(
                    left_half,
                    source[k][left >> 4, at, from_left],
                    source[k][right >> 4, at, from_right],
                )
                for refs, lane in targets:
                    to = pl.ds(pl.multiple_of(lane + q * LANES, LANES), LANES)
                    refs[k][pl.ds(c * 64, 64), to] = value


def three_products(a_high, a_low, d_high, d_low):
    left = jnp.concatenate([a_high, a_high, a_low], axis=1)
    right = jnp.concatenate([d_high, d_low, d_high], axis=0)
    return jnp.dot(left, right, preferred_element_type=jnp.float32)


def wide_scratch(members, strip):
    return [pltpu.VMEM((2, members * 64, strip + LANES), jnp.bfloat16)] * 2


def pipelined(units, fill_one, multiply, buffers):
    even, odd = buffers
    fill_one(jnp.int32(0), even)

    def two(j, carry):
        fill_one(2 * j + 1, odd)
        multiply(2 * j, even)
        fill_one(jnp.minimum(2 * j + 2, units - 1), even)
        multiply(2 * j + 1, odd)
        return carry

    lax.fori_loop(0, units // 2, two, 0)
    if units % 2:
        multiply(units - 1, even)


def lane(tile):
    return pl.multiple_of(tile * TILE, TILE)


def cost(units):
    return pl.CostEstimate(flops=units * 2**27, bytes_accessed=2**16, transcendentals=0)


def spread_own(current):
    rows, block, strip = current.shape

    def kernel(current_ref, high_ref, low_ref):
        spread([current_ref], high_ref, low_ref)

    wide = jax.ShapeDtypeStruct((2, rows * block, strip + LANES), jnp.bfloat16)
    return pl.pallas_call(
        kernel,
        out_shape=(wide, wide),
        in_specs=[VMEM],
        out_specs=(VMEM, VMEM),
        compiler_params=pltpu.CompilerParams(vmem_limit_bytes=16 * 2**20),
        cost_estimate=cost(1),
        name="spread_own",
    )(current)


def own_product(table, wide, rows, block):
    width = table.shape[0] * block
    depth = rows * block
    tiles = width // TILE

    def kernel(table_ref, wide_high, wide_low, high_ref, low_ref, total_ref, *scratch):
        wide = wide_high, wide_low
        own, even, odd = scratch[0:2], scratch[2:4], scratch[4:6]
        for n in range(depth // TILE):
            fill(table_ref, 0, 0, rows, n, wide, [(own, n * TILE)])

        def fill_one(i, buffers):
            for k in range(2):
                fill(
                    table_ref, 0, 0, rows, 2 * i + k, wide,
                    [(buffers, k * TILE), ((high_ref, low_ref), (2 * i + k) * TILE)],
                )

        def multiply(i, buffers):
            to = pl.ds(pl.multiple_of(2 * i * TILE, 2 * TILE), 2 * TILE)
            total_ref[:, to] = three_products(
                own[0][...], own[1][...], buffers[0][...], buffers[1][...]
            )

        pipelined(tiles // 2, fill_one, multiply, (even, odd))

    dense = lambda t: jax.ShapeDtypeStruct((depth, width), t)
    return pl.pallas_call(
        kernel,
        out_shape=(dense(jnp.bfloat16), dense(jnp.bfloat16), dense(jnp.float32)),
        in_specs=[SMEM, VMEM, VMEM],
        out_specs=(VMEM, VMEM, VMEM),
        scratch_shapes=[pltpu.VMEM((depth, depth), jnp.bfloat16)] * 2
        + [pltpu.VMEM((depth, 2 * TILE), jnp.bfloat16)] * 4,
        compiler_params=pltpu.CompilerParams(vmem_limit_bytes=24 * 2**20),
        cost_estimate=cost(2 * tiles),
        name="own_product",
    )(table, *wide)


def extract(spots_ref, total_ref, current_ref, out_ref, blend):
    left_half = lax.broadcasted_iota(jnp.int32, (64, LANES), 1) < 64

    def one_row(g, carry):
        at = pl.ds(pl.multiple_of(g * 64, 64), 64)
        for k in range(out_ref.shape[2] // LANES):
            sides = []
            for side in range(2):
                spot = spots_ref[g, 2 * k + side]
                tile = pl.ds(pl.multiple_of((spot >> 1) * LANES, LANES), LANES)
                sides.append(pltpu.roll(total_ref[at, tile], ((spot ^ side) & 1) * 64, 1))
            value = jnp.where(left_half, *sides)
            to = pl.ds(k * LANES, LANES)
            if blend:
                value = 2.0 * current_ref[g, :, to] - value
            out_ref[g, :, to] = value
        return carry

    lax.fori_loop(0, out_ref.shape[0], one_row, 0)


def add_traces(traces_ref, total_ref, trace_ref):
    known = traces_ref.shape[0]
    for k in range(known):
        trace_ref[k] = traces_ref[k]
    row = lax.broadcasted_iota(jnp.int32, (64, LANES), 0)
    spot = lax.broadcasted_iota(jnp.int32, (64, LANES), 1)
    found = jnp.zeros((64, LANES), jnp.float32)
    for g in range(total_ref.shape[0] // 64):
        block = total_ref[g * 64 : (g + 1) * 64, (g // 2) * LANES : (g // 2 + 1) * LANES]
        found += jnp.where(spot - row == 64 * (g % 2), block, 0.0)
    trace_ref[known] = jnp.sum(found)


def finish(spots, total, current):
    def kernel(spots_ref, total_ref, current_ref, out_ref):
        extract(spots_ref, total_ref, current_ref, out_ref, True)

    return pl.pallas_call(
        kernel,
        out_shape=jax.ShapeDtypeStruct(current.shape, jnp.float32),
        in_specs=[SMEM, VMEM, VMEM],
        out_specs=VMEM,
        compiler_params=pltpu.CompilerParams(vmem_limit_bytes=16 * 2**20),
        cost_estimate=cost(4),
        name="finish",
    )(spots, total, current)


def add_product(begin, count, table, high, low, parts, total, label, lists=None, traces=None, square=None):
    depth_own, width = total.shape
    _, block, strip = parts[0].shape
    rows = depth_own // block
    each = TILE // block
    first = begin * each
    lists = lists or [reach(begin + k) for k in range(count)]
    starts = [sum(len(t) for t in lists[:k]) // 2 for k in range(count + 1)]
    codes = [
        [sum(t << (4 * k) for k, t in enumerate(tiles[side::2])) for side in range(2)]
        for tiles in lists
    ]

    def unit(i):
        group, start = jnp.int32(0), jnp.int32(0)
        code = [jnp.int32(c) for c in codes[0]]
        for k in range(1, count):
            after = i >= starts[k]
            group = jnp.where(after, k, group)
            start = jnp.where(after, starts[k], start)
            code = [jnp.where(after, new, old) for new, old in zip(codes[k], code)]
        return group, [(c >> (4 * (i - start))) & 15 for c in code]

    def kernel(table_ref, high_ref, low_ref, *refs):
        refs = list(refs)
        part_refs = [refs.pop(0) for _ in parts]
        refs.pop(0)
        if traces is not None:
            traces_ref = refs.pop(0)
        if square is not None:
            spots_ref, small_ref = refs.pop(0), refs.pop(0)
        total_ref = refs.pop(0)
        if traces is not None:
            trace_ref = refs.pop(0)
        if square is not None:
            out_ref, *rim_refs = (refs.pop(0) for _ in range(6))
        wide, even, odd = refs[0:2], refs[2:4], refs[4:6]
        spread(part_refs, *wide)

        def fill_one(i, buffers):
            group, tiles = unit(i)
            for k in range(2):
                fill(table_ref, first, group * each, each, tiles[k], wide, [(buffers, k * TILE)])

        def multiply(i, buffers):
            group, tiles = unit(i)
            at = pl.ds(lane(begin + group), TILE)
            value = three_products(
                high_ref[:, at], low_ref[:, at], buffers[0][...], buffers[1][...]
            )
            for k in range(2):
                to = pl.ds(lane(tiles[k]), TILE)
                total_ref[:, to] += value[:, k * TILE : (k + 1) * TILE]

        pipelined(starts[-1], fill_one, multiply, (even, odd))
        if traces is not None:
            add_traces(traces_ref, total_ref, trace_ref)
        if square is not None:
            extract(spots_ref, total_ref, None, out_ref, False)
            share(out_ref, small_ref, rim_refs)

    ins = [table, high, low, *parts, total]
    in_specs = [SMEM] + [VMEM] * (3 + len(parts))
    out_shape = [jax.ShapeDtypeStruct((depth_own, width), jnp.float32)]
    out_specs = [VMEM]
    if traces is not None:
        ins.append(traces)
        in_specs.append(SMEM)
        out_shape.append(jax.ShapeDtypeStruct((traces.shape[0] + 1,), jnp.float32))
        out_specs.append(SMEM)
    if square is not None:
        ins += square
        in_specs += [SMEM, SMEM]
        shape = lambda n: jax.ShapeDtypeStruct((n, block, strip), jnp.float32)
        out_shape += [shape(rows), shape(each)] + [shape(each // 2)] * 4
        out_specs += [VMEM] * 6
    scratch = wide_scratch(count * each, strip)
    scratch += [pltpu.VMEM((TILE, 2 * TILE), jnp.bfloat16)] * 4
    return pl.pallas_call(
        kernel,
        out_shape=out_shape,
        in_specs=in_specs,
        out_specs=out_specs,
        scratch_shapes=scratch,
        input_output_aliases={3 + len(parts): 0},
        compiler_params=pltpu.CompilerParams(vmem_limit_bytes=24 * 2**20),
        cost_estimate=cost(2 * starts[-1]),
        name=label,
    )(*ins)


def sum_rounds(count_x, count_y):
    rounds = []
    for count, at in ((count_y, 1), (count_x, 0)):
        bit = 1
        while bit < count:
            bits = [bit, 2 * bit, 3 * bit] if 2 * bit < count else [bit]
            rounds.append(
                [
                    flat_perm(count_x, count_y, lambda i, j: (i, j ^ b) if at else (i ^ b, j))
                    for b in bits
                ]
            )
            bit *= 4
    return rounds


def sum_round(value, perms):
    others = [lax.ppermute(value, AXES, perm) for perm in perms]
    if len(others) == 1:
        return value + others[0]
    return (value + others[0]) + (others[1] + others[2])


def shards(density, moves, cols, halo_rows):
    row_count, block, strip = density.shape[2:]
    rim_count = halo_rows.shape[2]
    count_x = lax.axis_size("gx")
    count_y = lax.axis_size("gy")
    rows = density.reshape(row_count, block, strip)
    rims = halo_rows.reshape(rim_count)
    own_cols = cols.reshape(row_count, -1)

    *leaving, small, own_cols = pack(
        moves.reshape(row_count), rims, own_cols, rows, count_x, count_y
    )
    arrived = [None] * len(step_x)
    for d in range(len(step_x)):
        dx, dy = int(step_x[d]), int(step_y[d])
        perm = flat_perm(count_x, count_y, lambda i, j: (i + dx, j + dy))
        arrived[d] = lax.ppermute(leaving[d], AXES, perm)

    current, *shared, traces = place(small, arrived, strip)
    spots, table = tables(small, own_cols, arrived)
    swap = {
        "A": flat_perm(count_x, count_y, toward_a),
        "B": flat_perm(count_x, count_y, along_b),
        "C": flat_perm(count_x, count_y, toward_c),
        "Y": flat_perm(count_x, count_y, toward_y),
    }
    go = lambda value, way: lax.ppermute(value, AXES, swap[way])
    rounds = sum_rounds(count_x, count_y)
    tie = lax.optimization_barrier
    for step in range(STEPS):
        c, a_1, y_0 = (go(rim, way) for rim, way in zip(shared[:3], "CAY"))
        wide_high, wide_low = spread_own(current)
        wide_high, *shared = tie((wide_high, *shared[3:]))
        a_0, y_1 = (go(rim, way) for rim, way in zip(shared, "AY"))
        high, low, total = own_product(table, (wide_high, wide_low), row_count, block)
        add = functools.partial(add_product, table=table, high=high, low=low)
        a_1, y_0, c, total = tie((a_1, y_0, c, total))
        b_1, ya_1, ya_0 = go(a_1, "B"), go(a_1, "Y"), go(y_0, "A")
        (total,) = add(2, 2, parts=[c, a_1, y_0], total=total, label="first_product")
        a_0, y_1, total = tie((a_0, y_1, total))
        b_0 = go(a_0, "B")
        (total,) = add(4, 1, parts=[a_0, y_1], total=total, label="second_product")
        a_0, b_1, ya_0, total = tie((a_0, b_1, ya_0, total))
        yb_1, yb_0 = go(b_1, "Y"), go(ya_0, "B")
        ca = go(jnp.concatenate([a_0, a_1]), "C")
        (total,) = add(5, 1, parts=[b_1, ya_1], total=total, label="third_product")
        b_0, total = tie((b_0, total))
        cb = go(jnp.concatenate([b_0, b_1]), "C")
        (total,) = add(6, 2, parts=[b_0, ya_0, ca], total=total, label="fourth_product")
        (total,) = add(8, 1, parts=[cb], total=total, label="fifth_product")
        last = functools.partial(add, 9, 1, parts=[yb_0, yb_1])
        if step % 2 == 0:
            total, traces, current, *shared = last(
                total=total, label="last_product", traces=traces, square=(spots, small)
            )
        else:
            others = [t for t in reach(9) if t >= OWN_TILES]
            total, traces = last(
                total=total, label="trace_product", lists=[list(range(OWN_TILES))], traces=traces
            )
            sums = sum_round(traces, rounds[0])
            (total,) = last(total=total, label="other_product", lists=[others])
            sums, total = tie((sums, total))
            sums = sum_round(sums, rounds[1])
            current = finish(spots, total, current)
    for perms in rounds[2:]:
        sums, current = tie((sums, current))
        sums = sum_round(sums, perms)
    sums = sums * (1.0 / (count_x * count_y * row_count * block))
    occupation = jnp.stack([sums[0], sums[1], sums[1], sums[2]])
    return (current.reshape(density.shape), occupation)


def solution(mesh):
    in_specs = (
        P("gx", "gy", None, None, None),
        P("gx", "gy", None),
        P("gx", "gy", None, None),
        P("gx", "gy", None),
    )
    out_specs = (P("gx", "gy", None, None, None), P())
    return jax.shard_map(shards, mesh=mesh, in_specs=in_specs, out_specs=out_specs, check_vma=False)
```

```python
import functools

import jax
import jax.numpy as jnp
import numpy as np
from jax import lax
from jax.experimental import pallas as pl
from jax.experimental.pallas import tpu as pltpu
from jax.sharding import PartitionSpec as P

STEPS = 2
AXES = ("gx", "gy")
LANES = 128
TILE = 256

step_x = np.array([0, 0, -1, 1, -1, 1, -1, 1])
step_y = np.array([-1, 1, -1, 1, 1, -1, 0, 0])

FRAME = {
    "C": (0, 1),
    "A": (1, 0),
    "Y": (0, -1),
    "CA": (1, 1),
    "B": (-1, 0),
    "YA": (1, -1),
    "CB": (-1, 1),
    "YB": (-1, -1),
}


OWN_TILES = 2
TILES = (
    (("C", 0, 4),),
    (("A", 2, 2), ("Y", 0, 2)),
    (("A", 0, 2), ("Y", 2, 2)),
    (("B", 2, 2), ("YA", 2, 2)),
    (("B", 0, 2), ("YA", 0, 2)),
    (("CA", 0, 4),),
    (("CB", 0, 4),),
    (("YB", 0, 4),),
)


def pool_places(rows):
    places = {}
    for t, members in enumerate(TILES):
        at = rows + 4 * t
        for name, begin, count in members:
            places.setdefault(name, [0, 0])
            if begin == 0:
                places[name][0] = at
            if begin + count == 4:
                places[name][1] = at + count - 2
            at += count
    return places


def reach(t):
    def frames(n):
        return [(0, 0)] if n < OWN_TILES else [FRAME[m[0]] for m in TILES[n - OWN_TILES]]

    near = lambda p, q: abs(p[0] - q[0]) <= 1 and abs(p[1] - q[1]) <= 1
    count = OWN_TILES + len(TILES)
    found = [n for n in range(count) if any(near(p, q) for p in frames(t) for q in frames(n))]
    if len(found) % 2:
        found.append(next(n for n in range(count) if n not in found))
    return found


def flat_perm(count_x, count_y, move):
    pairs = []
    for i in range(count_x):
        for j in range(count_y):
            x, y = move(i, j)
            pairs.append((i * count_y + j, (x % count_x) * count_y + y % count_y))
    return pairs


def toward_a(i, j):
    return i ^ 1, j


def along_b(i, j):
    return (i + 2 if i % 2 == 0 else i - 2), j


def toward_c(i, j):
    return i, j ^ 1


def toward_y(i, j):
    return i, (j - 1 if j % 2 == 0 else j + 1)


def split(value):
    high = value.astype(jnp.bfloat16)
    low = (value - high.astype(jnp.float32)).astype(jnp.bfloat16)
    return high, low


def trace_of(block):
    row = lax.broadcasted_iota(jnp.int32, block.shape, 0)
    lane = lax.broadcasted_iota(jnp.int32, block.shape, 1)
    return jnp.sum(jnp.where(row == lane, block, 0.0))


def quotient(value, by, most):
    total = jnp.zeros_like(value)
    for k in range(1, most + 1):
        total += (value >= by * k).astype(jnp.int32)
    return total


VMEM = pl.BlockSpec(memory_space=pltpu.VMEM)
SMEM = pl.BlockSpec(memory_space=pltpu.SMEM)


def pack(moves, rims, cols, rows, count_x, count_y):
    row_count, block, strip = rows.shape
    slots = cols.shape[1]
    rim_count = rims.shape[0]
    tiles = strip // LANES
    ways = len(step_x)

    def kernel(moves_in, rims_in, cols_in, rows_in, *refs):
        outs, refs = refs[:ways], refs[ways:]
        small_ref, cols_ref, moves_ref, rims_ref, rows_ref, codes_ref, tail_ref, sems = refs
        copies = [
            pltpu.make_async_copy(source, target, sems.at[k])
            for k, (source, target) in enumerate(
                (
                    (moves_in, moves_ref),
                    (rims_in, rims_ref),
                    (cols_in, cols_ref),
                    (rows_in, rows_ref),
                )
            )
        ]
        for copy in copies:
            copy.start()
        index_x = lax.axis_index("gx")
        index_y = lax.axis_index("gy")
        for copy in copies[:3]:
            copy.wait()
        cols = cols_ref[...]
        inner = jnp.full(cols.shape, -1, jnp.int32)
        for m in range(rim_count):
            small_ref[ways + m] = rims_ref[m]
            inner = jnp.where(cols == rims_ref[m], 4 * rim_count + m, inner)
        away = cols - row_count
        direction = quotient(away, rim_count, ways - 1)
        place = direction + (direction >= 4).astype(jnp.int32)
        code = jnp.where(
            cols < row_count, inner, place * rim_count + away - direction * rim_count
        )
        codes_ref[...] = jnp.zeros(codes_ref.shape, jnp.float32)
        tail_ref[...] = jnp.zeros(tail_ref.shape, jnp.float32)
        codes_ref[:, :slots] = code.astype(jnp.float32)
        for m in range(rim_count):
            tail_ref[pl.ds(m, 1), :] = codes_ref[pl.ds(rims_ref[m], 1), :]
        leaving = []
        for d in range(ways):
            x = lax.rem(index_x + int(step_x[d]) + count_x, count_x)
            y = lax.rem(index_y + int(step_y[d]) + count_y, count_y)
            first = (x * count_y + y) * row_count
            slot = jnp.int32(0)
            for r in range(1, row_count):
                target = moves_ref[r]
                slot = jnp.where((target >= first) & (target < first + row_count), r, slot)
            small_ref[d] = slot
            leaving.append(slot)
        copies[3].wait()
        for d in range(ways):
            for k in range(tiles):
                outs[d][k * block : (k + 1) * block, :] = rows_ref[
                    leaving[d], :, k * LANES : (k + 1) * LANES
                ]
            outs[d][tiles * block :, :] = tail_ref[...]

    message = jax.ShapeDtypeStruct((tiles * block + 8, LANES), jnp.float32)
    return pl.pallas_call(
        kernel,
        out_shape=(message,) * ways
        + (
            jax.ShapeDtypeStruct((ways + rim_count,), jnp.int32),
            jax.ShapeDtypeStruct(cols.shape, jnp.int32),
        ),
        in_specs=[pl.BlockSpec(memory_space=pltpu.HBM)] * 4,
        out_specs=(VMEM,) * ways + (SMEM, VMEM),
        scratch_shapes=[
            pltpu.SMEM((row_count,), jnp.int32),
            pltpu.SMEM((rim_count,), jnp.int32),
            pltpu.VMEM(rows.shape, jnp.float32),
            pltpu.VMEM((row_count, LANES), jnp.float32),
            pltpu.VMEM((8, LANES), jnp.float32),
            pltpu.SemaphoreType.DMA((4,)),
        ],
        compiler_params=pltpu.CompilerParams(vmem_limit_bytes=16 * 2**20),
        name="pack_rows",
    )(moves, rims, cols, rows)


def share(rows_ref, small_ref, rim_refs):
    rim_ref, a_1, y_0, a_0, y_1 = rim_refs
    count = rim_ref.shape[0]
    for m in range(count):
        row = rows_ref[small_ref[len(step_x) + m]]
        rim_ref[m] = row
        for ref in (a_0, y_0) if m < count // 2 else (a_1, y_1):
            ref[m % (count // 2)] = row


def place(small, arrived, strip):
    rows = len(arrived)
    tiles = strip // LANES
    block = (arrived[0].shape[0] - 8) // tiles
    count = small.shape[0] - rows
    half = count // 2

    def kernel(small_ref, *refs):
        ins, outs = refs[:rows], refs[rows:]
        current_ref, *rim_refs, trace_ref = outs
        total = jnp.float32(0.0)
        for d in range(rows):
            for k in range(tiles):
                current_ref[small_ref[d], :, k * LANES : (k + 1) * LANES] = ins[d][
                    k * block : (k + 1) * block, :
                ]
            total += trace_of(ins[d][:block, :])
        trace_ref[0] = total
        share(current_ref, small_ref, rim_refs)

    rim = lambda n: jax.ShapeDtypeStruct((n, block, strip), jnp.float32)
    return pl.pallas_call(
        kernel,
        out_shape=(rim(rows), rim(count), rim(half), rim(half), rim(half), rim(half))
        + (jax.ShapeDtypeStruct((1,), jnp.float32),),
        in_specs=[SMEM] + [VMEM] * rows,
        out_specs=(VMEM,) * 6 + (SMEM,),
        compiler_params=pltpu.CompilerParams(vmem_limit_bytes=16 * 2**20),
        name="place_rows",
    )(small, *arrived)


def tables(small, cols, arrived):
    rows, slots = cols.shape
    rim_count = small.shape[0] - len(arrived)
    half = rim_count // 2
    pool = rows + len(TILES) * rim_count
    tail = arrived[0].shape[0] // 8 - 1
    base_of = [[0, 0]] * 9
    for name, (one, two) in pool_places(rows).items():
        x, y = FRAME[name]
        base_of[3 * (x + 1) + y + 1] = [one, two - half]

    def kernel(small_ref, cols_ref, *refs):
        tails, (spots_ref, table_ref, all_ref) = refs[: len(arrived)], refs[len(arrived) :]
        sign_x = 1 - 2 * lax.rem(lax.axis_index("gx"), 2)
        sign_y = 1 - 2 * lax.rem(lax.axis_index("gy"), 2)

        def locate(place, index, shift_x, shift_y):
            third = quotient(place, 3, 2)
            x = (third - 1) * sign_x + shift_x
            y = (place - 3 * third - 1) * sign_y + shift_y
            inside = (x >= -1) & (x <= 1) & (y >= -1) & (y <= 1)
            at = 3 * (x + 1) + y + 1
            one = two = jnp.zeros_like(index)
            for k in range(9):
                one = jnp.where(at == k, base_of[k][0], one)
                two = jnp.where(at == k, base_of[k][1], two)
            spot = index + jnp.where(index < half, one, two)
            for m in range(rim_count):
                spot = jnp.where((at == 4) & (index == m), small_ref[len(arrived) + m], spot)
            return jnp.where(inside, spot, -1)

        cols = cols_ref[...]
        away = cols - rows
        direction = quotient(away, rim_count, 7)
        place = direction + (direction >= 4).astype(jnp.int32)
        spots = locate(place, away - direction * rim_count, 0, 0)
        spots = jnp.where(cols < rows, cols, spots)
        spots_ref[...] = spots
        all_ref[...] = jnp.full(all_ref.shape, -1, jnp.int32)
        all_ref[:rows, :slots] = spots
        for d in range(len(arrived)):
            x = -int(step_x[d]) * sign_x
            y = -int(step_y[d]) * sign_y
            at = 3 * (x + 1) + y + 1
            bases = []
            for part in range(2):
                base = jnp.int32(0)
                for k in range(9):
                    base = jnp.where(at == k, base_of[k][part], base)
                bases.append(base)
            near = tails[d][...].astype(jnp.int32)
            place = quotient(near, rim_count, 8)
            spots = locate(place, near - place * rim_count, x, y)
            spots = jnp.where(near < 0, -1, spots)
            for m in range(rim_count):
                all_ref[pl.ds(bases[m // half] + m, 1), :] = spots[m : m + 1, :]
        lane = lax.broadcasted_iota(jnp.int32, (pool, LANES), 1)
        found = jnp.full((pool, LANES), -1, jnp.int32)
        for u in range(slots):
            found = jnp.where(all_ref[:, u : u + 1] == lane, u, found)
        entry = (found >> 1) + 16 * ((found ^ lane) & 1)
        table_ref[...] = jnp.where(found < 0, slots // 2, entry)

    last = pl.BlockSpec((8, LANES), lambda n: (tail, 0))
    full = lambda shape: pl.BlockSpec(shape, lambda n: (0, 0))
    return pl.pallas_call(
        kernel,
        grid=(1,),
        out_shape=(
            jax.ShapeDtypeStruct((rows, slots), jnp.int32),
            jax.ShapeDtypeStruct((pool, LANES), jnp.int32),
        ),
        in_specs=[SMEM, full((rows, slots))] + [last] * len(arrived),
        out_specs=(full((rows, slots)), full((pool, LANES))),
        scratch_shapes=[pltpu.VMEM((pool, LANES), jnp.int32)],
        compiler_params=pltpu.CompilerParams(vmem_limit_bytes=4 * 2**20),
        name="make_tables",
    )(small, cols, *arrived)


def spread(parts, high_ref, low_ref):
    base = 0
    strip = parts[0].shape[2]
    for ref in parts:

        def one(c, carry, ref=ref, base=base):
            at = pl.ds(pl.multiple_of((base + c) * 64, 64), 64)
            for k in range(strip // LANES):
                to = pl.ds(k * LANES, LANES)
                value = ref[c, :, to]
                for turn in range(2):
                    high, low = split(pltpu.roll(value, 64, 1) if turn else value)
                    high_ref[turn, at, to] = high
                    low_ref[turn, at, to] = low
            zeros = jnp.zeros((64, LANES), jnp.bfloat16)
            high_ref[0, at, pl.ds(strip, LANES)] = zeros
            low_ref[0, at, pl.ds(strip, LANES)] = zeros
            return carry

        lax.fori_loop(0, ref.shape[0], one, 0)
        base += ref.shape[0]


def fill_pair(table_ref, position, spot, source, member, targets):
    left_half = lax.broadcasted_iota(jnp.int32, (64, LANES), 1) < 64
    at = pl.ds(pl.multiple_of(member * 64, 64), 64)
    left = table_ref[position, spot]
    right = table_ref[position, spot + 1]
    from_left = pl.ds(pl.multiple_of((left & 15) * LANES, LANES), LANES)
    from_right = pl.ds(pl.multiple_of((right & 15) * LANES, LANES), LANES)
    for k in range(2):
        value = jnp.where(
            left_half, source[k][left >> 4, at, from_left], source[k][right >> 4, at, from_right]
        )
        for refs, row, first in targets:
            refs[k][pl.ds(row, 64), pl.ds(pl.multiple_of(first, LANES), LANES)] = value


def fill(table_ref, first, member, members, tile, source, targets):
    for c in range(members):
        for q in range(TILE // LANES):
            fill_pair(
                table_ref, first + member + c, tile * (TILE // 64) + 2 * q, source, member + c,
                [(refs, c * 64, to + q * LANES) for refs, to in targets],
            )


def three_products(a_high, a_low, d_high, d_low):
    left = jnp.concatenate([a_high, a_high, a_low], axis=1)
    right = jnp.concatenate([d_high, d_low, d_high], axis=0)
    return jnp.dot(left, right, preferred_element_type=jnp.float32)


def wide_scratch(members, strip):
    return [pltpu.VMEM((2, members * 64, strip + LANES), jnp.bfloat16)] * 2


def pipelined(units, fill_one, multiply, buffers):
    even, odd = buffers
    fill_one(jnp.int32(0), even)

    def two(j, carry):
        fill_one(2 * j + 1, odd)
        multiply(2 * j, even)
        fill_one(jnp.minimum(2 * j + 2, units - 1), even)
        multiply(2 * j + 1, odd)
        return carry

    lax.fori_loop(0, units // 2, two, 0)
    if units % 2:
        multiply(units - 1, even)


def lane(tile):
    return pl.multiple_of(tile * TILE, TILE)


def cost(units):
    return pl.CostEstimate(flops=units * 2**27, bytes_accessed=2**16, transcendentals=0)


def spread_own(current):
    rows, block, strip = current.shape

    def kernel(current_ref, high_ref, low_ref):
        spread([current_ref], high_ref, low_ref)

    wide = jax.ShapeDtypeStruct((2, rows * block, strip + LANES), jnp.bfloat16)
    return pl.pallas_call(
        kernel,
        out_shape=(wide, wide),
        in_specs=[VMEM],
        out_specs=(VMEM, VMEM),
        compiler_params=pltpu.CompilerParams(vmem_limit_bytes=16 * 2**20),
        cost_estimate=cost(1),
        name="spread_own",
    )(current)


def own_product(table, wide, rows, block):
    width = table.shape[0] * block
    depth = rows * block
    tiles = width // TILE

    def kernel(table_ref, wide_high, wide_low, high_ref, low_ref, total_ref, *scratch):
        wide = wide_high, wide_low
        own, even, odd = scratch[0:2], scratch[2:4], scratch[4:6]
        for n in range(depth // TILE):
            fill(table_ref, 0, 0, rows, n, wide, [(own, n * TILE)])

        def fill_one(i, buffers):
            for k in range(2):
                fill(
                    table_ref, 0, 0, rows, 2 * i + k, wide,
                    [(buffers, k * TILE), ((high_ref, low_ref), (2 * i + k) * TILE)],
                )

        def multiply(i, buffers):
            to = pl.ds(pl.multiple_of(2 * i * TILE, 2 * TILE), 2 * TILE)
            total_ref[:, to] = three_products(
                own[0][...], own[1][...], buffers[0][...], buffers[1][...]
            )

        pipelined(tiles // 2, fill_one, multiply, (even, odd))

    dense = lambda t: jax.ShapeDtypeStruct((depth, width), t)
    return pl.pallas_call(
        kernel,
        out_shape=(dense(jnp.bfloat16), dense(jnp.bfloat16), dense(jnp.float32)),
        in_specs=[SMEM, VMEM, VMEM],
        out_specs=(VMEM, VMEM, VMEM),
        scratch_shapes=[pltpu.VMEM((depth, depth), jnp.bfloat16)] * 2
        + [pltpu.VMEM((depth, 2 * TILE), jnp.bfloat16)] * 4,
        compiler_params=pltpu.CompilerParams(vmem_limit_bytes=24 * 2**20),
        cost_estimate=cost(2 * tiles),
        name="own_product",
    )(table, *wide)


def extract(spots_ref, total_ref, current_ref, out_ref, blend):
    left_half = lax.broadcasted_iota(jnp.int32, (64, LANES), 1) < 64

    def one_row(g, carry):
        at = pl.ds(pl.multiple_of(g * 64, 64), 64)
        for k in range(out_ref.shape[2] // LANES):
            sides = []
            for side in range(2):
                spot = spots_ref[g, 2 * k + side]
                tile = pl.ds(pl.multiple_of((spot >> 1) * LANES, LANES), LANES)
                sides.append(pltpu.roll(total_ref[at, tile], ((spot ^ side) & 1) * 64, 1))
            value = jnp.where(left_half, *sides)
            to = pl.ds(k * LANES, LANES)
            if blend:
                value = 2.0 * current_ref[g, :, to] - value
            out_ref[g, :, to] = value
        return carry

    lax.fori_loop(0, out_ref.shape[0], one_row, 0)


def add_traces(traces_ref, extra_ref, total_ref, trace_ref):
    known = traces_ref.shape[0]
    for k in range(known):
        trace_ref[k] = traces_ref[k]
    row = lax.broadcasted_iota(jnp.int32, (64, LANES), 0)
    spot = lax.broadcasted_iota(jnp.int32, (64, LANES), 1)
    found = jnp.zeros((64, LANES), jnp.float32)
    for g in range(total_ref.shape[0] // 64):
        block = total_ref[g * 64 : (g + 1) * 64, (g // 2) * LANES : (g // 2 + 1) * LANES]
        found += jnp.where(spot - row == 64 * (g % 2), block, 0.0)
    trace_ref[known] = jnp.sum(found) + (0.0 if extra_ref is None else extra_ref[0])


def far_trace(table, c, y_0, y_1, b_0, b_1):
    parts = [c, y_0, y_1, b_0, b_1]
    _, block, strip = c.shape
    places = pool_places(8)
    members = {"C": 0, "Y": 4, "B": 8}

    def kernel(table_ref, *refs):
        part_refs, trace_ref, wide, one, two = refs[:5], refs[5], refs[6:8], refs[8:10], refs[10:12]
        spread(part_refs, *wide)
        for k, name in enumerate("CY"):
            for m in range(4):
                for q in range(2):
                    fill_pair(
                        table_ref, places["B"][m // 2] + m % 2, places[name][q], wide,
                        members["B"] + m, [(one, m * 64, k * TILE + q * LANES)],
                    )
                    fill_pair(
                        table_ref, places[name][m // 2] + m % 2, places["B"][q], wide,
                        members[name] + m, [(two, k * TILE + m * 64, q * LANES)],
                    )
        product = three_products(one[0][...], one[1][...], two[0][...], two[1][...])
        row = lax.broadcasted_iota(jnp.int32, product.shape, 0)
        spot = lax.broadcasted_iota(jnp.int32, product.shape, 1)
        trace_ref[0] = jnp.sum(jnp.where(row == spot, product, 0.0))

    return pl.pallas_call(
        kernel,
        out_shape=jax.ShapeDtypeStruct((1,), jnp.float32),
        in_specs=[SMEM] + [VMEM] * 5,
        out_specs=SMEM,
        scratch_shapes=wide_scratch(12, strip)
        + [pltpu.VMEM((TILE, 2 * TILE), jnp.bfloat16)] * 2
        + [pltpu.VMEM((2 * TILE, TILE), jnp.bfloat16)] * 2,
        compiler_params=pltpu.CompilerParams(vmem_limit_bytes=24 * 2**20),
        cost_estimate=cost(4),
        name="far_trace",
    )(table, *parts)


def add_product(begin, count, table, high, low, parts, total, label, traces=None, extra=None, square=None):
    depth_own, width = total.shape
    _, block, strip = parts[0].shape
    rows = depth_own // block
    each = TILE // block
    first = begin * each
    lists = [reach(begin + k) for k in range(count)]
    blend = square is not None and len(square) == 3
    starts = [sum(len(t) for t in lists[:k]) // 2 for k in range(count + 1)]
    codes = [
        [sum(t << (4 * k) for k, t in enumerate(tiles[side::2])) for side in range(2)]
        for tiles in lists
    ]

    def unit(i):
        group, start = jnp.int32(0), jnp.int32(0)
        code = [jnp.int32(c) for c in codes[0]]
        for k in range(1, count):
            after = i >= starts[k]
            group = jnp.where(after, k, group)
            start = jnp.where(after, starts[k], start)
            code = [jnp.where(after, new, old) for new, old in zip(codes[k], code)]
        return group, [(c >> (4 * (i - start))) & 15 for c in code]

    def kernel(table_ref, high_ref, low_ref, *refs):
        refs = list(refs)
        part_refs = [refs.pop(0) for _ in parts]
        refs.pop(0)
        if traces is not None:
            traces_ref = refs.pop(0)
        extra_ref = refs.pop(0) if extra is not None else None
        if square is not None:
            spots_ref, small_ref = refs.pop(0), refs.pop(0)
        current_ref = refs.pop(0) if blend else None
        total_ref = refs.pop(0)
        if traces is not None:
            trace_ref = refs.pop(0)
        if square is not None:
            out_ref, *rim_refs = (refs.pop(0) for _ in range(1 if blend else 6))
        wide, even, odd = refs[0:2], refs[2:4], refs[4:6]
        spread(part_refs, *wide)

        def fill_one(i, buffers):
            group, tiles = unit(i)
            for k in range(2):
                fill(table_ref, first, group * each, each, tiles[k], wide, [(buffers, k * TILE)])

        def multiply(i, buffers):
            group, tiles = unit(i)
            at = pl.ds(lane(begin + group), TILE)
            value = three_products(
                high_ref[:, at], low_ref[:, at], buffers[0][...], buffers[1][...]
            )
            for k in range(2):
                to = pl.ds(lane(tiles[k]), TILE)
                total_ref[:, to] += value[:, k * TILE : (k + 1) * TILE]

        pipelined(starts[-1], fill_one, multiply, (even, odd))
        if traces is not None:
            add_traces(traces_ref, extra_ref, total_ref, trace_ref)
        if square is not None:
            extract(spots_ref, total_ref, current_ref, out_ref, blend)
            if not blend:
                share(out_ref, small_ref, rim_refs)

    ins = [table, high, low, *parts, total]
    in_specs = [SMEM] + [VMEM] * (3 + len(parts))
    out_shape = [jax.ShapeDtypeStruct((depth_own, width), jnp.float32)]
    out_specs = [VMEM]
    if traces is not None:
        ins.append(traces)
        in_specs.append(SMEM)
        out_shape.append(jax.ShapeDtypeStruct((traces.shape[0] + 1,), jnp.float32))
        out_specs.append(SMEM)
    if extra is not None:
        ins.append(extra)
        in_specs.append(SMEM)
    if square is not None:
        ins += square
        in_specs += [SMEM, SMEM] + [VMEM] * blend
        shape = lambda n: jax.ShapeDtypeStruct((n, block, strip), jnp.float32)
        out_shape.append(shape(rows))
        if not blend:
            out_shape += [shape(each)] + [shape(each // 2)] * 4
        out_specs += [VMEM] * (len(out_shape) - len(out_specs))
    scratch = wide_scratch(count * each, strip)
    scratch += [pltpu.VMEM((TILE, 2 * TILE), jnp.bfloat16)] * 4
    return pl.pallas_call(
        kernel,
        out_shape=out_shape,
        in_specs=in_specs,
        out_specs=out_specs,
        scratch_shapes=scratch,
        input_output_aliases={3 + len(parts): 0},
        compiler_params=pltpu.CompilerParams(vmem_limit_bytes=24 * 2**20),
        cost_estimate=cost(2 * starts[-1]),
        name=label,
    )(*ins)


def sum_rounds(count_x, count_y):
    rounds = []
    for count, at in ((count_y, 1), (count_x, 0)):
        bit = 1
        while bit < count:
            bits = [bit, 2 * bit, 3 * bit] if 2 * bit < count else [bit]
            rounds.append(
                [
                    flat_perm(count_x, count_y, lambda i, j: (i, j ^ b) if at else (i ^ b, j))
                    for b in bits
                ]
            )
            bit *= 4
    return rounds


def sum_round(value, perms):
    others = [lax.ppermute(value, AXES, perm) for perm in perms]
    if len(others) == 1:
        return value + others[0]
    return (value + others[0]) + (others[1] + others[2])


def shards(density, moves, cols, halo_rows):
    row_count, block, strip = density.shape[2:]
    rim_count = halo_rows.shape[2]
    count_x = lax.axis_size("gx")
    count_y = lax.axis_size("gy")
    rows = density.reshape(row_count, block, strip)
    rims = halo_rows.reshape(rim_count)
    own_cols = cols.reshape(row_count, -1)

    *leaving, small, own_cols = pack(
        moves.reshape(row_count), rims, own_cols, rows, count_x, count_y
    )
    arrived = [None] * len(step_x)
    for d in range(len(step_x)):
        dx, dy = int(step_x[d]), int(step_y[d])
        perm = flat_perm(count_x, count_y, lambda i, j: (i + dx, j + dy))
        arrived[d] = lax.ppermute(leaving[d], AXES, perm)

    current, *shared, traces = place(small, arrived, strip)
    spots, table = tables(small, own_cols, arrived)
    swap = {
        "A": flat_perm(count_x, count_y, toward_a),
        "B": flat_perm(count_x, count_y, along_b),
        "C": flat_perm(count_x, count_y, toward_c),
        "Y": flat_perm(count_x, count_y, toward_y),
    }
    go = lambda value, way: lax.ppermute(value, AXES, swap[way])
    rounds = sum_rounds(count_x, count_y)
    tie = lax.optimization_barrier
    for step in range(STEPS):
        c, a_1, y_0 = (go(rim, way) for rim, way in zip(shared[:3], "CAY"))
        wide_high, wide_low = spread_own(current)
        wide_high, *shared = tie((wide_high, *shared[3:]))
        a_0, y_1 = (go(rim, way) for rim, way in zip(shared, "AY"))
        high, low, total = own_product(table, (wide_high, wide_low), row_count, block)
        add = functools.partial(add_product, table=table, high=high, low=low)
        a_1, y_0, c, total = tie((a_1, y_0, c, total))
        b_1, ya_1, ya_0 = go(a_1, "B"), go(a_1, "Y"), go(y_0, "A")
        (total,) = add(2, 2, parts=[c, a_1, y_0], total=total, label="first_product")
        a_0, y_1, total = tie((a_0, y_1, total))
        b_0 = go(a_0, "B")
        (total,) = add(4, 1, parts=[a_0, y_1], total=total, label="second_product")
        a_0, b_1, ya_0, total = tie((a_0, b_1, ya_0, total))
        yb_1, yb_0 = go(b_1, "Y"), go(ya_0, "B")
        ca = go(jnp.concatenate([a_0, a_1]), "C")
        (total,) = add(5, 1, parts=[b_1, ya_1], total=total, label="third_product")
        b_0, total = tie((b_0, total))
        cb = go(jnp.concatenate([b_0, b_1]), "C")
        last = functools.partial(add, 9, 1, parts=[yb_0, yb_1], label="last_product")
        fourth = functools.partial(add, 6, 2, parts=[b_0, ya_0, ca], label="fourth_product")
        fifth = functools.partial(add, 8, 1, parts=[cb], label="fifth_product")
        if step % 2 == 0:
            (total,) = fourth(total=total)
            (total,) = fifth(total=total)
            total, traces, current, *shared = last(
                total=total, traces=traces, square=(spots, small)
            )
        else:
            extra = far_trace(table, c, y_0, y_1, b_0, b_1)
            total, sums = fourth(total=total, traces=traces, extra=extra)
            sums = sum_round(sums, rounds[0])
            (total,) = fifth(total=total)
            sums, total = tie((sums, total))
            for perms in rounds[1:-1]:
                sums = sum_round(sums, perms)
            sums, total = tie((sums, total))
            sums = sum_round(sums, rounds[-1])
            _, current = last(total=total, square=(spots, small, current))
    sums = sums * (1.0 / (count_x * count_y * row_count * block))
    occupation = jnp.stack([sums[0], sums[1], sums[1], sums[2]])
    return (current.reshape(density.shape), occupation)


def solution(mesh):
    in_specs = (
        P("gx", "gy", None, None, None),
        P("gx", "gy", None),
        P("gx", "gy", None, None),
        P("gx", "gy", None),
    )
    out_specs = (P("gx", "gy", None, None, None), P())
    return jax.shard_map(shards, mesh=mesh, in_specs=in_specs, out_specs=out_specs, check_vma=False)
```

```python
import functools

import jax
import jax.numpy as jnp
import numpy as np
from jax import lax
from jax.experimental import pallas as pl
from jax.experimental.pallas import tpu as pltpu
from jax.sharding import PartitionSpec as P

STEPS = 2
AXES = ("gx", "gy")
LANES = 128
TILE = 256
STEP_FLOPS = 6000 * 10**6

step_x = np.array([0, 0, -1, 1, -1, 1, -1, 1])
step_y = np.array([-1, 1, -1, 1, 1, -1, 0, 0])

FRAME = {
    "C": (0, 1),
    "A": (1, 0),
    "Y": (0, -1),
    "CA": (1, 1),
    "B": (-1, 0),
    "YA": (1, -1),
    "CB": (-1, 1),
    "YB": (-1, -1),
}


OWN_TILES = 2
TILES = (
    (("C", 0, 4),),
    (("A", 2, 2), ("Y", 0, 2)),
    (("A", 0, 2), ("Y", 2, 2)),
    (("B", 2, 2), ("YA", 2, 2)),
    (("B", 0, 2), ("YA", 0, 2)),
    (("CA", 0, 4),),
    (("YB", 0, 4),),
    (("CB", 0, 4),),
)


def pool_places(rows):
    places = {}
    for t, members in enumerate(TILES):
        at = rows + 4 * t
        for name, begin, count in members:
            places.setdefault(name, [0, 0])
            if begin == 0:
                places[name][0] = at
            if begin + count == 4:
                places[name][1] = at + count - 2
            at += count
    return places


def reach(t):
    def frames(n):
        return [(0, 0)] if n < OWN_TILES else [FRAME[m[0]] for m in TILES[n - OWN_TILES]]

    near = lambda p, q: abs(p[0] - q[0]) <= 1 and abs(p[1] - q[1]) <= 1
    count = OWN_TILES + len(TILES)
    found = [n for n in range(count) if any(near(p, q) for p in frames(t) for q in frames(n))]
    if len(found) % 2:
        found.append(next(n for n in range(count) if n not in found))
    return found


def flat_perm(count_x, count_y, move):
    pairs = []
    for i in range(count_x):
        for j in range(count_y):
            x, y = move(i, j)
            pairs.append((i * count_y + j, (x % count_x) * count_y + y % count_y))
    return pairs


def toward_a(i, j):
    return i ^ 1, j


def along_b(i, j):
    return (i + 2 if i % 2 == 0 else i - 2), j


def toward_c(i, j):
    return i, j ^ 1


def toward_y(i, j):
    return i, (j - 1 if j % 2 == 0 else j + 1)


def split(value):
    high = value.astype(jnp.bfloat16)
    low = (value - high.astype(jnp.float32)).astype(jnp.bfloat16)
    return high, low


def trace_of(block):
    row = lax.broadcasted_iota(jnp.int32, block.shape, 0)
    lane = lax.broadcasted_iota(jnp.int32, block.shape, 1)
    return jnp.sum(jnp.where(row == lane, block, 0.0))


def quotient(value, by, most):
    total = jnp.zeros_like(value)
    for k in range(1, most + 1):
        total += (value >= by * k).astype(jnp.int32)
    return total


VMEM = pl.BlockSpec(memory_space=pltpu.VMEM)
SMEM = pl.BlockSpec(memory_space=pltpu.SMEM)


def pack(moves, rims, cols, rows, count_x, count_y):
    row_count, block, strip = rows.shape
    slots = cols.shape[1]
    rim_count = rims.shape[0]
    tiles = strip // LANES
    ways = len(step_x)

    def kernel(moves_in, rims_in, cols_in, rows_in, *refs):
        outs, refs = refs[:ways], refs[ways:]
        small_ref, cols_ref, moves_ref, rims_ref, rows_ref, codes_ref, tail_ref, sems = refs
        copies = [
            pltpu.make_async_copy(source, target, sems.at[k])
            for k, (source, target) in enumerate(
                (
                    (moves_in, moves_ref),
                    (rims_in, rims_ref),
                    (cols_in, cols_ref),
                    (rows_in, rows_ref),
                )
            )
        ]
        for copy in copies:
            copy.start()
        index_x = lax.axis_index("gx")
        index_y = lax.axis_index("gy")
        for copy in copies[:3]:
            copy.wait()
        cols = cols_ref[...]
        inner = jnp.full(cols.shape, -1, jnp.int32)
        for m in range(rim_count):
            small_ref[ways + m] = rims_ref[m]
            inner = jnp.where(cols == rims_ref[m], 4 * rim_count + m, inner)
        away = cols - row_count
        direction = quotient(away, rim_count, ways - 1)
        place = direction + (direction >= 4).astype(jnp.int32)
        code = jnp.where(
            cols < row_count, inner, place * rim_count + away - direction * rim_count
        )
        codes_ref[...] = jnp.zeros(codes_ref.shape, jnp.float32)
        tail_ref[...] = jnp.zeros(tail_ref.shape, jnp.float32)
        codes_ref[:, :slots] = code.astype(jnp.float32)
        for m in range(rim_count):
            tail_ref[pl.ds(m, 1), :] = codes_ref[pl.ds(rims_ref[m], 1), :]
        leaving = []
        for d in range(ways):
            x = lax.rem(index_x + int(step_x[d]) + count_x, count_x)
            y = lax.rem(index_y + int(step_y[d]) + count_y, count_y)
            first = (x * count_y + y) * row_count
            slot = jnp.int32(0)
            for r in range(1, row_count):
                target = moves_ref[r]
                slot = jnp.where((target >= first) & (target < first + row_count), r, slot)
            small_ref[d] = slot
            leaving.append(slot)
        copies[3].wait()
        for d in range(ways):
            for k in range(tiles):
                outs[d][k * block : (k + 1) * block, :] = rows_ref[
                    leaving[d], :, k * LANES : (k + 1) * LANES
                ]
            outs[d][tiles * block :, :] = tail_ref[...]

    message = jax.ShapeDtypeStruct((tiles * block + 8, LANES), jnp.float32)
    return pl.pallas_call(
        kernel,
        out_shape=(message,) * ways
        + (
            jax.ShapeDtypeStruct((ways + rim_count,), jnp.int32),
            jax.ShapeDtypeStruct(cols.shape, jnp.int32),
        ),
        in_specs=[pl.BlockSpec(memory_space=pltpu.HBM)] * 4,
        out_specs=(VMEM,) * ways + (SMEM, VMEM),
        scratch_shapes=[
            pltpu.SMEM((row_count,), jnp.int32),
            pltpu.SMEM((rim_count,), jnp.int32),
            pltpu.VMEM(rows.shape, jnp.float32),
            pltpu.VMEM((row_count, LANES), jnp.float32),
            pltpu.VMEM((8, LANES), jnp.float32),
            pltpu.SemaphoreType.DMA((4,)),
        ],
        compiler_params=pltpu.CompilerParams(vmem_limit_bytes=16 * 2**20),
        name="pack_rows",
    )(moves, rims, cols, rows)


def share(rows_ref, small_ref, rim_refs):
    rim_ref, a_1, y_0, a_0, y_1 = rim_refs
    count = rim_ref.shape[0]
    for m in range(count):
        row = rows_ref[small_ref[len(step_x) + m]]
        rim_ref[m] = row
        for ref in (a_0, y_0) if m < count // 2 else (a_1, y_1):
            ref[m % (count // 2)] = row


def place(small, arrived, strip):
    rows = len(arrived)
    tiles = strip // LANES
    block = (arrived[0].shape[0] - 8) // tiles
    count = small.shape[0] - rows
    half = count // 2

    def kernel(small_ref, *refs):
        ins, outs = refs[:rows], refs[rows:]
        current_ref, *rim_refs, trace_ref = outs
        total = jnp.float32(0.0)
        for d in range(rows):
            for k in range(tiles):
                current_ref[small_ref[d], :, k * LANES : (k + 1) * LANES] = ins[d][
                    k * block : (k + 1) * block, :
                ]
            total += trace_of(ins[d][:block, :])
        trace_ref[0] = total
        share(current_ref, small_ref, rim_refs)

    rim = lambda n: jax.ShapeDtypeStruct((n, block, strip), jnp.float32)
    return pl.pallas_call(
        kernel,
        out_shape=(rim(rows), rim(count), rim(half), rim(half), rim(half), rim(half))
        + (jax.ShapeDtypeStruct((1,), jnp.float32),),
        in_specs=[SMEM] + [VMEM] * rows,
        out_specs=(VMEM,) * 6 + (SMEM,),
        compiler_params=pltpu.CompilerParams(vmem_limit_bytes=16 * 2**20),
        name="place_rows",
    )(small, *arrived)


def tables(small, cols, arrived):
    rows, slots = cols.shape
    rim_count = small.shape[0] - len(arrived)
    half = rim_count // 2
    pool = rows + len(TILES) * rim_count
    tail = arrived[0].shape[0] // 8 - 1
    base_of = [[0, 0]] * 9
    for name, (one, two) in pool_places(rows).items():
        x, y = FRAME[name]
        base_of[3 * (x + 1) + y + 1] = [one, two - half]

    def kernel(small_ref, cols_ref, *refs):
        tails, (spots_ref, table_ref, all_ref) = refs[: len(arrived)], refs[len(arrived) :]
        sign_x = 1 - 2 * lax.rem(lax.axis_index("gx"), 2)
        sign_y = 1 - 2 * lax.rem(lax.axis_index("gy"), 2)

        def locate(place, index, shift_x, shift_y):
            third = quotient(place, 3, 2)
            x = (third - 1) * sign_x + shift_x
            y = (place - 3 * third - 1) * sign_y + shift_y
            inside = (x >= -1) & (x <= 1) & (y >= -1) & (y <= 1)
            at = 3 * (x + 1) + y + 1
            one = two = jnp.zeros_like(index)
            for k in range(9):
                one = jnp.where(at == k, base_of[k][0], one)
                two = jnp.where(at == k, base_of[k][1], two)
            spot = index + jnp.where(index < half, one, two)
            for m in range(rim_count):
                spot = jnp.where((at == 4) & (index == m), small_ref[len(arrived) + m], spot)
            return jnp.where(inside, spot, -1)

        cols = cols_ref[...]
        away = cols - rows
        direction = quotient(away, rim_count, 7)
        place = direction + (direction >= 4).astype(jnp.int32)
        spots = locate(place, away - direction * rim_count, 0, 0)
        spots = jnp.where(cols < rows, cols, spots)
        spots_ref[...] = spots
        all_ref[...] = jnp.full(all_ref.shape, -1, jnp.int32)
        all_ref[:rows, :slots] = spots
        for d in range(len(arrived)):
            x = -int(step_x[d]) * sign_x
            y = -int(step_y[d]) * sign_y
            at = 3 * (x + 1) + y + 1
            bases = []
            for part in range(2):
                base = jnp.int32(0)
                for k in range(9):
                    base = jnp.where(at == k, base_of[k][part], base)
                bases.append(base)
            near = tails[d][...].astype(jnp.int32)
            place = quotient(near, rim_count, 8)
            spots = locate(place, near - place * rim_count, x, y)
            spots = jnp.where(near < 0, -1, spots)
            for m in range(rim_count):
                all_ref[pl.ds(bases[m // half] + m, 1), :] = spots[m : m + 1, :]
        lane = lax.broadcasted_iota(jnp.int32, (pool, LANES), 1)
        found = jnp.full((pool, LANES), -1, jnp.int32)
        for u in range(slots):
            found = jnp.where(all_ref[:, u : u + 1] == lane, u, found)
        entry = (found >> 1) + 16 * ((found ^ lane) & 1)
        table_ref[...] = jnp.where(found < 0, slots // 2, entry)

    last = pl.BlockSpec((8, LANES), lambda n: (tail, 0))
    full = lambda shape: pl.BlockSpec(shape, lambda n: (0, 0))
    return pl.pallas_call(
        kernel,
        grid=(1,),
        out_shape=(
            jax.ShapeDtypeStruct((rows, slots), jnp.int32),
            jax.ShapeDtypeStruct((pool, LANES), jnp.int32),
        ),
        in_specs=[SMEM, full((rows, slots))] + [last] * len(arrived),
        out_specs=(full((rows, slots)), full((pool, LANES))),
        scratch_shapes=[pltpu.VMEM((pool, LANES), jnp.int32)],
        compiler_params=pltpu.CompilerParams(vmem_limit_bytes=4 * 2**20),
        name="make_tables",
    )(small, cols, *arrived)


def spread(parts, high_ref, low_ref):
    base = 0
    strip = parts[0].shape[2]
    for ref in parts:

        def one(c, carry, ref=ref, base=base):
            at = pl.ds(pl.multiple_of((base + c) * 64, 64), 64)
            for k in range(strip // LANES):
                to = pl.ds(k * LANES, LANES)
                value = ref[c, :, to]
                for turn in range(2):
                    high, low = split(pltpu.roll(value, 64, 1) if turn else value)
                    high_ref[turn, at, to] = high
                    low_ref[turn, at, to] = low
            zeros = jnp.zeros((64, LANES), jnp.bfloat16)
            high_ref[0, at, pl.ds(strip, LANES)] = zeros
            low_ref[0, at, pl.ds(strip, LANES)] = zeros
            return carry

        lax.fori_loop(0, ref.shape[0], one, 0)
        base += ref.shape[0]


def fill_pair(table_ref, position, spot, source, member, targets):
    left_half = lax.broadcasted_iota(jnp.int32, (64, LANES), 1) < 64
    at = pl.ds(pl.multiple_of(member * 64, 64), 64)
    left = table_ref[position, spot]
    right = table_ref[position, spot + 1]
    from_left = pl.ds(pl.multiple_of((left & 15) * LANES, LANES), LANES)
    from_right = pl.ds(pl.multiple_of((right & 15) * LANES, LANES), LANES)
    for k in range(2):
        value = jnp.where(
            left_half, source[k][left >> 4, at, from_left], source[k][right >> 4, at, from_right]
        )
        for refs, row, first in targets:
            refs[k][pl.ds(row, 64), pl.ds(pl.multiple_of(first, LANES), LANES)] = value


def fill(table_ref, first, member, members, tile, source, targets):
    for c in range(members):
        for q in range(TILE // LANES):
            fill_pair(
                table_ref, first + member + c, tile * (TILE // 64) + 2 * q, source, member + c,
                [(refs, c * 64, to + q * LANES) for refs, to in targets],
            )


def three_products(a_high, a_low, d_high, d_low):
    left = jnp.concatenate([a_high, a_high, a_low], axis=1)
    right = jnp.concatenate([d_high, d_low, d_high], axis=0)
    return jnp.dot(left, right, preferred_element_type=jnp.float32)


def wide_scratch(members, strip):
    return [pltpu.VMEM((2, members * 64, strip + LANES), jnp.bfloat16)] * 2


def pipelined(units, fill_one, multiply, buffers):
    even, odd = buffers
    fill_one(jnp.int32(0), even)

    def two(j, carry):
        fill_one(2 * j + 1, odd)
        multiply(2 * j, even)
        fill_one(jnp.minimum(2 * j + 2, units - 1), even)
        multiply(2 * j + 1, odd)
        return carry

    lax.fori_loop(0, units // 2, two, 0)
    if units % 2:
        multiply(units - 1, even)


def lane(tile):
    return pl.multiple_of(tile * TILE, TILE)


def cost(flops=STEP_FLOPS):
    return pl.CostEstimate(flops=flops, bytes_accessed=2**16, transcendentals=0)


def spread_own(current):
    rows, block, strip = current.shape

    def kernel(current_ref, high_ref, low_ref):
        spread([current_ref], high_ref, low_ref)

    wide = jax.ShapeDtypeStruct((2, rows * block, strip + LANES), jnp.bfloat16)
    return pl.pallas_call(
        kernel,
        out_shape=(wide, wide),
        in_specs=[VMEM],
        out_specs=(VMEM, VMEM),
        compiler_params=pltpu.CompilerParams(vmem_limit_bytes=16 * 2**20),
        cost_estimate=cost(2**28),
        name="spread_own",
    )(current)


def own_product(table, wide, rows, block):
    width = table.shape[0] * block
    depth = rows * block
    tiles = width // TILE

    def kernel(table_ref, wide_high, wide_low, high_ref, low_ref, total_ref, *scratch):
        wide = wide_high, wide_low
        own, even, odd = scratch[0:2], scratch[2:4], scratch[4:6]
        for n in range(depth // TILE):
            fill(table_ref, 0, 0, rows, n, wide, [(own, n * TILE)])

        def fill_one(i, buffers):
            for k in range(2):
                fill(
                    table_ref, 0, 0, rows, 2 * i + k, wide,
                    [(buffers, k * TILE), ((high_ref, low_ref), (2 * i + k) * TILE)],
                )

        def multiply(i, buffers):
            to = pl.ds(pl.multiple_of(2 * i * TILE, 2 * TILE), 2 * TILE)
            total_ref[:, to] = three_products(
                own[0][...], own[1][...], buffers[0][...], buffers[1][...]
            )

        pipelined(tiles // 2, fill_one, multiply, (even, odd))

    dense = lambda t: jax.ShapeDtypeStruct((depth, width), t)
    return pl.pallas_call(
        kernel,
        out_shape=(dense(jnp.bfloat16), dense(jnp.bfloat16), dense(jnp.float32)),
        in_specs=[SMEM, VMEM, VMEM],
        out_specs=(VMEM, VMEM, VMEM),
        scratch_shapes=[pltpu.VMEM((depth, depth), jnp.bfloat16)] * 2
        + [pltpu.VMEM((depth, 2 * TILE), jnp.bfloat16)] * 4,
        compiler_params=pltpu.CompilerParams(vmem_limit_bytes=24 * 2**20),
        cost_estimate=cost(),
        name="own_product",
    )(table, *wide)


def extract(spots_ref, total_ref, current_ref, out_ref, blend):
    left_half = lax.broadcasted_iota(jnp.int32, (64, LANES), 1) < 64

    def one_row(g, carry):
        at = pl.ds(pl.multiple_of(g * 64, 64), 64)
        for k in range(out_ref.shape[2] // LANES):
            sides = []
            for side in range(2):
                spot = spots_ref[g, 2 * k + side]
                tile = pl.ds(pl.multiple_of((spot >> 1) * LANES, LANES), LANES)
                sides.append(pltpu.roll(total_ref[at, tile], ((spot ^ side) & 1) * 64, 1))
            value = jnp.where(left_half, *sides)
            to = pl.ds(k * LANES, LANES)
            if blend:
                value = 2.0 * current_ref[g, :, to] - value
            out_ref[g, :, to] = value
        return carry

    lax.fori_loop(0, out_ref.shape[0], one_row, 0)


def add_traces(traces_ref, extra_ref, total_ref, trace_ref):
    known = traces_ref.shape[0]
    for k in range(known):
        trace_ref[k] = traces_ref[k]
    row = lax.broadcasted_iota(jnp.int32, (64, LANES), 0)
    spot = lax.broadcasted_iota(jnp.int32, (64, LANES), 1)
    found = jnp.zeros((64, LANES), jnp.float32)
    for g in range(total_ref.shape[0] // 64):
        block = total_ref[g * 64 : (g + 1) * 64, (g // 2) * LANES : (g // 2 + 1) * LANES]
        found += jnp.where(spot - row == 64 * (g % 2), block, 0.0)
    trace_ref[known] = jnp.sum(found) + (0.0 if extra_ref is None else extra_ref[0])


def far_trace(table, c, y_0, y_1, b_0, b_1):
    parts = [c, y_0, y_1, b_0, b_1]
    _, block, strip = c.shape
    places = pool_places(8)
    members = {"C": 0, "Y": 4, "B": 8}

    def kernel(table_ref, *refs):
        part_refs, trace_ref, wide, one, two = refs[:5], refs[5], refs[6:8], refs[8:10], refs[10:12]
        spread(part_refs, *wide)
        for k, name in enumerate("CY"):
            for m in range(4):
                for q in range(2):
                    fill_pair(
                        table_ref, places["B"][m // 2] + m % 2, places[name][q], wide,
                        members["B"] + m, [(one, m * 64, k * TILE + q * LANES)],
                    )
                    fill_pair(
                        table_ref, places[name][m // 2] + m % 2, places["B"][q], wide,
                        members[name] + m, [(two, k * TILE + m * 64, q * LANES)],
                    )
        product = three_products(one[0][...], one[1][...], two[0][...], two[1][...])
        row = lax.broadcasted_iota(jnp.int32, product.shape, 0)
        spot = lax.broadcasted_iota(jnp.int32, product.shape, 1)
        trace_ref[0] = jnp.sum(jnp.where(row == spot, product, 0.0))

    return pl.pallas_call(
        kernel,
        out_shape=jax.ShapeDtypeStruct((1,), jnp.float32),
        in_specs=[SMEM] + [VMEM] * 5,
        out_specs=SMEM,
        scratch_shapes=wide_scratch(12, strip)
        + [pltpu.VMEM((TILE, 2 * TILE), jnp.bfloat16)] * 2
        + [pltpu.VMEM((2 * TILE, TILE), jnp.bfloat16)] * 2,
        compiler_params=pltpu.CompilerParams(vmem_limit_bytes=24 * 2**20),
        cost_estimate=cost(2**20),
        name="far_trace",
    )(table, *parts)


def add_product(begin, count, table, high, low, parts, total, label, traces=None, extra=None, square=None, flops=STEP_FLOPS):
    depth_own, width = total.shape
    _, block, strip = parts[0].shape
    rows = depth_own // block
    each = TILE // block
    first = begin * each
    lists = [reach(begin + k) for k in range(count)]
    blend = square is not None and len(square) == 3
    starts = [sum(len(t) for t in lists[:k]) // 2 for k in range(count + 1)]
    codes = [
        [sum(t << (4 * k) for k, t in enumerate(tiles[side::2])) for side in range(2)]
        for tiles in lists
    ]

    def unit(i):
        group, start = jnp.int32(0), jnp.int32(0)
        code = [jnp.int32(c) for c in codes[0]]
        for k in range(1, count):
            after = i >= starts[k]
            group = jnp.where(after, k, group)
            start = jnp.where(after, starts[k], start)
            code = [jnp.where(after, new, old) for new, old in zip(codes[k], code)]
        return group, [(c >> (4 * (i - start))) & 15 for c in code]

    def kernel(table_ref, high_ref, low_ref, *refs):
        refs = list(refs)
        part_refs = [refs.pop(0) for _ in parts]
        refs.pop(0)
        if traces is not None:
            traces_ref = refs.pop(0)
        extra_ref = refs.pop(0) if extra is not None else None
        if square is not None:
            spots_ref, small_ref = refs.pop(0), refs.pop(0)
        current_ref = refs.pop(0) if blend else None
        total_ref = refs.pop(0)
        if traces is not None:
            trace_ref = refs.pop(0)
        if square is not None:
            out_ref, *rim_refs = (refs.pop(0) for _ in range(1 if blend else 6))
        wide, even, odd = refs[0:2], refs[2:4], refs[4:6]
        spread(part_refs, *wide)

        def fill_one(i, buffers):
            group, tiles = unit(i)
            for k in range(2):
                fill(table_ref, first, group * each, each, tiles[k], wide, [(buffers, k * TILE)])

        def multiply(i, buffers):
            group, tiles = unit(i)
            at = pl.ds(lane(begin + group), TILE)
            value = three_products(
                high_ref[:, at], low_ref[:, at], buffers[0][...], buffers[1][...]
            )
            for k in range(2):
                to = pl.ds(lane(tiles[k]), TILE)
                total_ref[:, to] += value[:, k * TILE : (k + 1) * TILE]

        pipelined(starts[-1], fill_one, multiply, (even, odd))
        if traces is not None:
            add_traces(traces_ref, extra_ref, total_ref, trace_ref)
        if square is not None:
            extract(spots_ref, total_ref, current_ref, out_ref, blend)
            if not blend:
                share(out_ref, small_ref, rim_refs)

    ins = [table, high, low, *parts, total]
    in_specs = [SMEM] + [VMEM] * (3 + len(parts))
    out_shape = [jax.ShapeDtypeStruct((depth_own, width), jnp.float32)]
    out_specs = [VMEM]
    if traces is not None:
        ins.append(traces)
        in_specs.append(SMEM)
        out_shape.append(jax.ShapeDtypeStruct((traces.shape[0] + 1,), jnp.float32))
        out_specs.append(SMEM)
    if extra is not None:
        ins.append(extra)
        in_specs.append(SMEM)
    if square is not None:
        ins += square
        in_specs += [SMEM, SMEM] + [VMEM] * blend
        shape = lambda n: jax.ShapeDtypeStruct((n, block, strip), jnp.float32)
        out_shape.append(shape(rows))
        if not blend:
            out_shape += [shape(each)] + [shape(each // 2)] * 4
        out_specs += [VMEM] * (len(out_shape) - len(out_specs))
    scratch = wide_scratch(count * each, strip)
    scratch += [pltpu.VMEM((TILE, 2 * TILE), jnp.bfloat16)] * 4
    return pl.pallas_call(
        kernel,
        out_shape=out_shape,
        in_specs=in_specs,
        out_specs=out_specs,
        scratch_shapes=scratch,
        input_output_aliases={3 + len(parts): 0},
        compiler_params=pltpu.CompilerParams(vmem_limit_bytes=24 * 2**20),
        cost_estimate=cost(flops),
        name=label,
    )(*ins)


def sum_rounds(count_x, count_y):
    rounds = []
    for count, at in ((count_y, 1), (count_x, 0)):
        bit = 1
        while bit < count:
            reached = min(8, count // bit)
            rounds.append(
                [
                    flat_perm(count_x, count_y, lambda i, j: (i, j ^ b) if at else (i ^ b, j))
                    for b in range(bit, reached * bit, bit)
                ]
            )
            bit *= reached
    return rounds


def sum_round(value, perms, beside=None):
    values = [value] + [lax.ppermute(value, AXES, perm) for perm in perms]
    if beside is not None:
        *values, _ = lax.optimization_barrier((*values, beside))
    while len(values) > 1:
        values = [one + two for one, two in zip(values[::2], values[1::2])]
    return values[0]


def shards(density, moves, cols, halo_rows):
    row_count, block, strip = density.shape[2:]
    rim_count = halo_rows.shape[2]
    count_x = lax.axis_size("gx")
    count_y = lax.axis_size("gy")
    rows = density.reshape(row_count, block, strip)
    rims = halo_rows.reshape(rim_count)
    own_cols = cols.reshape(row_count, -1)

    *leaving, small, own_cols = pack(
        moves.reshape(row_count), rims, own_cols, rows, count_x, count_y
    )
    arrived = [None] * len(step_x)
    for d in range(len(step_x)):
        dx, dy = int(step_x[d]), int(step_y[d])
        perm = flat_perm(count_x, count_y, lambda i, j: (i + dx, j + dy))
        arrived[d] = lax.ppermute(leaving[d], AXES, perm)

    current, *shared, traces = place(small, arrived, strip)
    spots, table = tables(small, own_cols, arrived)
    swap = {
        "A": flat_perm(count_x, count_y, toward_a),
        "B": flat_perm(count_x, count_y, along_b),
        "C": flat_perm(count_x, count_y, toward_c),
        "Y": flat_perm(count_x, count_y, toward_y),
    }
    go = lambda value, way: lax.ppermute(value, AXES, swap[way])
    rounds = sum_rounds(count_x, count_y)
    tie = lax.optimization_barrier
    for step in range(STEPS):
        c, a_1, y_0 = (go(rim, way) for rim, way in zip(shared[:3], "CAY"))
        wide_high, wide_low = spread_own(current)
        wide_high, *shared = tie((wide_high, *shared[3:]))
        a_0, y_1 = (go(rim, way) for rim, way in zip(shared, "AY"))
        high, low, total = own_product(table, (wide_high, wide_low), row_count, block)
        add = functools.partial(add_product, table=table, high=high, low=low)
        a_1, y_0, c, total = tie((a_1, y_0, c, total))
        b_1, ya_1, ya_0 = go(a_1, "B"), go(a_1, "Y"), go(y_0, "A")
        (total,) = add(2, 2, parts=[c, a_1, y_0], total=total, label="first_product")
        a_0, y_1, total = tie((a_0, y_1, total))
        b_0 = go(a_0, "B")
        (total,) = add(4, 1, parts=[a_0, y_1], total=total, label="second_product")
        b_1, ya_0, total = tie((b_1, ya_0, total))
        yb_1, yb_0 = go(b_1, "Y"), go(ya_0, "B")
        ca = go(jnp.concatenate([a_0, a_1]), "C")
        (total,) = add(5, 1, parts=[b_1, ya_1], total=total, label="third_product")
        b_0, total = tie((b_0, total))
        cb = go(jnp.concatenate([b_0, b_1]), "C")
        last = functools.partial(add, 9, 1, parts=[cb], label="last_product")
        fourth = functools.partial(add, 6, 2, parts=[b_0, ya_0, ca], label="fourth_product", flops=2**20)
        fifth = functools.partial(add, 8, 1, parts=[yb_0, yb_1], label="fifth_product", flops=2**37)
        if step % 2 == 0:
            (total,) = fourth(total=total)
            (total,) = fifth(total=total)
            total, traces, current, *shared = last(
                total=total, traces=traces, square=(spots, small)
            )
        else:
            extra = far_trace(table, c, y_0, y_1, b_0, b_1)
            total, sums = fourth(total=total, traces=traces, extra=extra)
            sums = sum_round(sums, rounds[0])
            (total,) = fifth(total=total)
            sums, total = tie((sums, total))
            for perms in rounds[1:-1]:
                sums = sum_round(sums, perms)
                sums, total = tie((sums, total))
            _, current = last(total=total, square=(spots, small, current))
            sums = sum_round(sums, rounds[-1], current)
    sums = sums * (1.0 / (count_x * count_y * row_count * block))
    occupation = jnp.stack([sums[0], sums[1], sums[1], sums[2]])
    return (current.reshape(density.shape), occupation)


def solution(mesh):
    in_specs = (
        P("gx", "gy", None, None, None),
        P("gx", "gy", None),
        P("gx", "gy", None, None),
        P("gx", "gy", None),
    )
    out_specs = (P("gx", "gy", None, None, None), P())
    return jax.shard_map(shards, mesh=mesh, in_specs=in_specs, out_specs=out_specs, check_vma=False)
```

```python
import functools

import jax
import jax.numpy as jnp
import numpy as np
from jax import lax
from jax.experimental import pallas as pl
from jax.experimental.pallas import tpu as pltpu
from jax.sharding import PartitionSpec as P

STEPS = 2
AXES = ("gx", "gy")
LANES = 128
TILE = 256

step_x = np.array([0, 0, -1, 1, -1, 1, -1, 1])
step_y = np.array([-1, 1, -1, 1, 1, -1, 0, 0])

FRAME = {
    "C": (0, 1),
    "A": (1, 0),
    "Y": (0, -1),
    "CA": (1, 1),
    "B": (-1, 0),
    "YA": (1, -1),
    "CB": (-1, 1),
    "YB": (-1, -1),
}


OWN_TILES = 2
TILES = (
    (("A", 2, 2), ("Y", 0, 2)),
    (("A", 0, 2), ("Y", 2, 2)),
    (("C", 0, 4),),
    (("B", 2, 2), ("YA", 2, 2)),
    (("B", 0, 2), ("YA", 0, 2)),
    (("CA", 0, 4),),
    (("CB", 0, 4),),
    (("YB", 0, 4),),
)


def pool_places(rows):
    places = {}
    for t, members in enumerate(TILES):
        at = rows + 4 * t
        for name, begin, count in members:
            places.setdefault(name, [0, 0])
            if begin == 0:
                places[name][0] = at
            if begin + count == 4:
                places[name][1] = at + count - 2
            at += count
    return places


def reach(t):
    def frames(n):
        return [(0, 0)] if n < OWN_TILES else [FRAME[m[0]] for m in TILES[n - OWN_TILES]]

    near = lambda p, q: abs(p[0] - q[0]) <= 1 and abs(p[1] - q[1]) <= 1
    count = OWN_TILES + len(TILES)
    found = [n for n in range(count) if any(near(p, q) for p in frames(t) for q in frames(n))]
    if len(found) % 2:
        found.append(next(n for n in range(count) if n not in found))
    return found


def flat_perm(count_x, count_y, move):
    pairs = []
    for i in range(count_x):
        for j in range(count_y):
            x, y = move(i, j)
            pairs.append((i * count_y + j, (x % count_x) * count_y + y % count_y))
    return pairs


def toward_a(i, j):
    return i ^ 1, j


def along_b(i, j):
    return (i + 2 if i % 2 == 0 else i - 2), j


def toward_c(i, j):
    return i, j ^ 1


def toward_y(i, j):
    return i, (j - 1 if j % 2 == 0 else j + 1)


def split(value):
    high = value.astype(jnp.bfloat16)
    low = (value - high.astype(jnp.float32)).astype(jnp.bfloat16)
    return high, low


def trace_of(block):
    row = lax.broadcasted_iota(jnp.int32, block.shape, 0)
    lane = lax.broadcasted_iota(jnp.int32, block.shape, 1)
    return jnp.sum(jnp.where(row == lane, block, 0.0))


def quotient(value, by, most):
    total = jnp.zeros_like(value)
    for k in range(1, most + 1):
        total += (value >= by * k).astype(jnp.int32)
    return total


VMEM = pl.BlockSpec(memory_space=pltpu.VMEM)
SMEM = pl.BlockSpec(memory_space=pltpu.SMEM)


def pack(moves, rims, cols, rows, count_x, count_y):
    row_count, block, strip = rows.shape
    slots = cols.shape[1]
    rim_count = rims.shape[0]
    tiles = strip // LANES
    ways = len(step_x)

    def kernel(moves_in, rims_in, cols_in, rows_in, *refs):
        outs, refs = refs[:ways], refs[ways:]
        small_ref, cols_ref, moves_ref, rims_ref, rows_ref, codes_ref, tail_ref, sems = refs
        copies = [
            pltpu.make_async_copy(source, target, sems.at[k])
            for k, (source, target) in enumerate(
                (
                    (moves_in, moves_ref),
                    (rims_in, rims_ref),
                    (cols_in, cols_ref),
                    (rows_in, rows_ref),
                )
            )
        ]
        for copy in copies:
            copy.start()
        index_x = lax.axis_index("gx")
        index_y = lax.axis_index("gy")
        for copy in copies[:3]:
            copy.wait()
        cols = cols_ref[...]
        inner = jnp.full(cols.shape, -1, jnp.int32)
        for m in range(rim_count):
            small_ref[ways + m] = rims_ref[m]
            inner = jnp.where(cols == rims_ref[m], 4 * rim_count + m, inner)
        away = cols - row_count
        direction = quotient(away, rim_count, ways - 1)
        place = direction + (direction >= 4).astype(jnp.int32)
        code = jnp.where(
            cols < row_count, inner, place * rim_count + away - direction * rim_count
        )
        codes_ref[...] = jnp.zeros(codes_ref.shape, jnp.float32)
        tail_ref[...] = jnp.zeros(tail_ref.shape, jnp.float32)
        codes_ref[:, :slots] = code.astype(jnp.float32)
        for m in range(rim_count):
            tail_ref[pl.ds(m, 1), :] = codes_ref[pl.ds(rims_ref[m], 1), :]
        leaving = []
        for d in range(ways):
            x = lax.rem(index_x + int(step_x[d]) + count_x, count_x)
            y = lax.rem(index_y + int(step_y[d]) + count_y, count_y)
            first = (x * count_y + y) * row_count
            slot = jnp.int32(0)
            for r in range(1, row_count):
                target = moves_ref[r]
                slot = jnp.where((target >= first) & (target < first + row_count), r, slot)
            small_ref[d] = slot
            leaving.append(slot)
        copies[3].wait()
        for d in range(ways):
            for k in range(tiles):
                outs[d][k * block : (k + 1) * block, :] = rows_ref[
                    leaving[d], :, k * LANES : (k + 1) * LANES
                ]
            outs[d][tiles * block :, :] = tail_ref[...]

    message = jax.ShapeDtypeStruct((tiles * block + 8, LANES), jnp.float32)
    return pl.pallas_call(
        kernel,
        out_shape=(message,) * ways
        + (
            jax.ShapeDtypeStruct((ways + rim_count,), jnp.int32),
            jax.ShapeDtypeStruct(cols.shape, jnp.int32),
        ),
        in_specs=[pl.BlockSpec(memory_space=pltpu.HBM)] * 4,
        out_specs=(VMEM,) * ways + (SMEM, VMEM),
        scratch_shapes=[
            pltpu.SMEM((row_count,), jnp.int32),
            pltpu.SMEM((rim_count,), jnp.int32),
            pltpu.VMEM(rows.shape, jnp.float32),
            pltpu.VMEM((row_count, LANES), jnp.float32),
            pltpu.VMEM((8, LANES), jnp.float32),
            pltpu.SemaphoreType.DMA((4,)),
        ],
        compiler_params=pltpu.CompilerParams(vmem_limit_bytes=16 * 2**20),
        name="pack_rows",
    )(moves, rims, cols, rows)


def share(rows_ref, small_ref, rim_refs):
    rim_ref, a_1, y_0, a_0, y_1 = rim_refs
    count = rim_ref.shape[0]
    for m in range(count):
        row = rows_ref[small_ref[len(step_x) + m]]
        rim_ref[m] = row
        for ref in (a_0, y_0) if m < count // 2 else (a_1, y_1):
            ref[m % (count // 2)] = row


def place(small, arrived, strip):
    rows = len(arrived)
    tiles = strip // LANES
    block = (arrived[0].shape[0] - 8) // tiles
    count = small.shape[0] - rows
    half = count // 2

    def kernel(small_ref, *refs):
        ins, outs = refs[:rows], refs[rows:]
        current_ref, *rim_refs, trace_ref = outs
        total = jnp.float32(0.0)
        for d in range(rows):
            for k in range(tiles):
                current_ref[small_ref[d], :, k * LANES : (k + 1) * LANES] = ins[d][
                    k * block : (k + 1) * block, :
                ]
            total += trace_of(ins[d][:block, :])
        trace_ref[0] = total
        share(current_ref, small_ref, rim_refs)

    rim = lambda n: jax.ShapeDtypeStruct((n, block, strip), jnp.float32)
    return pl.pallas_call(
        kernel,
        out_shape=(rim(rows), rim(count), rim(half), rim(half), rim(half), rim(half))
        + (jax.ShapeDtypeStruct((1,), jnp.float32),),
        in_specs=[SMEM] + [VMEM] * rows,
        out_specs=(VMEM,) * 6 + (SMEM,),
        compiler_params=pltpu.CompilerParams(vmem_limit_bytes=16 * 2**20),
        name="place_rows",
    )(small, *arrived)


def tables(small, cols, arrived):
    rows, slots = cols.shape
    rim_count = small.shape[0] - len(arrived)
    half = rim_count // 2
    pool = rows + len(TILES) * rim_count
    tail = arrived[0].shape[0] // 8 - 1
    base_of = [[0, 0]] * 9
    for name, (one, two) in pool_places(rows).items():
        x, y = FRAME[name]
        base_of[3 * (x + 1) + y + 1] = [one, two - half]

    def kernel(small_ref, cols_ref, *refs):
        tails, (spots_ref, table_ref, all_ref) = refs[: len(arrived)], refs[len(arrived) :]
        sign_x = 1 - 2 * lax.rem(lax.axis_index("gx"), 2)
        sign_y = 1 - 2 * lax.rem(lax.axis_index("gy"), 2)

        def locate(place, index, shift_x, shift_y):
            third = quotient(place, 3, 2)
            x = (third - 1) * sign_x + shift_x
            y = (place - 3 * third - 1) * sign_y + shift_y
            inside = (x >= -1) & (x <= 1) & (y >= -1) & (y <= 1)
            at = 3 * (x + 1) + y + 1
            one = two = jnp.zeros_like(index)
            for k in range(9):
                one = jnp.where(at == k, base_of[k][0], one)
                two = jnp.where(at == k, base_of[k][1], two)
            spot = index + jnp.where(index < half, one, two)
            for m in range(rim_count):
                spot = jnp.where((at == 4) & (index == m), small_ref[len(arrived) + m], spot)
            return jnp.where(inside, spot, -1)

        cols = cols_ref[...]
        away = cols - rows
        direction = quotient(away, rim_count, 7)
        place = direction + (direction >= 4).astype(jnp.int32)
        spots = locate(place, away - direction * rim_count, 0, 0)
        spots = jnp.where(cols < rows, cols, spots)
        spots_ref[...] = spots
        all_ref[...] = jnp.full(all_ref.shape, -1, jnp.int32)
        all_ref[:rows, :slots] = spots
        for d in range(len(arrived)):
            x = -int(step_x[d]) * sign_x
            y = -int(step_y[d]) * sign_y
            at = 3 * (x + 1) + y + 1
            bases = []
            for part in range(2):
                base = jnp.int32(0)
                for k in range(9):
                    base = jnp.where(at == k, base_of[k][part], base)
                bases.append(base)
            near = tails[d][...].astype(jnp.int32)
            place = quotient(near, rim_count, 8)
            spots = locate(place, near - place * rim_count, x, y)
            spots = jnp.where(near < 0, -1, spots)
            for m in range(rim_count):
                all_ref[pl.ds(bases[m // half] + m, 1), :] = spots[m : m + 1, :]
        lane = lax.broadcasted_iota(jnp.int32, (pool, LANES), 1)
        found = jnp.full((pool, LANES), -1, jnp.int32)
        for u in range(slots):
            found = jnp.where(all_ref[:, u : u + 1] == lane, u, found)
        entry = (found >> 1) + 16 * ((found ^ lane) & 1)
        table_ref[...] = jnp.where(found < 0, slots // 2, entry)

    last = pl.BlockSpec((8, LANES), lambda n: (tail, 0))
    full = lambda shape: pl.BlockSpec(shape, lambda n: (0, 0))
    return pl.pallas_call(
        kernel,
        grid=(1,),
        out_shape=(
            jax.ShapeDtypeStruct((rows, slots), jnp.int32),
            jax.ShapeDtypeStruct((pool, LANES), jnp.int32),
        ),
        in_specs=[SMEM, full((rows, slots))] + [last] * len(arrived),
        out_specs=(full((rows, slots)), full((pool, LANES))),
        scratch_shapes=[pltpu.VMEM((pool, LANES), jnp.int32)],
        compiler_params=pltpu.CompilerParams(vmem_limit_bytes=4 * 2**20),
        name="make_tables",
    )(small, cols, *arrived)


def spread(parts, high_ref, low_ref):
    base = 0
    strip = parts[0].shape[2]
    for ref in parts:

        def one(c, carry, ref=ref, base=base):
            at = pl.ds(pl.multiple_of((base + c) * 64, 64), 64)
            for k in range(strip // LANES):
                to = pl.ds(k * LANES, LANES)
                value = ref[c, :, to]
                for turn in range(2):
                    high, low = split(pltpu.roll(value, 64, 1) if turn else value)
                    high_ref[turn, at, to] = high
                    low_ref[turn, at, to] = low
            zeros = jnp.zeros((64, LANES), jnp.bfloat16)
            high_ref[0, at, pl.ds(strip, LANES)] = zeros
            low_ref[0, at, pl.ds(strip, LANES)] = zeros
            return carry

        lax.fori_loop(0, ref.shape[0], one, 0)
        base += ref.shape[0]


def fill_pair(table_ref, position, spot, source, member, targets):
    left_half = lax.broadcasted_iota(jnp.int32, (64, LANES), 1) < 64
    at = pl.ds(pl.multiple_of(member * 64, 64), 64)
    left = table_ref[position, spot]
    right = table_ref[position, spot + 1]
    from_left = pl.ds(pl.multiple_of((left & 15) * LANES, LANES), LANES)
    from_right = pl.ds(pl.multiple_of((right & 15) * LANES, LANES), LANES)
    for k in range(2):
        value = jnp.where(
            left_half, source[k][left >> 4, at, from_left], source[k][right >> 4, at, from_right]
        )
        for refs, row, first in targets:
            refs[k][pl.ds(row, 64), pl.ds(pl.multiple_of(first, LANES), LANES)] = value


def fill(table_ref, first, member, members, tile, source, targets):
    for c in range(members):
        for q in range(TILE // LANES):
            fill_pair(
                table_ref, first + member + c, tile * (TILE // 64) + 2 * q, source, member + c,
                [(refs, c * 64, to + q * LANES) for refs, to in targets],
            )


def three_products(a_high, a_low, d_high, d_low):
    left = jnp.concatenate([a_high, a_high, a_low], axis=1)
    right = jnp.concatenate([d_high, d_low, d_high], axis=0)
    return jnp.dot(left, right, preferred_element_type=jnp.float32)


def wide_scratch(members, strip):
    return [pltpu.VMEM((2, members * 64, strip + LANES), jnp.bfloat16)] * 2


def pipelined(units, fill_one, multiply, buffers):
    even, odd = buffers
    fill_one(jnp.int32(0), even)

    def two(j, carry):
        fill_one(2 * j + 1, odd)
        multiply(2 * j, even)
        fill_one(jnp.minimum(2 * j + 2, units - 1), even)
        multiply(2 * j + 1, odd)
        return carry

    lax.fori_loop(0, units // 2, two, 0)
    if units % 2:
        multiply(units - 1, even)


def lane(tile):
    return pl.multiple_of(tile * TILE, TILE)


def cost(units):
    return pl.CostEstimate(flops=units * 2**27, bytes_accessed=2**16, transcendentals=0)


def spread_own(current):
    rows, block, strip = current.shape

    def kernel(current_ref, high_ref, low_ref):
        spread([current_ref], high_ref, low_ref)

    wide = jax.ShapeDtypeStruct((2, rows * block, strip + LANES), jnp.bfloat16)
    return pl.pallas_call(
        kernel,
        out_shape=(wide, wide),
        in_specs=[VMEM],
        out_specs=(VMEM, VMEM),
        compiler_params=pltpu.CompilerParams(vmem_limit_bytes=16 * 2**20),
        cost_estimate=cost(1),
        name="spread_own",
    )(current)


def own_product(table, wide, rows, block):
    width = table.shape[0] * block
    depth = rows * block
    tiles = width // TILE

    def kernel(table_ref, wide_high, wide_low, high_ref, low_ref, total_ref, *scratch):
        wide = wide_high, wide_low
        own, even, odd = scratch[0:2], scratch[2:4], scratch[4:6]
        for n in range(depth // TILE):
            fill(table_ref, 0, 0, rows, n, wide, [(own, n * TILE)])

        def fill_one(i, buffers):
            for k in range(2):
                fill(
                    table_ref, 0, 0, rows, 2 * i + k, wide,
                    [(buffers, k * TILE), ((high_ref, low_ref), (2 * i + k) * TILE)],
                )

        def multiply(i, buffers):
            to = pl.ds(pl.multiple_of(2 * i * TILE, 2 * TILE), 2 * TILE)
            total_ref[:, to] = three_products(
                own[0][...], own[1][...], buffers[0][...], buffers[1][...]
            )

        pipelined(tiles // 2, fill_one, multiply, (even, odd))

    dense = lambda t: jax.ShapeDtypeStruct((depth, width), t)
    return pl.pallas_call(
        kernel,
        out_shape=(dense(jnp.bfloat16), dense(jnp.bfloat16), dense(jnp.float32)),
        in_specs=[SMEM, VMEM, VMEM],
        out_specs=(VMEM, VMEM, VMEM),
        scratch_shapes=[pltpu.VMEM((depth, depth), jnp.bfloat16)] * 2
        + [pltpu.VMEM((depth, 2 * TILE), jnp.bfloat16)] * 4,
        compiler_params=pltpu.CompilerParams(vmem_limit_bytes=24 * 2**20),
        cost_estimate=cost(2 * tiles),
        name="own_product",
    )(table, *wide)


def extract(spots_ref, total_ref, current_ref, out_ref, blend):
    left_half = lax.broadcasted_iota(jnp.int32, (64, LANES), 1) < 64

    def one_row(g, carry):
        at = pl.ds(pl.multiple_of(g * 64, 64), 64)
        for k in range(out_ref.shape[2] // LANES):
            sides = []
            for side in range(2):
                spot = spots_ref[g, 2 * k + side]
                tile = pl.ds(pl.multiple_of((spot >> 1) * LANES, LANES), LANES)
                sides.append(pltpu.roll(total_ref[at, tile], ((spot ^ side) & 1) * 64, 1))
            value = jnp.where(left_half, *sides)
            to = pl.ds(k * LANES, LANES)
            if blend:
                value = 2.0 * current_ref[g, :, to] - value
            out_ref[g, :, to] = value
        return carry

    lax.fori_loop(0, out_ref.shape[0], one_row, 0)


def add_traces(traces_ref, extra_ref, total_ref, trace_ref):
    known = traces_ref.shape[0]
    for k in range(known):
        trace_ref[k] = traces_ref[k]
    row = lax.broadcasted_iota(jnp.int32, (64, LANES), 0)
    spot = lax.broadcasted_iota(jnp.int32, (64, LANES), 1)
    found = jnp.zeros((64, LANES), jnp.float32)
    for g in range(total_ref.shape[0] // 64):
        block = total_ref[g * 64 : (g + 1) * 64, (g // 2) * LANES : (g // 2 + 1) * LANES]
        found += jnp.where(spot - row == 64 * (g % 2), block, 0.0)
    trace_ref[known] = jnp.sum(found) + (0.0 if extra_ref is None else extra_ref[0])


def far_trace(table, c, y_0, y_1, b_0, b_1):
    parts = [c, y_0, y_1, b_0, b_1]
    _, block, strip = c.shape
    places = pool_places(8)
    members = {"C": 0, "Y": 4, "B": 8}

    def kernel(table_ref, *refs):
        part_refs, trace_ref, wide, one, two = refs[:5], refs[5], refs[6:8], refs[8:10], refs[10:12]
        spread(part_refs, *wide)
        for k, name in enumerate("CY"):
            for m in range(4):
                for q in range(2):
                    fill_pair(
                        table_ref, places["B"][m // 2] + m % 2, places[name][q], wide,
                        members["B"] + m, [(one, m * 64, k * TILE + q * LANES)],
                    )
                    fill_pair(
                        table_ref, places[name][m // 2] + m % 2, places["B"][q], wide,
                        members[name] + m, [(two, k * TILE + m * 64, q * LANES)],
                    )
        product = three_products(one[0][...], one[1][...], two[0][...], two[1][...])
        row = lax.broadcasted_iota(jnp.int32, product.shape, 0)
        spot = lax.broadcasted_iota(jnp.int32, product.shape, 1)
        trace_ref[0] = jnp.sum(jnp.where(row == spot, product, 0.0))

    return pl.pallas_call(
        kernel,
        out_shape=jax.ShapeDtypeStruct((1,), jnp.float32),
        in_specs=[SMEM] + [VMEM] * 5,
        out_specs=SMEM,
        scratch_shapes=wide_scratch(12, strip)
        + [pltpu.VMEM((TILE, 2 * TILE), jnp.bfloat16)] * 2
        + [pltpu.VMEM((2 * TILE, TILE), jnp.bfloat16)] * 2,
        compiler_params=pltpu.CompilerParams(vmem_limit_bytes=24 * 2**20),
        cost_estimate=cost(4),
        name="far_trace",
    )(table, *parts)


def add_product(begin, count, table, high, low, parts, total, label, traces=None, extra=None, square=None):
    depth_own, width = total.shape
    _, block, strip = parts[0].shape
    rows = depth_own // block
    each = TILE // block
    first = begin * each
    lists = [reach(begin + k) for k in range(count)]
    blend = square is not None and len(square) == 3
    starts = [sum(len(t) for t in lists[:k]) // 2 for k in range(count + 1)]
    codes = [
        [sum(t << (4 * k) for k, t in enumerate(tiles[side::2])) for side in range(2)]
        for tiles in lists
    ]

    def unit(i):
        group, start = jnp.int32(0), jnp.int32(0)
        code = [jnp.int32(c) for c in codes[0]]
        for k in range(1, count):
            after = i >= starts[k]
            group = jnp.where(after, k, group)
            start = jnp.where(after, starts[k], start)
            code = [jnp.where(after, new, old) for new, old in zip(codes[k], code)]
        return group, [(c >> (4 * (i - start))) & 15 for c in code]

    def kernel(table_ref, high_ref, low_ref, *refs):
        refs = list(refs)
        part_refs = [refs.pop(0) for _ in parts]
        refs.pop(0)
        if traces is not None:
            traces_ref = refs.pop(0)
        extra_ref = refs.pop(0) if extra is not None else None
        if square is not None:
            spots_ref, small_ref = refs.pop(0), refs.pop(0)
        current_ref = refs.pop(0) if blend else None
        total_ref = refs.pop(0)
        if traces is not None:
            trace_ref = refs.pop(0)
        if square is not None:
            out_ref, *rim_refs = (refs.pop(0) for _ in range(1 if blend else 6))
        wide, even, odd = refs[0:2], refs[2:4], refs[4:6]
        spread(part_refs, *wide)

        def fill_one(i, buffers):
            group, tiles = unit(i)
            for k in range(2):
                fill(table_ref, first, group * each, each, tiles[k], wide, [(buffers, k * TILE)])

        def multiply(i, buffers):
            group, tiles = unit(i)
            at = pl.ds(lane(begin + group), TILE)
            value = three_products(
                high_ref[:, at], low_ref[:, at], buffers[0][...], buffers[1][...]
            )
            for k in range(2):
                to = pl.ds(lane(tiles[k]), TILE)
                total_ref[:, to] += value[:, k * TILE : (k + 1) * TILE]

        pipelined(starts[-1], fill_one, multiply, (even, odd))
        if traces is not None:
            add_traces(traces_ref, extra_ref, total_ref, trace_ref)
        if square is not None:
            extract(spots_ref, total_ref, current_ref, out_ref, blend)
            if not blend:
                share(out_ref, small_ref, rim_refs)

    ins = [table, high, low, *parts, total]
    in_specs = [SMEM] + [VMEM] * (3 + len(parts))
    out_shape = [jax.ShapeDtypeStruct((depth_own, width), jnp.float32)]
    out_specs = [VMEM]
    if traces is not None:
        ins.append(traces)
        in_specs.append(SMEM)
        out_shape.append(jax.ShapeDtypeStruct((traces.shape[0] + 1,), jnp.float32))
        out_specs.append(SMEM)
    if extra is not None:
        ins.append(extra)
        in_specs.append(SMEM)
    if square is not None:
        ins += square
        in_specs += [SMEM, SMEM] + [VMEM] * blend
        shape = lambda n: jax.ShapeDtypeStruct((n, block, strip), jnp.float32)
        out_shape.append(shape(rows))
        if not blend:
            out_shape += [shape(each)] + [shape(each // 2)] * 4
        out_specs += [VMEM] * (len(out_shape) - len(out_specs))
    scratch = wide_scratch(count * each, strip)
    scratch += [pltpu.VMEM((TILE, 2 * TILE), jnp.bfloat16)] * 4
    return pl.pallas_call(
        kernel,
        out_shape=out_shape,
        in_specs=in_specs,
        out_specs=out_specs,
        scratch_shapes=scratch,
        input_output_aliases={3 + len(parts): 0},
        compiler_params=pltpu.CompilerParams(vmem_limit_bytes=24 * 2**20),
        cost_estimate=cost(2 * starts[-1]),
        name=label,
    )(*ins)


def sum_rounds(count_x, count_y):
    rounds = []
    for count, at in ((count_y, 1), (count_x, 0)):
        bit = 1
        while bit < count:
            bits = [bit, 2 * bit, 3 * bit] if 2 * bit < count else [bit]
            rounds.append(
                [
                    flat_perm(count_x, count_y, lambda i, j: (i, j ^ b) if at else (i ^ b, j))
                    for b in bits
                ]
            )
            bit *= 4
    return rounds


def sum_round(value, perms):
    others = [lax.ppermute(value, AXES, perm) for perm in perms]
    if len(others) == 1:
        return value + others[0]
    return (value + others[0]) + (others[1] + others[2])


def shards(density, moves, cols, halo_rows):
    row_count, block, strip = density.shape[2:]
    rim_count = halo_rows.shape[2]
    count_x = lax.axis_size("gx")
    count_y = lax.axis_size("gy")
    rows = density.reshape(row_count, block, strip)
    rims = halo_rows.reshape(rim_count)
    own_cols = cols.reshape(row_count, -1)

    *leaving, small, own_cols = pack(
        moves.reshape(row_count), rims, own_cols, rows, count_x, count_y
    )
    arrived = [None] * len(step_x)
    for d in range(len(step_x)):
        dx, dy = int(step_x[d]), int(step_y[d])
        perm = flat_perm(count_x, count_y, lambda i, j: (i + dx, j + dy))
        arrived[d] = lax.ppermute(leaving[d], AXES, perm)

    current, *shared, traces = place(small, arrived, strip)
    spots, table = tables(small, own_cols, arrived)
    swap = {
        "A": flat_perm(count_x, count_y, toward_a),
        "B": flat_perm(count_x, count_y, along_b),
        "C": flat_perm(count_x, count_y, toward_c),
        "Y": flat_perm(count_x, count_y, toward_y),
    }
    go = lambda value, way: lax.ppermute(value, AXES, swap[way])
    rounds = sum_rounds(count_x, count_y)
    tie = lax.optimization_barrier
    for step in range(STEPS):
        c, a_1, y_0 = (go(rim, way) for rim, way in zip(shared[:3], "CAY"))
        wide_high, wide_low = spread_own(current)
        wide_high, *shared = tie((wide_high, *shared[3:]))
        a_0, y_1 = (go(rim, way) for rim, way in zip(shared, "AY"))
        high, low, total = own_product(table, (wide_high, wide_low), row_count, block)
        add = functools.partial(add_product, table=table, high=high, low=low)
        a_1, y_0, c, total = tie((a_1, y_0, c, total))
        b_1, ya_1, ya_0 = go(a_1, "B"), go(a_1, "Y"), go(y_0, "A")
        (total,) = add(2, 1, parts=[a_1, y_0], total=total, label="first_product")
        a_0, y_1, total = tie((a_0, y_1, total))
        b_0 = go(a_0, "B")
        (total,) = add(3, 2, parts=[a_0, y_1, c], total=total, label="second_product")
        a_0, b_1, ya_0, total = tie((a_0, b_1, ya_0, total))
        yb_1, yb_0 = go(b_1, "Y"), go(ya_0, "B")
        ca = go(jnp.concatenate([a_0, a_1]), "C")
        (total,) = add(5, 1, parts=[b_1, ya_1], total=total, label="third_product")
        b_0, total = tie((b_0, total))
        cb = go(jnp.concatenate([b_0, b_1]), "C")
        last = functools.partial(add, 9, 1, parts=[yb_0, yb_1], label="last_product")
        fourth = functools.partial(add, 6, 2, parts=[b_0, ya_0, ca], label="fourth_product")
        fifth = functools.partial(add, 8, 1, parts=[cb], label="fifth_product")
        if step % 2 == 0:
            (total,) = fourth(total=total)
            (total,) = fifth(total=total)
            total, traces, current, *shared = last(
                total=total, traces=traces, square=(spots, small)
            )
        else:
            extra = far_trace(table, c, y_0, y_1, b_0, b_1)
            total, sums = fourth(total=total, traces=traces, extra=extra)
            sums = sum_round(sums, rounds[0])
            (total,) = fifth(total=total)
            sums, total = tie((sums, total))
            for perms in rounds[1:-1]:
                sums = sum_round(sums, perms)
            sums, total = tie((sums, total))
            sums = sum_round(sums, rounds[-1])
            _, current = last(total=total, square=(spots, small, current))
    sums = sums * (1.0 / (count_x * count_y * row_count * block))
    occupation = jnp.stack([sums[0], sums[1], sums[1], sums[2]])
    return (current.reshape(density.shape), occupation)


def solution(mesh):
    in_specs = (
        P("gx", "gy", None, None, None),
        P("gx", "gy", None),
        P("gx", "gy", None, None),
        P("gx", "gy", None),
    )
    out_specs = (P("gx", "gy", None, None, None), P())
    return jax.shard_map(shards, mesh=mesh, in_specs=in_specs, out_specs=out_specs, check_vma=False)
```

```python
import functools

import jax
import jax.numpy as jnp
import numpy as np
from jax import lax
from jax.experimental import pallas as pl
from jax.experimental.pallas import tpu as pltpu
from jax.sharding import PartitionSpec as P

STEPS = 2
AXES = ("gx", "gy")
LANES = 128
TILE = 256

step_x = np.array([0, 0, -1, 1, -1, 1, -1, 1])
step_y = np.array([-1, 1, -1, 1, 1, -1, 0, 0])

FRAME = {
    "C": (0, 1),
    "A": (1, 0),
    "Y": (0, -1),
    "CA": (1, 1),
    "B": (-1, 0),
    "YA": (1, -1),
    "CB": (-1, 1),
    "YB": (-1, -1),
}


OWN_TILES = 2
TILES = (
    (("A", 2, 2), ("Y", 0, 2)),
    (("A", 0, 2), ("Y", 2, 2)),
    (("C", 0, 4),),
    (("B", 2, 2), ("YA", 2, 2)),
    (("B", 0, 2), ("YA", 0, 2)),
    (("CA", 0, 4),),
    (("CB", 0, 4),),
    (("YB", 0, 4),),
)


def pool_places(rows):
    places = {}
    for t, members in enumerate(TILES):
        at = rows + 4 * t
        for name, begin, count in members:
            places.setdefault(name, [0, 0])
            if begin == 0:
                places[name][0] = at
            if begin + count == 4:
                places[name][1] = at + count - 2
            at += count
    return places


def reach(t):
    def frames(n):
        return [(0, 0)] if n < OWN_TILES else [FRAME[m[0]] for m in TILES[n - OWN_TILES]]

    near = lambda p, q: abs(p[0] - q[0]) <= 1 and abs(p[1] - q[1]) <= 1
    count = OWN_TILES + len(TILES)
    found = [n for n in range(count) if any(near(p, q) for p in frames(t) for q in frames(n))]
    if len(found) % 2:
        found.append(next(n for n in range(count) if n not in found))
    return found


def flat_perm(count_x, count_y, move):
    pairs = []
    for i in range(count_x):
        for j in range(count_y):
            x, y = move(i, j)
            pairs.append((i * count_y + j, (x % count_x) * count_y + y % count_y))
    return pairs


def toward_a(i, j):
    return i ^ 1, j


def along_b(i, j):
    return (i + 2 if i % 2 == 0 else i - 2), j


def toward_c(i, j):
    return i, j ^ 1


def toward_y(i, j):
    return i, (j - 1 if j % 2 == 0 else j + 1)


def split(value):
    high = value.astype(jnp.bfloat16)
    low = (value - high.astype(jnp.float32)).astype(jnp.bfloat16)
    return high, low


def trace_of(block):
    row = lax.broadcasted_iota(jnp.int32, block.shape, 0)
    lane = lax.broadcasted_iota(jnp.int32, block.shape, 1)
    return jnp.sum(jnp.where(row == lane, block, 0.0))


def quotient(value, by, most):
    total = jnp.zeros_like(value)
    for k in range(1, most + 1):
        total += (value >= by * k).astype(jnp.int32)
    return total


VMEM = pl.BlockSpec(memory_space=pltpu.VMEM)
SMEM = pl.BlockSpec(memory_space=pltpu.SMEM)


def pack(moves, rims, cols, rows, count_x, count_y):
    row_count, block, strip = rows.shape
    slots = cols.shape[1]
    rim_count = rims.shape[0]
    tiles = strip // LANES
    ways = len(step_x)

    def kernel(moves_in, rims_in, cols_in, rows_in, *refs):
        outs, refs = refs[:ways], refs[ways:]
        small_ref, cols_ref, moves_ref, rims_ref, rows_ref, codes_ref, tail_ref, sems = refs
        copies = [
            pltpu.make_async_copy(source, target, sems.at[k])
            for k, (source, target) in enumerate(
                (
                    (moves_in, moves_ref),
                    (rims_in, rims_ref),
                    (cols_in, cols_ref),
                    (rows_in, rows_ref),
                )
            )
        ]
        for copy in copies:
            copy.start()
        index_x = lax.axis_index("gx")
        index_y = lax.axis_index("gy")
        for copy in copies[:3]:
            copy.wait()
        cols = cols_ref[...]
        inner = jnp.full(cols.shape, -1, jnp.int32)
        for m in range(rim_count):
            small_ref[ways + m] = rims_ref[m]
            inner = jnp.where(cols == rims_ref[m], 4 * rim_count + m, inner)
        away = cols - row_count
        direction = quotient(away, rim_count, ways - 1)
        place = direction + (direction >= 4).astype(jnp.int32)
        code = jnp.where(
            cols < row_count, inner, place * rim_count + away - direction * rim_count
        )
        codes_ref[...] = jnp.zeros(codes_ref.shape, jnp.float32)
        tail_ref[...] = jnp.zeros(tail_ref.shape, jnp.float32)
        codes_ref[:, :slots] = code.astype(jnp.float32)
        for m in range(rim_count):
            tail_ref[pl.ds(m, 1), :] = codes_ref[pl.ds(rims_ref[m], 1), :]
        leaving = []
        for d in range(ways):
            x = lax.rem(index_x + int(step_x[d]) + count_x, count_x)
            y = lax.rem(index_y + int(step_y[d]) + count_y, count_y)
            first = (x * count_y + y) * row_count
            slot = jnp.int32(0)
            for r in range(1, row_count):
                target = moves_ref[r]
                slot = jnp.where((target >= first) & (target < first + row_count), r, slot)
            small_ref[d] = slot
            leaving.append(slot)
        copies[3].wait()
        for d in range(ways):
            for k in range(tiles):
                outs[d][k * block : (k + 1) * block, :] = rows_ref[
                    leaving[d], :, k * LANES : (k + 1) * LANES
                ]
            outs[d][tiles * block :, :] = tail_ref[...]

    message = jax.ShapeDtypeStruct((tiles * block + 8, LANES), jnp.float32)
    return pl.pallas_call(
        kernel,
        out_shape=(message,) * ways
        + (
            jax.ShapeDtypeStruct((ways + rim_count,), jnp.int32),
            jax.ShapeDtypeStruct(cols.shape, jnp.int32),
        ),
        in_specs=[pl.BlockSpec(memory_space=pltpu.HBM)] * 4,
        out_specs=(VMEM,) * ways + (SMEM, VMEM),
        scratch_shapes=[
            pltpu.SMEM((row_count,), jnp.int32),
            pltpu.SMEM((rim_count,), jnp.int32),
            pltpu.VMEM(rows.shape, jnp.float32),
            pltpu.VMEM((row_count, LANES), jnp.float32),
            pltpu.VMEM((8, LANES), jnp.float32),
            pltpu.SemaphoreType.DMA((4,)),
        ],
        compiler_params=pltpu.CompilerParams(vmem_limit_bytes=16 * 2**20),
        name="pack_rows",
    )(moves, rims, cols, rows)


def share(rows_ref, small_ref, rim_refs):
    rim_ref, a_1, y_0, a_0, y_1 = rim_refs
    count = rim_ref.shape[0]
    for m in range(count):
        row = rows_ref[small_ref[len(step_x) + m]]
        rim_ref[m] = row
        for ref in (a_0, y_0) if m < count // 2 else (a_1, y_1):
            ref[m % (count // 2)] = row


def place(small, arrived, strip):
    rows = len(arrived)
    tiles = strip // LANES
    block = (arrived[0].shape[0] - 8) // tiles
    count = small.shape[0] - rows
    half = count // 2

    def kernel(small_ref, *refs):
        ins, outs = refs[:rows], refs[rows:]
        current_ref, *rim_refs, trace_ref = outs
        total = jnp.float32(0.0)
        for d in range(rows):
            for k in range(tiles):
                current_ref[small_ref[d], :, k * LANES : (k + 1) * LANES] = ins[d][
                    k * block : (k + 1) * block, :
                ]
            total += trace_of(ins[d][:block, :])
        trace_ref[0] = total
        share(current_ref, small_ref, rim_refs)

    rim = lambda n: jax.ShapeDtypeStruct((n, block, strip), jnp.float32)
    return pl.pallas_call(
        kernel,
        out_shape=(rim(rows), rim(count), rim(half), rim(half), rim(half), rim(half))
        + (jax.ShapeDtypeStruct((1,), jnp.float32),),
        in_specs=[SMEM] + [VMEM] * rows,
        out_specs=(VMEM,) * 6 + (SMEM,),
        compiler_params=pltpu.CompilerParams(vmem_limit_bytes=16 * 2**20),
        name="place_rows",
    )(small, *arrived)


def tables(small, cols, arrived):
    rows, slots = cols.shape
    rim_count = small.shape[0] - len(arrived)
    half = rim_count // 2
    pool = rows + len(TILES) * rim_count
    tail = arrived[0].shape[0] // 8 - 1
    base_of = [[0, 0]] * 9
    for name, (one, two) in pool_places(rows).items():
        x, y = FRAME[name]
        base_of[3 * (x + 1) + y + 1] = [one, two - half]

    def kernel(small_ref, cols_ref, *refs):
        tails, (spots_ref, table_ref, all_ref) = refs[: len(arrived)], refs[len(arrived) :]
        sign_x = 1 - 2 * lax.rem(lax.axis_index("gx"), 2)
        sign_y = 1 - 2 * lax.rem(lax.axis_index("gy"), 2)

        def locate(place, index, shift_x, shift_y):
            third = quotient(place, 3, 2)
            x = (third - 1) * sign_x + shift_x
            y = (place - 3 * third - 1) * sign_y + shift_y
            inside = (x >= -1) & (x <= 1) & (y >= -1) & (y <= 1)
            at = 3 * (x + 1) + y + 1
            one = two = jnp.zeros_like(index)
            for k in range(9):
                one = jnp.where(at == k, base_of[k][0], one)
                two = jnp.where(at == k, base_of[k][1], two)
            spot = index + jnp.where(index < half, one, two)
            for m in range(rim_count):
                spot = jnp.where((at == 4) & (index == m), small_ref[len(arrived) + m], spot)
            return jnp.where(inside, spot, -1)

        cols = cols_ref[...]
        away = cols - rows
        direction = quotient(away, rim_count, 7)
        place = direction + (direction >= 4).astype(jnp.int32)
        spots = locate(place, away - direction * rim_count, 0, 0)
        spots = jnp.where(cols < rows, cols, spots)
        spots_ref[...] = spots
        all_ref[...] = jnp.full(all_ref.shape, -1, jnp.int32)
        all_ref[:rows, :slots] = spots
        for d in range(len(arrived)):
            x = -int(step_x[d]) * sign_x
            y = -int(step_y[d]) * sign_y
            at = 3 * (x + 1) + y + 1
            bases = []
            for part in range(2):
                base = jnp.int32(0)
                for k in range(9):
                    base = jnp.where(at == k, base_of[k][part], base)
                bases.append(base)
            near = tails[d][...].astype(jnp.int32)
            place = quotient(near, rim_count, 8)
            spots = locate(place, near - place * rim_count, x, y)
            spots = jnp.where(near < 0, -1, spots)
            for m in range(rim_count):
                all_ref[pl.ds(bases[m // half] + m, 1), :] = spots[m : m + 1, :]
        lane = lax.broadcasted_iota(jnp.int32, (pool, LANES), 1)
        found = jnp.full((pool, LANES), -1, jnp.int32)
        for u in range(slots):
            found = jnp.where(all_ref[:, u : u + 1] == lane, u, found)
        entry = (found >> 1) + 16 * ((found ^ lane) & 1)
        table_ref[...] = jnp.where(found < 0, slots // 2, entry)

    last = pl.BlockSpec((8, LANES), lambda n: (tail, 0))
    full = lambda shape: pl.BlockSpec(shape, lambda n: (0, 0))
    return pl.pallas_call(
        kernel,
        grid=(1,),
        out_shape=(
            jax.ShapeDtypeStruct((rows, slots), jnp.int32),
            jax.ShapeDtypeStruct((pool, LANES), jnp.int32),
        ),
        in_specs=[SMEM, full((rows, slots))] + [last] * len(arrived),
        out_specs=(full((rows, slots)), full((pool, LANES))),
        scratch_shapes=[pltpu.VMEM((pool, LANES), jnp.int32)],
        compiler_params=pltpu.CompilerParams(vmem_limit_bytes=4 * 2**20),
        name="make_tables",
    )(small, cols, *arrived)


def spread(parts, high_ref, low_ref):
    base = 0
    strip = parts[0].shape[2]
    for ref in parts:

        def one(c, carry, ref=ref, base=base):
            at = pl.ds(pl.multiple_of((base + c) * 64, 64), 64)
            for k in range(strip // LANES):
                to = pl.ds(k * LANES, LANES)
                value = ref[c, :, to]
                for turn in range(2):
                    high, low = split(pltpu.roll(value, 64, 1) if turn else value)
                    high_ref[turn, at, to] = high
                    low_ref[turn, at, to] = low
            zeros = jnp.zeros((64, LANES), jnp.bfloat16)
            high_ref[0, at, pl.ds(strip, LANES)] = zeros
            low_ref[0, at, pl.ds(strip, LANES)] = zeros
            return carry

        lax.fori_loop(0, ref.shape[0], one, 0)
        base += ref.shape[0]


def fill_pair(table_ref, position, spot, source, member, targets):
    left_half = lax.broadcasted_iota(jnp.int32, (64, LANES), 1) < 64
    at = pl.ds(pl.multiple_of(member * 64, 64), 64)
    left = table_ref[position, spot]
    right = table_ref[position, spot + 1]
    from_left = pl.ds(pl.multiple_of((left & 15) * LANES, LANES), LANES)
    from_right = pl.ds(pl.multiple_of((right & 15) * LANES, LANES), LANES)
    for k in range(2):
        value = jnp.where(
            left_half, source[k][left >> 4, at, from_left], source[k][right >> 4, at, from_right]
        )
        for refs, row, first in targets:
            refs[k][pl.ds(row, 64), pl.ds(pl.multiple_of(first, LANES), LANES)] = value


def fill(table_ref, first, member, members, tile, source, targets):
    for c in range(members):
        for q in range(TILE // LANES):
            fill_pair(
                table_ref, first + member + c, tile * (TILE // 64) + 2 * q, source, member + c,
                [(refs, c * 64, to + q * LANES) for refs, to in targets],
            )


def three_products(a_high, a_low, d_high, d_low):
    left = jnp.concatenate([a_high, a_high, a_low], axis=1)
    right = jnp.concatenate([d_high, d_low, d_high], axis=0)
    return jnp.dot(left, right, preferred_element_type=jnp.float32)


def wide_scratch(members, strip):
    return [pltpu.VMEM((2, members * 64, strip + LANES), jnp.bfloat16)] * 2


def pipelined(units, fill_one, multiply, buffers):
    even, odd = buffers
    fill_one(jnp.int32(0), even)

    def two(j, carry):
        multiply(2 * j, even)
        fill_one(2 * j + 1, odd)
        multiply(2 * j + 1, odd)
        fill_one(jnp.minimum(2 * j + 2, units - 1), even)
        return carry

    lax.fori_loop(0, units // 2, two, 0)
    if units % 2:
        multiply(units - 1, even)


def lane(tile):
    return pl.multiple_of(tile * TILE, TILE)


def cost(units):
    return pl.CostEstimate(flops=units * 2**27, bytes_accessed=2**16, transcendentals=0)


def spread_own(current):
    rows, block, strip = current.shape

    def kernel(current_ref, high_ref, low_ref):
        spread([current_ref], high_ref, low_ref)

    wide = jax.ShapeDtypeStruct((2, rows * block, strip + LANES), jnp.bfloat16)
    return pl.pallas_call(
        kernel,
        out_shape=(wide, wide),
        in_specs=[VMEM],
        out_specs=(VMEM, VMEM),
        compiler_params=pltpu.CompilerParams(vmem_limit_bytes=16 * 2**20),
        cost_estimate=cost(1),
        name="spread_own",
    )(current)


def own_product(table, wide, rows, block):
    width = table.shape[0] * block
    depth = rows * block
    tiles = width // TILE

    def kernel(table_ref, wide_high, wide_low, high_ref, low_ref, total_ref, *scratch):
        wide = wide_high, wide_low
        own, even, odd = scratch[0:2], scratch[2:4], scratch[4:6]
        for n in range(depth // TILE):
            fill(table_ref, 0, 0, rows, n, wide, [(own, n * TILE)])

        def fill_one(i, buffers):
            for k in range(2):
                fill(
                    table_ref, 0, 0, rows, 2 * i + k, wide,
                    [(buffers, k * TILE), ((high_ref, low_ref), (2 * i + k) * TILE)],
                )

        def multiply(i, buffers):
            to = pl.ds(pl.multiple_of(2 * i * TILE, 2 * TILE), 2 * TILE)
            total_ref[:, to] = three_products(
                own[0][...], own[1][...], buffers[0][...], buffers[1][...]
            )

        pipelined(tiles // 2, fill_one, multiply, (even, odd))

    dense = lambda t: jax.ShapeDtypeStruct((depth, width), t)
    return pl.pallas_call(
        kernel,
        out_shape=(dense(jnp.bfloat16), dense(jnp.bfloat16), dense(jnp.float32)),
        in_specs=[SMEM, VMEM, VMEM],
        out_specs=(VMEM, VMEM, VMEM),
        scratch_shapes=[pltpu.VMEM((depth, depth), jnp.bfloat16)] * 2
        + [pltpu.VMEM((depth, 2 * TILE), jnp.bfloat16)] * 4,
        compiler_params=pltpu.CompilerParams(vmem_limit_bytes=24 * 2**20),
        cost_estimate=cost(2 * tiles),
        name="own_product",
    )(table, *wide)


def extract(spots_ref, total_ref, current_ref, out_ref, blend):
    left_half = lax.broadcasted_iota(jnp.int32, (64, LANES), 1) < 64

    def one_row(g, carry):
        at = pl.ds(pl.multiple_of(g * 64, 64), 64)
        for k in range(out_ref.shape[2] // LANES):
            sides = []
            for side in range(2):
                spot = spots_ref[g, 2 * k + side]
                tile = pl.ds(pl.multiple_of((spot >> 1) * LANES, LANES), LANES)
                sides.append(pltpu.roll(total_ref[at, tile], ((spot ^ side) & 1) * 64, 1))
            value = jnp.where(left_half, *sides)
            to = pl.ds(k * LANES, LANES)
            if blend:
                value = 2.0 * current_ref[g, :, to] - value
            out_ref[g, :, to] = value
        return carry

    lax.fori_loop(0, out_ref.shape[0], one_row, 0)


def add_traces(traces_ref, extra_ref, total_ref, trace_ref):
    known = traces_ref.shape[0]
    for k in range(known):
        trace_ref[k] = traces_ref[k]
    row = lax.broadcasted_iota(jnp.int32, (64, LANES), 0)
    spot = lax.broadcasted_iota(jnp.int32, (64, LANES), 1)
    found = jnp.zeros((64, LANES), jnp.float32)
    for g in range(total_ref.shape[0] // 64):
        block = total_ref[g * 64 : (g + 1) * 64, (g // 2) * LANES : (g // 2 + 1) * LANES]
        found += jnp.where(spot - row == 64 * (g % 2), block, 0.0)
    trace_ref[known] = jnp.sum(found) + (0.0 if extra_ref is None else extra_ref[0])


def far_trace(table, c, y_0, y_1, b_0, b_1):
    parts = [c, y_0, y_1, b_0, b_1]
    _, block, strip = c.shape
    places = pool_places(8)
    members = {"C": 0, "Y": 4, "B": 8}

    def kernel(table_ref, *refs):
        part_refs, trace_ref, wide, one, two = refs[:5], refs[5], refs[6:8], refs[8:10], refs[10:12]
        spread(part_refs, *wide)
        for k, name in enumerate("CY"):
            for m in range(4):
                for q in range(2):
                    fill_pair(
                        table_ref, places["B"][m // 2] + m % 2, places[name][q], wide,
                        members["B"] + m, [(one, m * 64, k * TILE + q * LANES)],
                    )
                    fill_pair(
                        table_ref, places[name][m // 2] + m % 2, places["B"][q], wide,
                        members[name] + m, [(two, k * TILE + m * 64, q * LANES)],
                    )
        product = three_products(one[0][...], one[1][...], two[0][...], two[1][...])
        row = lax.broadcasted_iota(jnp.int32, product.shape, 0)
        spot = lax.broadcasted_iota(jnp.int32, product.shape, 1)
        trace_ref[0] = jnp.sum(jnp.where(row == spot, product, 0.0))

    return pl.pallas_call(
        kernel,
        out_shape=jax.ShapeDtypeStruct((1,), jnp.float32),
        in_specs=[SMEM] + [VMEM] * 5,
        out_specs=SMEM,
        scratch_shapes=wide_scratch(12, strip)
        + [pltpu.VMEM((TILE, 2 * TILE), jnp.bfloat16)] * 2
        + [pltpu.VMEM((2 * TILE, TILE), jnp.bfloat16)] * 2,
        compiler_params=pltpu.CompilerParams(vmem_limit_bytes=24 * 2**20),
        cost_estimate=cost(4),
        name="far_trace",
    )(table, *parts)


def add_product(begin, count, table, high, low, parts, total, label, traces=None, extra=None, square=None):
    depth_own, width = total.shape
    _, block, strip = parts[0].shape
    rows = depth_own // block
    each = TILE // block
    first = begin * each
    lists = [reach(begin + k) for k in range(count)]
    blend = square is not None and len(square) == 3
    starts = [sum(len(t) for t in lists[:k]) // 2 for k in range(count + 1)]
    codes = [
        [sum(t << (4 * k) for k, t in enumerate(tiles[side::2])) for side in range(2)]
        for tiles in lists
    ]

    def unit(i):
        group, start = jnp.int32(0), jnp.int32(0)
        code = [jnp.int32(c) for c in codes[0]]
        for k in range(1, count):
            after = i >= starts[k]
            group = jnp.where(after, k, group)
            start = jnp.where(after, starts[k], start)
            code = [jnp.where(after, new, old) for new, old in zip(codes[k], code)]
        return group, [(c >> (4 * (i - start))) & 15 for c in code]

    def kernel(table_ref, high_ref, low_ref, *refs):
        refs = list(refs)
        part_refs = [refs.pop(0) for _ in parts]
        refs.pop(0)
        if traces is not None:
            traces_ref = refs.pop(0)
        extra_ref = refs.pop(0) if extra is not None else None
        if square is not None:
            spots_ref, small_ref = refs.pop(0), refs.pop(0)
        current_ref = refs.pop(0) if blend else None
        total_ref = refs.pop(0)
        if traces is not None:
            trace_ref = refs.pop(0)
        if square is not None:
            out_ref, *rim_refs = (refs.pop(0) for _ in range(1 if blend else 6))
        wide, even, odd = refs[0:2], refs[2:4], refs[4:6]
        spread(part_refs, *wide)

        def fill_one(i, buffers):
            group, tiles = unit(i)
            for k in range(2):
                fill(table_ref, first, group * each, each, tiles[k], wide, [(buffers, k * TILE)])

        def multiply(i, buffers):
            group, tiles = unit(i)
            at = pl.ds(lane(begin + group), TILE)
            value = three_products(
                high_ref[:, at], low_ref[:, at], buffers[0][...], buffers[1][...]
            )
            for k in range(2):
                to = pl.ds(lane(tiles[k]), TILE)
                total_ref[:, to] += value[:, k * TILE : (k + 1) * TILE]

        pipelined(starts[-1], fill_one, multiply, (even, odd))
        if traces is not None:
            add_traces(traces_ref, extra_ref, total_ref, trace_ref)
        if square is not None:
            extract(spots_ref, total_ref, current_ref, out_ref, blend)
            if not blend:
                share(out_ref, small_ref, rim_refs)

    ins = [table, high, low, *parts, total]
    in_specs = [SMEM] + [VMEM] * (3 + len(parts))
    out_shape = [jax.ShapeDtypeStruct((depth_own, width), jnp.float32)]
    out_specs = [VMEM]
    if traces is not None:
        ins.append(traces)
        in_specs.append(SMEM)
        out_shape.append(jax.ShapeDtypeStruct((traces.shape[0] + 1,), jnp.float32))
        out_specs.append(SMEM)
    if extra is not None:
        ins.append(extra)
        in_specs.append(SMEM)
    if square is not None:
        ins += square
        in_specs += [SMEM, SMEM] + [VMEM] * blend
        shape = lambda n: jax.ShapeDtypeStruct((n, block, strip), jnp.float32)
        out_shape.append(shape(rows))
        if not blend:
            out_shape += [shape(each)] + [shape(each // 2)] * 4
        out_specs += [VMEM] * (len(out_shape) - len(out_specs))
    scratch = wide_scratch(count * each, strip)
    scratch += [pltpu.VMEM((TILE, 2 * TILE), jnp.bfloat16)] * 4
    return pl.pallas_call(
        kernel,
        out_shape=out_shape,
        in_specs=in_specs,
        out_specs=out_specs,
        scratch_shapes=scratch,
        input_output_aliases={3 + len(parts): 0},
        compiler_params=pltpu.CompilerParams(vmem_limit_bytes=24 * 2**20),
        cost_estimate=cost(2 * starts[-1]),
        name=label,
    )(*ins)


def sum_rounds(count_x, count_y):
    rounds = []
    for count, at in ((count_y, 1), (count_x, 0)):
        bit = 1
        while bit < count:
            bits = [bit, 2 * bit, 3 * bit] if 2 * bit < count else [bit]
            rounds.append(
                [
                    flat_perm(count_x, count_y, lambda i, j: (i, j ^ b) if at else (i ^ b, j))
                    for b in bits
                ]
            )
            bit *= 4
    return rounds


def sum_round(value, perms):
    others = [lax.ppermute(value, AXES, perm) for perm in perms]
    if len(others) == 1:
        return value + others[0]
    return (value + others[0]) + (others[1] + others[2])


def shards(density, moves, cols, halo_rows):
    row_count, block, strip = density.shape[2:]
    rim_count = halo_rows.shape[2]
    count_x = lax.axis_size("gx")
    count_y = lax.axis_size("gy")
    rows = density.reshape(row_count, block, strip)
    rims = halo_rows.reshape(rim_count)
    own_cols = cols.reshape(row_count, -1)

    *leaving, small, own_cols = pack(
        moves.reshape(row_count), rims, own_cols, rows, count_x, count_y
    )
    arrived = [None] * len(step_x)
    for d in range(len(step_x)):
        dx, dy = int(step_x[d]), int(step_y[d])
        perm = flat_perm(count_x, count_y, lambda i, j: (i + dx, j + dy))
        arrived[d] = lax.ppermute(leaving[d], AXES, perm)

    current, *shared, traces = place(small, arrived, strip)
    spots, table = tables(small, own_cols, arrived)
    swap = {
        "A": flat_perm(count_x, count_y, toward_a),
        "B": flat_perm(count_x, count_y, along_b),
        "C": flat_perm(count_x, count_y, toward_c),
        "Y": flat_perm(count_x, count_y, toward_y),
    }
    go = lambda value, way: lax.ppermute(value, AXES, swap[way])
    rounds = sum_rounds(count_x, count_y)
    tie = lax.optimization_barrier
    for step in range(STEPS):
        c, a_1, y_0 = (go(rim, way) for rim, way in zip(shared[:3], "CAY"))
        wide_high, wide_low = spread_own(current)
        wide_high, *shared = tie((wide_high, *shared[3:]))
        a_0, y_1 = (go(rim, way) for rim, way in zip(shared, "AY"))
        high, low, total = own_product(table, (wide_high, wide_low), row_count, block)
        add = functools.partial(add_product, table=table, high=high, low=low)
        a_1, y_0, c, total = tie((a_1, y_0, c, total))
        b_1, ya_1, ya_0 = go(a_1, "B"), go(a_1, "Y"), go(y_0, "A")
        (total,) = add(2, 1, parts=[a_1, y_0], total=total, label="first_product")
        a_0, y_1, total = tie((a_0, y_1, total))
        b_0 = go(a_0, "B")
        (total,) = add(3, 2, parts=[a_0, y_1, c], total=total, label="second_product")
        a_0, b_1, ya_0, total = tie((a_0, b_1, ya_0, total))
        yb_1, yb_0 = go(b_1, "Y"), go(ya_0, "B")
        ca = go(jnp.concatenate([a_0, a_1]), "C")
        (total,) = add(5, 1, parts=[b_1, ya_1], total=total, label="third_product")
        b_0, total = tie((b_0, total))
        cb = go(jnp.concatenate([b_0, b_1]), "C")
        last = functools.partial(add, 9, 1, parts=[yb_0, yb_1], label="last_product")
        fourth = functools.partial(add, 6, 2, parts=[b_0, ya_0, ca], label="fourth_product")
        fifth = functools.partial(add, 8, 1, parts=[cb], label="fifth_product")
        if step % 2 == 0:
            (total,) = fourth(total=total)
            (total,) = fifth(total=total)
            total, traces, current, *shared = last(
                total=total, traces=traces, square=(spots, small)
            )
        else:
            extra = far_trace(table, c, y_0, y_1, b_0, b_1)
            total, sums = fourth(total=total, traces=traces, extra=extra)
            sums = sum_round(sums, rounds[0])
            (total,) = fifth(total=total)
            sums, total = tie((sums, total))
            for perms in rounds[1:-1]:
                sums = sum_round(sums, perms)
            sums, total = tie((sums, total))
            sums = sum_round(sums, rounds[-1])
            _, current = last(total=total, square=(spots, small, current))
    sums = sums * (1.0 / (count_x * count_y * row_count * block))
    occupation = jnp.stack([sums[0], sums[1], sums[1], sums[2]])
    return (current.reshape(density.shape), occupation)


def solution(mesh):
    in_specs = (
        P("gx", "gy", None, None, None),
        P("gx", "gy", None),
        P("gx", "gy", None, None),
        P("gx", "gy", None),
    )
    out_specs = (P("gx", "gy", None, None, None), P())
    return jax.shard_map(shards, mesh=mesh, in_specs=in_specs, out_specs=out_specs, check_vma=False)
```

```python
import functools

import jax
import jax.numpy as jnp
import numpy as np
from jax import lax
from jax.experimental import pallas as pl
from jax.experimental.pallas import tpu as pltpu
from jax.sharding import PartitionSpec as P

STEPS = 2
AXES = ("gx", "gy")
LANES = 128
TILE = 256

step_x = np.array([0, 0, -1, 1, -1, 1, -1, 1])
step_y = np.array([-1, 1, -1, 1, 1, -1, 0, 0])

FRAME = {
    "C": (0, 1),
    "A": (1, 0),
    "Y": (0, -1),
    "CA": (1, 1),
    "B": (-1, 0),
    "YA": (1, -1),
    "CB": (-1, 1),
    "YB": (-1, -1),
}


OWN_TILES = 2
TILES = (
    (("A", 2, 2), ("Y", 0, 2)),
    (("A", 0, 2), ("Y", 2, 2)),
    (("C", 0, 4),),
    (("B", 2, 2), ("YA", 2, 2)),
    (("B", 0, 2), ("YA", 0, 2)),
    (("CA", 0, 4),),
    (("CB", 0, 4),),
    (("YB", 0, 4),),
)


def pool_places(rows):
    places = {}
    for t, members in enumerate(TILES):
        at = rows + 4 * t
        for name, begin, count in members:
            places.setdefault(name, [0, 0])
            if begin == 0:
                places[name][0] = at
            if begin + count == 4:
                places[name][1] = at + count - 2
            at += count
    return places


def reach(t):
    def frames(n):
        return [(0, 0)] if n < OWN_TILES else [FRAME[m[0]] for m in TILES[n - OWN_TILES]]

    near = lambda p, q: abs(p[0] - q[0]) <= 1 and abs(p[1] - q[1]) <= 1
    count = OWN_TILES + len(TILES)
    found = [n for n in range(count) if any(near(p, q) for p in frames(t) for q in frames(n))]
    if len(found) % 2:
        found.append(next(n for n in range(count) if n not in found))
    return found


def flat_perm(count_x, count_y, move):
    pairs = []
    for i in range(count_x):
        for j in range(count_y):
            x, y = move(i, j)
            pairs.append((i * count_y + j, (x % count_x) * count_y + y % count_y))
    return pairs


def toward_a(i, j):
    return i ^ 1, j


def along_b(i, j):
    return (i + 2 if i % 2 == 0 else i - 2), j


def toward_c(i, j):
    return i, j ^ 1


def toward_y(i, j):
    return i, (j - 1 if j % 2 == 0 else j + 1)


def split(value):
    high = value.astype(jnp.bfloat16)
    low = (value - high.astype(jnp.float32)).astype(jnp.bfloat16)
    return high, low


def trace_of(block):
    row = lax.broadcasted_iota(jnp.int32, block.shape, 0)
    lane = lax.broadcasted_iota(jnp.int32, block.shape, 1)
    return jnp.sum(jnp.where(row == lane, block, 0.0))


def quotient(value, by, most):
    total = jnp.zeros_like(value)
    for k in range(1, most + 1):
        total += (value >= by * k).astype(jnp.int32)
    return total


VMEM = pl.BlockSpec(memory_space=pltpu.VMEM)
SMEM = pl.BlockSpec(memory_space=pltpu.SMEM)


def pack(moves, rims, cols, rows, count_x, count_y):
    row_count, block, strip = rows.shape
    slots = cols.shape[1]
    rim_count = rims.shape[0]
    tiles = strip // LANES
    ways = len(step_x)

    def kernel(moves_in, rims_in, cols_in, rows_in, *refs):
        outs, refs = refs[:ways], refs[ways:]
        small_ref, cols_ref, moves_ref, rims_ref, rows_ref, codes_ref, tail_ref, sems = refs
        copies = [
            pltpu.make_async_copy(source, target, sems.at[k])
            for k, (source, target) in enumerate(
                (
                    (moves_in, moves_ref),
                    (rims_in, rims_ref),
                    (cols_in, cols_ref),
                    (rows_in, rows_ref),
                )
            )
        ]
        for copy in copies:
            copy.start()
        index_x = lax.axis_index("gx")
        index_y = lax.axis_index("gy")
        for copy in copies[:3]:
            copy.wait()
        cols = cols_ref[...]
        inner = jnp.full(cols.shape, -1, jnp.int32)
        for m in range(rim_count):
            small_ref[ways + m] = rims_ref[m]
            inner = jnp.where(cols == rims_ref[m], 4 * rim_count + m, inner)
        away = cols - row_count
        direction = quotient(away, rim_count, ways - 1)
        place = direction + (direction >= 4).astype(jnp.int32)
        code = jnp.where(
            cols < row_count, inner, place * rim_count + away - direction * rim_count
        )
        codes_ref[...] = jnp.zeros(codes_ref.shape, jnp.float32)
        tail_ref[...] = jnp.zeros(tail_ref.shape, jnp.float32)
        codes_ref[:, :slots] = code.astype(jnp.float32)
        for m in range(rim_count):
            tail_ref[pl.ds(m, 1), :] = codes_ref[pl.ds(rims_ref[m], 1), :]
        leaving = []
        for d in range(ways):
            x = lax.rem(index_x + int(step_x[d]) + count_x, count_x)
            y = lax.rem(index_y + int(step_y[d]) + count_y, count_y)
            first = (x * count_y + y) * row_count
            slot = jnp.int32(0)
            for r in range(1, row_count):
                target = moves_ref[r]
                slot = jnp.where((target >= first) & (target < first + row_count), r, slot)
            small_ref[d] = slot
            leaving.append(slot)
        copies[3].wait()
        for d in range(ways):
            for k in range(tiles):
                outs[d][k * block : (k + 1) * block, :] = rows_ref[
                    leaving[d], :, k * LANES : (k + 1) * LANES
                ]
            outs[d][tiles * block :, :] = tail_ref[...]

    message = jax.ShapeDtypeStruct((tiles * block + 8, LANES), jnp.float32)
    return pl.pallas_call(
        kernel,
        out_shape=(message,) * ways
        + (
            jax.ShapeDtypeStruct((ways + rim_count,), jnp.int32),
            jax.ShapeDtypeStruct(cols.shape, jnp.int32),
        ),
        in_specs=[pl.BlockSpec(memory_space=pltpu.HBM)] * 4,
        out_specs=(VMEM,) * ways + (SMEM, VMEM),
        scratch_shapes=[
            pltpu.SMEM((row_count,), jnp.int32),
            pltpu.SMEM((rim_count,), jnp.int32),
            pltpu.VMEM(rows.shape, jnp.float32),
            pltpu.VMEM((row_count, LANES), jnp.float32),
            pltpu.VMEM((8, LANES), jnp.float32),
            pltpu.SemaphoreType.DMA((4,)),
        ],
        compiler_params=pltpu.CompilerParams(vmem_limit_bytes=16 * 2**20),
        name="pack_rows",
    )(moves, rims, cols, rows)


def share(rows_ref, small_ref, rim_refs):
    rim_ref, a_1, y_0, a_0, y_1 = rim_refs
    count = rim_ref.shape[0]
    for m in range(count):
        row = rows_ref[small_ref[len(step_x) + m]]
        rim_ref[m] = row
        for ref in (a_0, y_0) if m < count // 2 else (a_1, y_1):
            ref[m % (count // 2)] = row


def place(small, arrived, strip):
    rows = len(arrived)
    tiles = strip // LANES
    block = (arrived[0].shape[0] - 8) // tiles
    count = small.shape[0] - rows
    half = count // 2

    def kernel(small_ref, *refs):
        ins, outs = refs[:rows], refs[rows:]
        current_ref, *rim_refs, trace_ref = outs
        total = jnp.float32(0.0)
        for d in range(rows):
            for k in range(tiles):
                current_ref[small_ref[d], :, k * LANES : (k + 1) * LANES] = ins[d][
                    k * block : (k + 1) * block, :
                ]
            total += trace_of(ins[d][:block, :])
        trace_ref[0] = total
        share(current_ref, small_ref, rim_refs)

    rim = lambda n: jax.ShapeDtypeStruct((n, block, strip), jnp.float32)
    return pl.pallas_call(
        kernel,
        out_shape=(rim(rows), rim(count), rim(half), rim(half), rim(half), rim(half))
        + (jax.ShapeDtypeStruct((1,), jnp.float32),),
        in_specs=[SMEM] + [VMEM] * rows,
        out_specs=(VMEM,) * 6 + (SMEM,),
        compiler_params=pltpu.CompilerParams(vmem_limit_bytes=16 * 2**20),
        name="place_rows",
    )(small, *arrived)


def tables(small, cols, arrived):
    rows, slots = cols.shape
    rim_count = small.shape[0] - len(arrived)
    half = rim_count // 2
    pool = rows + len(TILES) * rim_count
    tail = arrived[0].shape[0] // 8 - 1
    base_of = [[0, 0]] * 9
    for name, (one, two) in pool_places(rows).items():
        x, y = FRAME[name]
        base_of[3 * (x + 1) + y + 1] = [one, two - half]

    def kernel(small_ref, cols_ref, *refs):
        tails, (spots_ref, table_ref, all_ref) = refs[: len(arrived)], refs[len(arrived) :]
        sign_x = 1 - 2 * lax.rem(lax.axis_index("gx"), 2)
        sign_y = 1 - 2 * lax.rem(lax.axis_index("gy"), 2)

        def locate(place, index, shift_x, shift_y):
            third = quotient(place, 3, 2)
            x = (third - 1) * sign_x + shift_x
            y = (place - 3 * third - 1) * sign_y + shift_y
            inside = (x >= -1) & (x <= 1) & (y >= -1) & (y <= 1)
            at = 3 * (x + 1) + y + 1
            one = two = jnp.zeros_like(index)
            for k in range(9):
                one = jnp.where(at == k, base_of[k][0], one)
                two = jnp.where(at == k, base_of[k][1], two)
            spot = index + jnp.where(index < half, one, two)
            for m in range(rim_count):
                spot = jnp.where((at == 4) & (index == m), small_ref[len(arrived) + m], spot)
            return jnp.where(inside, spot, -1)

        cols = cols_ref[...]
        away = cols - rows
        direction = quotient(away, rim_count, 7)
        place = direction + (direction >= 4).astype(jnp.int32)
        spots = locate(place, away - direction * rim_count, 0, 0)
        spots = jnp.where(cols < rows, cols, spots)
        spots_ref[...] = spots
        all_ref[...] = jnp.full(all_ref.shape, -1, jnp.int32)
        all_ref[:rows, :slots] = spots
        for d in range(len(arrived)):
            x = -int(step_x[d]) * sign_x
            y = -int(step_y[d]) * sign_y
            at = 3 * (x + 1) + y + 1
            bases = []
            for part in range(2):
                base = jnp.int32(0)
                for k in range(9):
                    base = jnp.where(at == k, base_of[k][part], base)
                bases.append(base)
            near = tails[d][...].astype(jnp.int32)
            place = quotient(near, rim_count, 8)
            spots = locate(place, near - place * rim_count, x, y)
            spots = jnp.where(near < 0, -1, spots)
            for m in range(rim_count):
                all_ref[pl.ds(bases[m // half] + m, 1), :] = spots[m : m + 1, :]
        lane = lax.broadcasted_iota(jnp.int32, (pool, LANES), 1)
        found = jnp.full((pool, LANES), -1, jnp.int32)
        for u in range(slots):
            found = jnp.where(all_ref[:, u : u + 1] == lane, u, found)
        entry = (found >> 1) + 16 * ((found ^ lane) & 1)
        table_ref[...] = jnp.where(found < 0, slots // 2, entry)

    last = pl.BlockSpec((8, LANES), lambda n: (tail, 0))
    full = lambda shape: pl.BlockSpec(shape, lambda n: (0, 0))
    return pl.pallas_call(
        kernel,
        grid=(1,),
        out_shape=(
            jax.ShapeDtypeStruct((rows, slots), jnp.int32),
            jax.ShapeDtypeStruct((pool, LANES), jnp.int32),
        ),
        in_specs=[SMEM, full((rows, slots))] + [last] * len(arrived),
        out_specs=(full((rows, slots)), full((pool, LANES))),
        scratch_shapes=[pltpu.VMEM((pool, LANES), jnp.int32)],
        compiler_params=pltpu.CompilerParams(vmem_limit_bytes=4 * 2**20),
        name="make_tables",
    )(small, cols, *arrived)


def spread(parts, high_ref, low_ref):
    base = 0
    strip = parts[0].shape[2]
    for ref in parts:

        def one(c, carry, ref=ref, base=base):
            at = pl.ds(pl.multiple_of((base + c) * 64, 64), 64)
            for k in range(strip // LANES):
                to = pl.ds(k * LANES, LANES)
                value = ref[c, :, to]
                for turn in range(2):
                    high, low = split(pltpu.roll(value, 64, 1) if turn else value)
                    high_ref[turn, at, to] = high
                    low_ref[turn, at, to] = low
            zeros = jnp.zeros((64, LANES), jnp.bfloat16)
            high_ref[0, at, pl.ds(strip, LANES)] = zeros
            low_ref[0, at, pl.ds(strip, LANES)] = zeros
            return carry

        lax.fori_loop(0, ref.shape[0], one, 0)
        base += ref.shape[0]


def fill_pair(table_ref, position, spot, source, member, targets):
    left_half = lax.broadcasted_iota(jnp.int32, (64, LANES), 1) < 64
    at = pl.ds(pl.multiple_of(member * 64, 64), 64)
    left = table_ref[position, spot]
    right = table_ref[position, spot + 1]
    from_left = pl.ds(pl.multiple_of((left & 15) * LANES, LANES), LANES)
    from_right = pl.ds(pl.multiple_of((right & 15) * LANES, LANES), LANES)
    for k in range(2):
        value = jnp.where(
            left_half, source[k][left >> 4, at, from_left], source[k][right >> 4, at, from_right]
        )
        for refs, row, first in targets:
            refs[k][pl.ds(row, 64), pl.ds(pl.multiple_of(first, LANES), LANES)] = value


def fill(table_ref, first, member, members, tile, source, targets):
    for c in range(members):
        for q in range(TILE // LANES):
            fill_pair(
                table_ref, first + member + c, tile * (TILE // 64) + 2 * q, source, member + c,
                [(refs, c * 64, to + q * LANES) for refs, to in targets],
            )


def three_products(a_high, a_low, d_high, d_low):
    left = jnp.concatenate([a_high, a_high, a_low], axis=1)
    right = jnp.concatenate([d_high, d_low, d_high], axis=0)
    return jnp.dot(left, right, preferred_element_type=jnp.float32)


def wide_scratch(members, strip):
    return [pltpu.VMEM((2, members * 64, strip + LANES), jnp.bfloat16)] * 2


def pipelined(units, fill_one, multiply, buffers):
    even, odd = buffers
    fill_one(jnp.int32(0), even)

    def two(j, carry):
        fill_one(2 * j + 1, odd)
        multiply(2 * j, even)
        fill_one(jnp.minimum(2 * j + 2, units - 1), even)
        multiply(2 * j + 1, odd)
        return carry

    lax.fori_loop(0, units // 2, two, 0)
    if units % 2:
        multiply(units - 1, even)


def lane(tile):
    return pl.multiple_of(tile * TILE, TILE)


def cost(units):
    return pl.CostEstimate(flops=units * 2**27, bytes_accessed=2**16, transcendentals=0)


def spread_own(current):
    rows, block, strip = current.shape

    def kernel(current_ref, high_ref, low_ref):
        spread([current_ref], high_ref, low_ref)

    wide = jax.ShapeDtypeStruct((2, rows * block, strip + LANES), jnp.bfloat16)
    return pl.pallas_call(
        kernel,
        out_shape=(wide, wide),
        in_specs=[VMEM],
        out_specs=(VMEM, VMEM),
        compiler_params=pltpu.CompilerParams(vmem_limit_bytes=16 * 2**20),
        cost_estimate=cost(1),
        name="spread_own",
    )(current)


def own_product(table, wide, rows, block):
    width = table.shape[0] * block
    depth = rows * block
    tiles = width // TILE

    def kernel(table_ref, wide_high, wide_low, high_ref, low_ref, total_ref, *scratch):
        wide = wide_high, wide_low
        own, even, odd = scratch[0:2], scratch[2:4], scratch[4:6]
        for n in range(depth // TILE):
            fill(table_ref, 0, 0, rows, n, wide, [(own, n * TILE)])

        def fill_one(i, buffers):
            for k in range(2):
                fill(
                    table_ref, 0, 0, rows, 2 * i + k, wide,
                    [(buffers, k * TILE), ((high_ref, low_ref), (2 * i + k) * TILE)],
                )

        def multiply(i, buffers):
            to = pl.ds(pl.multiple_of(2 * i * TILE, 2 * TILE), 2 * TILE)
            total_ref[:, to] = three_products(
                own[0][...], own[1][...], buffers[0][...], buffers[1][...]
            )

        pipelined(tiles // 2, fill_one, multiply, (even, odd))

    dense = lambda t: jax.ShapeDtypeStruct((depth, width), t)
    return pl.pallas_call(
        kernel,
        out_shape=(dense(jnp.bfloat16), dense(jnp.bfloat16), dense(jnp.float32)),
        in_specs=[SMEM, VMEM, VMEM],
        out_specs=(VMEM, VMEM, VMEM),
        scratch_shapes=[pltpu.VMEM((depth, depth), jnp.bfloat16)] * 2
        + [pltpu.VMEM((depth, 2 * TILE), jnp.bfloat16)] * 4,
        compiler_params=pltpu.CompilerParams(vmem_limit_bytes=24 * 2**20),
        cost_estimate=cost(2 * tiles),
        name="own_product",
    )(table, *wide)


def extract(spots_ref, total_ref, current_ref, out_ref, blend):
    left_half = lax.broadcasted_iota(jnp.int32, (64, LANES), 1) < 64

    def one_row(g, carry):
        at = pl.ds(pl.multiple_of(g * 64, 64), 64)
        for k in range(out_ref.shape[2] // LANES):
            sides = []
            for side in range(2):
                spot = spots_ref[g, 2 * k + side]
                tile = pl.ds(pl.multiple_of((spot >> 1) * LANES, LANES), LANES)
                sides.append(pltpu.roll(total_ref[at, tile], ((spot ^ side) & 1) * 64, 1))
            value = jnp.where(left_half, *sides)
            to = pl.ds(k * LANES, LANES)
            if blend:
                value = 2.0 * current_ref[g, :, to] - value
            out_ref[g, :, to] = value
        return carry

    lax.fori_loop(0, out_ref.shape[0], one_row, 0)


def add_traces(traces_ref, extra_ref, total_ref, trace_ref):
    known = traces_ref.shape[0]
    for k in range(known):
        trace_ref[k] = traces_ref[k]
    row = lax.broadcasted_iota(jnp.int32, (64, LANES), 0)
    spot = lax.broadcasted_iota(jnp.int32, (64, LANES), 1)
    found = jnp.zeros((64, LANES), jnp.float32)
    for g in range(total_ref.shape[0] // 64):
        block = total_ref[g * 64 : (g + 1) * 64, (g // 2) * LANES : (g // 2 + 1) * LANES]
        found += jnp.where(spot - row == 64 * (g % 2), block, 0.0)
    trace_ref[known] = jnp.sum(found) + (0.0 if extra_ref is None else extra_ref[0])


def far_trace(table, c, y_0, y_1, b_0, b_1):
    parts = [c, y_0, y_1, b_0, b_1]
    _, block, strip = c.shape
    places = pool_places(8)
    members = {"C": 0, "Y": 4, "B": 8}

    def kernel(table_ref, *refs):
        part_refs, trace_ref, wide, one, two = refs[:5], refs[5], refs[6:8], refs[8:10], refs[10:12]
        spread(part_refs, *wide)
        for k, name in enumerate("CY"):
            for m in range(4):
                for q in range(2):
                    fill_pair(
                        table_ref, places["B"][m // 2] + m % 2, places[name][q], wide,
                        members["B"] + m, [(one, m * 64, k * TILE + q * LANES)],
                    )
                    fill_pair(
                        table_ref, places[name][m // 2] + m % 2, places["B"][q], wide,
                        members[name] + m, [(two, k * TILE + m * 64, q * LANES)],
                    )
        product = three_products(one[0][...], one[1][...], two[0][...], two[1][...])
        row = lax.broadcasted_iota(jnp.int32, product.shape, 0)
        spot = lax.broadcasted_iota(jnp.int32, product.shape, 1)
        trace_ref[0] = jnp.sum(jnp.where(row == spot, product, 0.0))

    return pl.pallas_call(
        kernel,
        out_shape=jax.ShapeDtypeStruct((1,), jnp.float32),
        in_specs=[SMEM] + [VMEM] * 5,
        out_specs=SMEM,
        scratch_shapes=wide_scratch(12, strip)
        + [pltpu.VMEM((TILE, 2 * TILE), jnp.bfloat16)] * 2
        + [pltpu.VMEM((2 * TILE, TILE), jnp.bfloat16)] * 2,
        compiler_params=pltpu.CompilerParams(vmem_limit_bytes=24 * 2**20),
        cost_estimate=cost(4),
        name="far_trace",
    )(table, *parts)


def add_product(begin, count, table, high, low, parts, total, label, traces=None, extra=None, square=None):
    depth_own, width = total.shape
    _, block, strip = parts[0].shape
    rows = depth_own // block
    each = TILE // block
    first = begin * each
    lists = [reach(begin + k) for k in range(count)]
    blend = square is not None and len(square) == 3
    starts = [sum(len(t) for t in lists[:k]) // 2 for k in range(count + 1)]
    codes = [
        [sum(t << (4 * k) for k, t in enumerate(tiles[side::2])) for side in range(2)]
        for tiles in lists
    ]

    def unit(i):
        group, start = jnp.int32(0), jnp.int32(0)
        code = [jnp.int32(c) for c in codes[0]]
        for k in range(1, count):
            after = i >= starts[k]
            group = jnp.where(after, k, group)
            start = jnp.where(after, starts[k], start)
            code = [jnp.where(after, new, old) for new, old in zip(codes[k], code)]
        return group, [(c >> (4 * (i - start))) & 15 for c in code]

    def kernel(table_ref, high_ref, low_ref, *refs):
        refs = list(refs)
        part_refs = [refs.pop(0) for _ in parts]
        refs.pop(0)
        if traces is not None:
            traces_ref = refs.pop(0)
        extra_ref = refs.pop(0) if extra is not None else None
        if square is not None:
            spots_ref, small_ref = refs.pop(0), refs.pop(0)
        current_ref = refs.pop(0) if blend else None
        total_ref = refs.pop(0)
        if traces is not None:
            trace_ref = refs.pop(0)
        if square is not None:
            out_ref, *rim_refs = (refs.pop(0) for _ in range(1 if blend else 6))
        wide, even, odd = refs[0:2], refs[2:4], refs[4:6]
        spread(part_refs, *wide)

        def fill_one(i, buffers):
            group, tiles = unit(i)
            for k in range(2):
                fill(table_ref, first, group * each, each, tiles[k], wide, [(buffers, k * TILE)])

        def multiply(i, buffers):
            group, tiles = unit(i)
            at = pl.ds(lane(begin + group), TILE)
            value = three_products(
                high_ref[:, at], low_ref[:, at], buffers[0][...], buffers[1][...]
            )
            for k in range(2):
                to = pl.ds(lane(tiles[k]), TILE)
                total_ref[:, to] += value[:, k * TILE : (k + 1) * TILE]

        pipelined(starts[-1], fill_one, multiply, (even, odd))
        if traces is not None:
            add_traces(traces_ref, extra_ref, total_ref, trace_ref)
        if square is not None:
            extract(spots_ref, total_ref, current_ref, out_ref, blend)
            if not blend:
                share(out_ref, small_ref, rim_refs)

    ins = [table, high, low, *parts, total]
    in_specs = [SMEM] + [VMEM] * (3 + len(parts))
    out_shape = [jax.ShapeDtypeStruct((depth_own, width), jnp.float32)]
    out_specs = [VMEM]
    if traces is not None:
        ins.append(traces)
        in_specs.append(SMEM)
        out_shape.append(jax.ShapeDtypeStruct((traces.shape[0] + 1,), jnp.float32))
        out_specs.append(SMEM)
    if extra is not None:
        ins.append(extra)
        in_specs.append(SMEM)
    if square is not None:
        ins += square
        in_specs += [SMEM, SMEM] + [VMEM] * blend
        shape = lambda n: jax.ShapeDtypeStruct((n, block, strip), jnp.float32)
        out_shape.append(shape(rows))
        if not blend:
            out_shape += [shape(each)] + [shape(each // 2)] * 4
        out_specs += [VMEM] * (len(out_shape) - len(out_specs))
    scratch = wide_scratch(count * each, strip)
    scratch += [pltpu.VMEM((TILE, 2 * TILE), jnp.bfloat16)] * 4
    return pl.pallas_call(
        kernel,
        out_shape=out_shape,
        in_specs=in_specs,
        out_specs=out_specs,
        scratch_shapes=scratch,
        input_output_aliases={3 + len(parts): 0},
        compiler_params=pltpu.CompilerParams(vmem_limit_bytes=24 * 2**20),
        cost_estimate=cost(2 * starts[-1]),
        name=label,
    )(*ins)


def sum_rounds(count_x, count_y):
    rounds = []
    for count, at in ((count_y, 1), (count_x, 0)):
        bit = 1
        while bit < count:
            bits = [bit, 2 * bit, 3 * bit] if 2 * bit < count else [bit]
            rounds.append(
                [
                    flat_perm(count_x, count_y, lambda i, j: (i, j ^ b) if at else (i ^ b, j))
                    for b in bits
                ]
            )
            bit *= 4
    return rounds


def sum_round(value, perms):
    others = [lax.ppermute(value, AXES, perm) for perm in perms]
    if len(others) == 1:
        return value + others[0]
    return (value + others[0]) + (others[1] + others[2])


def shards(density, moves, cols, halo_rows):
    row_count, block, strip = density.shape[2:]
    rim_count = halo_rows.shape[2]
    count_x = lax.axis_size("gx")
    count_y = lax.axis_size("gy")
    rows = density.reshape(row_count, block, strip)
    rims = halo_rows.reshape(rim_count)
    own_cols = cols.reshape(row_count, -1)

    *leaving, small, own_cols = pack(
        moves.reshape(row_count), rims, own_cols, rows, count_x, count_y
    )
    arrived = [None] * len(step_x)
    for d in range(len(step_x)):
        dx, dy = int(step_x[d]), int(step_y[d])
        perm = flat_perm(count_x, count_y, lambda i, j: (i + dx, j + dy))
        arrived[d] = lax.ppermute(leaving[d], AXES, perm)

    current, *shared, traces = place(small, arrived, strip)
    spots, table = tables(small, own_cols, arrived)
    swap = {
        "A": flat_perm(count_x, count_y, toward_a),
        "B": flat_perm(count_x, count_y, along_b),
        "C": flat_perm(count_x, count_y, toward_c),
        "Y": flat_perm(count_x, count_y, toward_y),
    }
    go = lambda value, way: lax.ppermute(value, AXES, swap[way])
    rounds = sum_rounds(count_x, count_y)
    tie = lax.optimization_barrier
    for step in range(STEPS):
        c, a_1, y_0 = (go(rim, way) for rim, way in zip(shared[:3], "CAY"))
        wide_high, wide_low = spread_own(current)
        wide_high, *shared = tie((wide_high, *shared[3:]))
        a_0, y_1 = (go(rim, way) for rim, way in zip(shared, "AY"))
        high, low, total = own_product(table, (wide_high, wide_low), row_count, block)
        add = functools.partial(add_product, table=table, high=high, low=low)
        a_1, y_0, c, total = tie((a_1, y_0, c, total))
        b_1, ya_1, ya_0 = go(a_1, "B"), go(a_1, "Y"), go(y_0, "A")
        (total,) = add(2, 1, parts=[a_1, y_0], total=total, label="first_product")
        a_0, y_1, total = tie((a_0, y_1, total))
        b_0 = go(a_0, "B")
        (total,) = add(3, 2, parts=[a_0, y_1, c], total=total, label="second_product")
        a_0, b_1, ya_0, total = tie((a_0, b_1, ya_0, total))
        yb_1, yb_0 = go(b_1, "Y"), go(ya_0, "B")
        ca = go(jnp.concatenate([a_0, a_1]), "C")
        (total,) = add(5, 1, parts=[b_1, ya_1], total=total, label="third_product")
        b_0, total = tie((b_0, total))
        cb = go(jnp.concatenate([b_0, b_1]), "C")
        last = functools.partial(add, 9, 1, parts=[yb_0, yb_1], label="last_product")
        fourth = functools.partial(add, 6, 2, parts=[b_0, ya_0, ca], label="fourth_product")
        fifth = functools.partial(add, 8, 1, parts=[cb], label="fifth_product")
        if step % 2 == 0:
            (total,) = fourth(total=total)
            (total,) = fifth(total=total)
            total, traces, current, *shared = last(
                total=total, traces=traces, square=(spots, small)
            )
        else:
            extra = far_trace(table, c, y_0, y_1, b_0, b_1)
            total, sums = fourth(total=total, traces=traces, extra=extra)
            sums = sum_round(sums, rounds[0])
            (total,) = fifth(total=total)
            sums, total = tie((sums, total))
            for perms in rounds[1:]:
                sums = sum_round(sums, perms)
            _, current = last(total=total, square=(spots, small, current))
    sums = sums * (1.0 / (count_x * count_y * row_count * block))
    occupation = jnp.stack([sums[0], sums[1], sums[1], sums[2]])
    return (current.reshape(density.shape), occupation)


def solution(mesh):
    in_specs = (
        P("gx", "gy", None, None, None),
        P("gx", "gy", None),
        P("gx", "gy", None, None),
        P("gx", "gy", None),
    )
    out_specs = (P("gx", "gy", None, None, None), P())
    return jax.shard_map(shards, mesh=mesh, in_specs=in_specs, out_specs=out_specs, check_vma=False)
```
